256 devices in a mesh: src: 32 (over z, y_lo, core), tgt: 8 (over y_hi, x).
Axes of the slice: x: 4, y: 4 (y_hi: 2, y_lo: 2; y = y_hi * 2 + y_lo), z: 8, core: 2. Of those that a mesh axis runs over, the one named last changes fastest.
Arguments:
- sources: bfloat16 [49152, 256], P('src'), may hold values from -6 to 6, as said below
- targets: bfloat16 [12288, 256], P('tgt'), may hold values from -6 to 6, as said below
- pairs: int32 [32, 8, 24, 2], P('src', 'tgt'), may hold values from 0 to 5, as said below
- counts: int32 [32, 8], P('src', 'tgt'), may hold values from 6 to 24, as said below
Outputs:
- forward_map: float32 [49152, 256], P(('src', 'tgt'))
- backward_map: float32 [12288, 256], P(('tgt', 'src'))
The draws below stay inside these ranges and needn't reach their ends.
Inputs may be any that keep to these rules, and one draw needn't show every extreme that they name: `sources`: latent entries lie within this range. `targets`: latent entries lie within this range. On each device all 24 slots hold distinct pairs; the first 6 slots name each of its source clusters once and each of its target clusters once. `counts`: uneven over devices; in every draw some device keeps all 24 slots.
All inputs are finite; a program needn't handle non-finite values.
Results may differ from the reference program's by a relative error of at most 0.0003.
Values sent between devices are 32-bit elements; how exact they have to be, the bound alone decides.
No kernel may reach another device: no remote copies, remote signals or barrier semaphores. Data moves between devices by JAX's collectives and lax.ppermute only.
A program may use at most 192 MiB of HBM per device.

```python
import math
import jax
import jax.numpy as jnp
from jax import lax

D = 256
BLK = 256
BLK_DEV = 6
ITERS = 2
PAIR_CAP = 24
N_SRC = 32
N_TGT = 8


def draw_sources(key, part):
    key = jax.random.fold_in(key, 3)
    first = jax.random.fold_in(key, 0)
    shape = (N_SRC * BLK_DEV * BLK, D)
    values = jnp.clip(jax.random.normal(first, shape), -6.0, 6.0)
    return values.astype(jnp.float32).astype(jnp.bfloat16)


def draw_targets(key, part):
    key = jax.random.fold_in(key, 5)
    first = jax.random.fold_in(key, 0)
    shape = (N_TGT * BLK_DEV * BLK, D)
    values = jnp.clip(jax.random.normal(first, shape), -6.0, 6.0)
    return values.astype(jnp.float32).astype(jnp.bfloat16)


def draw_pairs(key, part):
    key = jax.random.fold_in(key, 7)
    combos = BLK_DEV * BLK_DEV

    def device_list(device_key):
        first, second = jax.random.split(device_key)
        matching = jax.random.permutation(first, BLK_DEV).astype(jnp.int32)
        marked = jnp.zeros((combos,), jnp.int32).at[jnp.arange(BLK_DEV, dtype=jnp.int32) * BLK_DEV + matching].set(1)
        ranking = jax.random.randint(second, (combos,), 0, combos) * combos + jnp.arange(combos, dtype=jnp.int32) + marked * combos * combos
        chosen = lax.top_k(ranking, PAIR_CAP)[1].astype(jnp.int32)
        return jnp.stack([chosen // BLK_DEV, chosen % BLK_DEV], axis=-1)
    device_keys = jax.random.split(key, N_SRC * N_TGT)
    return jax.vmap(device_list)(device_keys).reshape(N_SRC, N_TGT, PAIR_CAP, 2).astype(jnp.int32)


def draw_counts(key, part):
    key = jax.random.fold_in(key, 9)
    first, second = jax.random.split(key)
    drawn = jax.random.randint(first, (N_SRC, N_TGT), BLK_DEV, PAIR_CAP + 1)
    chosen = jax.random.randint(second, (), 0, N_SRC * N_TGT)
    places = jnp.arange(N_SRC * N_TGT, dtype=jnp.int32).reshape(N_SRC, N_TGT)
    return jnp.where(places == chosen, PAIR_CAP, drawn).astype(jnp.int32)


def setup_inputs(seed: int = 0) -> dict:
    key_of = jax.random.split(jax.random.key(seed), 5)
    return {
        "sources": draw_sources(jax.random.fold_in(key_of[4], 71), 0),
        "targets": draw_targets(jax.random.fold_in(key_of[4], 71), 0),
        "pairs": draw_pairs(jax.random.fold_in(key_of[4], 71), 0),
        "counts": draw_counts(jax.random.fold_in(key_of[4], 71), 0),
    }


NEG_FILL = -1e+30

def reference(sources, targets, pairs, counts):
    width = sources.shape[1]
    temper = math.sqrt(width) / 4.0
    src_count = N_SRC * BLK_DEV
    tgt_count = N_TGT * BLK_DEV
    src_blocks = sources.reshape(src_count, BLK, width)
    tgt_blocks = targets.reshape(tgt_count, BLK, width)
    src_half = 0.5 * lax.optimization_barrier(jnp.sum(jnp.square(src_blocks.astype(jnp.float32)), axis=-1))
    tgt_half = 0.5 * lax.optimization_barrier(jnp.sum(jnp.square(tgt_blocks.astype(jnp.float32)), axis=-1))
    src_base = (jnp.arange(N_SRC, dtype=jnp.int32) * BLK_DEV)[:, None, None]
    tgt_base = (jnp.arange(N_TGT, dtype=jnp.int32) * BLK_DEV)[None, :, None]
    src_ids = (src_base + pairs[..., 0]).reshape(-1).astype(jnp.int32)
    tgt_ids = (tgt_base + pairs[..., 1]).reshape(-1).astype(jnp.int32)
    usable = (jnp.arange(PAIR_CAP, dtype=jnp.int32)[None, None, :] < counts[:, :, None]).reshape(-1)
    order = jnp.arange(src_ids.shape[0], dtype=jnp.int32)

    def pair_cost(index):
        cross = jnp.dot(src_blocks[src_ids[index]], tgt_blocks[tgt_ids[index]].T, preferred_element_type=jnp.float32)
        return src_half[src_ids[index]][:, None] + tgt_half[tgt_ids[index]][None, :] - cross

    def settle(peaks, sums, block_ids, count):
        peaks = jnp.where(usable[:, None], peaks, NEG_FILL)
        highest = jax.ops.segment_max(peaks, block_ids, num_segments=count)
        scaled = jnp.where(usable[:, None], sums * jnp.exp(peaks - highest[block_ids]), 0.0)
        return highest + jnp.log(jax.ops.segment_sum(scaled, block_ids, num_segments=count))

    def log_sums(src_pot, tgt_pot):

        def single(index):
            pair_tile = pair_cost(index)
            row_scores = (tgt_pot[tgt_ids[index]][None, :] - pair_tile) / temper
            col_scores = (src_pot[src_ids[index]][:, None] - pair_tile) / temper
            row_high = lax.optimization_barrier(jnp.max(row_scores, axis=1))
            col_high = lax.optimization_barrier(jnp.max(col_scores, axis=0))
            row_sums = lax.optimization_barrier(jnp.sum(jnp.exp(row_scores - row_high[:, None]), axis=1))
            col_sums = lax.optimization_barrier(jnp.sum(jnp.exp(col_scores - col_high[None, :]), axis=0))
            return (row_high, row_sums, col_high, col_sums)
        row_high, row_sums, col_high, col_sums = lax.map(single, order)
        return (settle(row_high, row_sums, src_ids, src_count), settle(col_high, col_sums, tgt_ids, tgt_count))
    src_pot = jnp.zeros((src_count, BLK), jnp.float32)
    tgt_pot = jnp.zeros((tgt_count, BLK), jnp.float32)
    for sweep_index in range(ITERS):
        row_lse, col_lse = log_sums(src_pot, tgt_pot)
        src_pot, tgt_pot = (0.5 * (src_pot - temper * row_lse), 0.5 * (tgt_pot - temper * col_lse))
    row_lse, col_lse = log_sums(src_pot, tgt_pot)

    def project(running, index):
        forward, backward = running
        pair_tile = pair_cost(index)
        keep = usable[index]
        row_weights = jnp.exp((tgt_pot[tgt_ids[index]][None, :] - pair_tile) / temper - row_lse[src_ids[index]][:, None])
        col_weights = jnp.exp((src_pot[src_ids[index]][:, None] - pair_tile) / temper - col_lse[tgt_ids[index]][None, :])
        row_weights = jnp.where(keep, row_weights, 0.0)
        col_weights = jnp.where(keep, col_weights, 0.0)
        forward = forward.at[src_ids[index]].add(jnp.dot(row_weights, tgt_blocks[tgt_ids[index]].astype(jnp.float32), precision=lax.Precision.HIGHEST))
        backward = backward.at[tgt_ids[index]].add(jnp.dot(col_weights.T, src_blocks[src_ids[index]].astype(jnp.float32), precision=lax.Precision.HIGHEST))
        return ((forward, backward), None)
    start = (jnp.zeros((src_count, BLK, width), jnp.float32), jnp.zeros((tgt_count, BLK, width), jnp.float32))
    (forward, backward), unused = lax.scan(project, start, order)
    return (forward.reshape(-1, width), backward.reshape(-1, width))
```

```python
import functools
import math

import jax
import jax.numpy as jnp
from jax import lax
from jax.experimental import pallas as pl
from jax.experimental.pallas import tpu as pltpu
from jax.sharding import PartitionSpec as P

BLK = 256
ITERS = 2
NEG = -1e30
VMEM_BYTES = 24 * 1024 * 1024


def log_sum(parts):
    high = functools.reduce(jnp.maximum, parts)
    total = functools.reduce(jnp.add, [jnp.exp2(part - high) for part in parts])
    return high + jnp.log2(total)


def down_rows(lanes, blocks, wide_ref):
    upright = jnp.transpose(lanes)
    for b in range(blocks):
        wide_ref[b] = jnp.broadcast_to(upright[:, b : b + 1], (BLK, 128))


def norms(z_ref, scale, blocks, wide_ref):
    lane = lax.broadcasted_iota(jnp.int32, (BLK, 128), 1)
    gathered = jnp.zeros((BLK, 128), jnp.float32)
    for b in range(blocks):
        z = z_ref[b].astype(jnp.float32)
        half = jnp.sum(z * z, axis=1, keepdims=True) * (-0.5 * scale)
        wide = jnp.broadcast_to(half, (BLK, 128))
        wide_ref[b] = wide
        gathered = jnp.where(lane == b, wide, gathered)
    return jnp.transpose(gathered)[:8]


def over_pairs(pairs_ref, kept, visit):
    def two(step, carry):
        p = 2 * step
        visit(pairs_ref[2 * p], pairs_ref[2 * p + 1])
        visit(pairs_ref[2 * p + 2], pairs_ref[2 * p + 3])
        return carry

    lax.fori_loop(0, kept // 2, two, 0)

    @pl.when(kept % 2 == 1)
    def _():
        p = kept - 1
        visit(pairs_ref[2 * p], pairs_ref[2 * p + 1])


def cross(a, b):
    return lax.dot_general(a, b, (((1,), (1,)), ((), ())), preferred_element_type=jnp.float32)


def fold(scores, wide, scale, high_ref, sum_ref, b):
    for h in range(2):
        at = slice(128 * h, 128 * h + 128)
        t = (scores[:, at] * scale + wide).reshape(BLK // 8, 8, 128)
        old = high_ref[b, :, at]
        high = jnp.maximum(old, jnp.max(t, axis=0))
        total = jnp.sum(jnp.exp2(t - high[None]), axis=0)
        sum_ref[b, :, at] = sum_ref[b, :, at] * jnp.exp2(old - high) + total
        high_ref[b, :, at] = high


def settle(high_ref, sum_ref, blocks):
    rows = []
    for b in range(blocks):
        high = high_ref[b]
        top = jnp.max(high, axis=0, keepdims=True)
        total = jnp.sum(sum_ref[b] * jnp.exp2(high - top), axis=0, keepdims=True)
        rows.append(top + jnp.log2(total))
    rows += [jnp.zeros((1, BLK), jnp.float32)] * (8 - blocks)
    return jnp.concatenate(rows, axis=0)


def start_potentials(x_ref, y_ref, rest, first, n_row, n_col, scale, blocks, f_wide, g_wide):
    if first:
        return norms(x_ref, scale, blocks, f_wide), norms(y_ref, scale, blocks, g_wide), rest
    f_old, g_old = rest[0][...], rest[1][...]
    rows = [part for r in rest[2 : 2 + n_row] for part in parts_of(r)]
    cols = [part for r in rest[2 + n_row : 2 + n_row + n_col] for part in parts_of(r)]
    f = 0.5 * (f_old - log_sum(rows))
    g = 0.5 * (g_old - log_sum(cols))
    down_rows(f, blocks, f_wide)
    down_rows(g, blocks, g_wide)
    return f, g, rest[2 + n_row + n_col :]


def parts_of(ref):
    if len(ref.shape) == 2:
        return [ref[...]]
    return [ref[k] for k in range(ref.shape[0])]


def pass_sums(pairs_ref, kept, x_ref, y_ref, scale, f_wide, g_wide, row_high, row_sum, col_high, col_sum):
    for ref in (row_high, col_high):
        ref[...] = jnp.full(ref.shape, NEG, jnp.float32)
    for ref in (row_sum, col_sum):
        ref[...] = jnp.zeros(ref.shape, jnp.float32)

    def visit(s, t):
        xs, yt = x_ref[s], y_ref[t]
        fold(cross(yt, xs), g_wide[t], scale, row_high, row_sum, s)
        fold(cross(xs, yt), f_wide[s], scale, col_high, col_sum, t)

    over_pairs(pairs_ref, kept, visit)


def sweep_kernel(first, n_row, n_col, scale, blocks, pairs_ref, count_ref, x_ref, y_ref, *rest):
    scratch = rest[-6:]
    f_wide, g_wide, row_high, row_sum, col_high, col_sum = scratch
    f, g, outs = start_potentials(
        x_ref, y_ref, rest[:-6], first, n_row, n_col, scale, blocks, f_wide, g_wide
    )
    f_out, g_out, row_out, col_out = outs
    f_out[...] = f
    g_out[...] = g
    pass_sums(pairs_ref, count_ref[0], x_ref, y_ref, scale, *scratch)
    row_out[...] = settle(row_high, row_sum, blocks)
    col_out[...] = settle(col_high, col_sum, blocks)


def split_two(w):
    high = w.astype(jnp.bfloat16)
    return high, (w - high.astype(jnp.float32)).astype(jnp.bfloat16)


def weigh(scores, scale, lanes, wide):
    halves = []
    for h in range(2):
        at = slice(128 * h, 128 * h + 128)
        t = (scores[:, at] * scale - wide).reshape(BLK // 8, 8, 128) + lanes[:, at][None]
        halves.append(jnp.exp2(t).reshape(BLK, 128))
    return jnp.concatenate(halves, axis=1)


def emit(image, log_sums, blocks, out_ref):
    n, rows = out_ref.shape[0], (blocks * BLK) // out_ref.shape[0]
    lane = lax.broadcasted_iota(jnp.int32, (1, BLK), 1)
    shifted = {}
    for b in range(n):
        done = 0
        while done < rows:
            at = b * rows + done
            k, off = at // BLK, at % BLK
            take = min(rows - done, BLK - off)
            out_ref[b, done : done + take, :] = image[k, off : off + take, :]
            done += take
        for part in range(0, rows, BLK):
            at = b * rows + part
            k, off = at // BLK, at % BLK
            if off not in shifted:
                shifted[off] = pltpu.roll(log_sums, BLK - off, 1) if off else log_sums
            turned = shifted[off]
            line = turned[k : k + 1]
            if off and k + 1 < blocks:
                line = jnp.where(lane < BLK - off, line, turned[k + 1 : k + 2])
            spot = rows + part // BLK
            out_ref[b, spot : spot + 1, :] = line


def project_kernel(n_row, n_col, scale, blocks, pairs_ref, count_ref, x_ref, y_ref, *rest):
    scratch = rest[-6:]
    f_wide, g_wide, row_high, row_sum, col_high, col_sum = scratch
    f_lanes, g_lanes, forward, backward = rest[-10:-6]
    f, g, outs = start_potentials(
        x_ref, y_ref, rest[:-10], False, n_row, n_col, scale, blocks, f_wide, g_wide
    )
    forward_out, backward_out = outs
    kept = count_ref[0]
    pass_sums(pairs_ref, kept, x_ref, y_ref, scale, *scratch)
    row = settle(row_high, row_sum, blocks)
    col = settle(col_high, col_sum, blocks)
    for b in range(blocks):
        f_lanes[b] = jnp.broadcast_to(f[b : b + 1], (8, BLK))
        g_lanes[b] = jnp.broadcast_to(g[b : b + 1], (8, BLK))
    down_rows(row, blocks, f_wide)
    down_rows(col, blocks, g_wide)
    forward[...] = jnp.zeros(forward.shape, jnp.float32)
    backward[...] = jnp.zeros(backward.shape, jnp.float32)

    def visit(s, t):
        xs, yt = x_ref[s], y_ref[t]
        high, low = split_two(weigh(cross(xs, yt), scale, g_lanes[t], f_wide[s]))
        forward[s] += jnp.dot(high, yt, preferred_element_type=jnp.float32) + jnp.dot(
            low, yt, preferred_element_type=jnp.float32
        )
        high, low = split_two(weigh(cross(yt, xs), scale, f_lanes[s], g_wide[t]))
        backward[t] += jnp.dot(high, xs, preferred_element_type=jnp.float32) + jnp.dot(
            low, xs, preferred_element_type=jnp.float32
        )

    over_pairs(pairs_ref, kept, visit)
    emit(forward, row, blocks, forward_out)
    emit(backward, col, blocks, backward_out)


def merge_kernel(rows, parts_ref, out_ref):
    n = parts_ref.shape[0]
    for part in range(0, rows, BLK):
        spot = rows + part // BLK
        size = min(BLK, rows - part)
        logs = jnp.concatenate([parts_ref[d, spot : spot + 1, :] for d in range(n)], axis=0)
        high = jnp.max(logs, axis=0, keepdims=True)
        lifted = jnp.exp2(logs - high)
        weights = lifted / jnp.sum(lifted, axis=0, keepdims=True)
        upright = jnp.transpose(weights)
        total = jnp.zeros((size, BLK), jnp.float32)
        for d in range(n):
            total += upright[:size, d : d + 1] * parts_ref[d, part : part + size, :]
        out_ref[part : part + size, :] = total


def in_vmem(n):
    return [pl.BlockSpec(memory_space=pltpu.VMEM)] * n


def shape(*dims):
    return jax.ShapeDtypeStruct(dims, jnp.float32)


def sums_scratch(blocks):
    return [pltpu.VMEM((blocks, BLK, 128), jnp.float32)] * 2 + [
        pltpu.VMEM((blocks, 8, BLK), jnp.float32)
    ] * 4


def gather_by_permutes(mine, axis, moves):
    return [mine] + [lax.ppermute(mine, axis, move) for move in moves]


def turns(groups):
    size = len(groups[0])
    return [
        [(g[k], g[(k + r) % size]) for g in groups for k in range(size)] for r in range(1, size)
    ]


def per_device(n_src, n_tgt, sources, targets, pairs, counts):
    width = sources.shape[1]
    scale = math.log2(math.e) / (math.sqrt(width) / 4.0)
    blocks = sources.shape[0] // BLK
    x = sources.reshape(blocks, BLK, width)
    y = targets.reshape(blocks, BLK, width)
    pair_list = pairs.reshape(-1)
    kept = counts.reshape(-1)
    head = [pl.BlockSpec(memory_space=pltpu.SMEM)] * 2 + in_vmem(2)
    params = pltpu.CompilerParams(vmem_limit_bytes=VMEM_BYTES)

    def sweep(first, extra, n_row, n_col):
        return pl.pallas_call(
            functools.partial(sweep_kernel, first, n_row, n_col, scale, blocks),
            out_shape=[shape(8, BLK)] * 4,
            in_specs=head + in_vmem(len(extra)),
            out_specs=in_vmem(4),
            scratch_shapes=sums_scratch(blocks),
            compiler_params=params,
        )(pair_list, kept, x, y, *extra)

    all_tgt = turns([list(range(n_tgt))])
    near = turns([list(range(k, k + 4)) for k in range(0, n_src, 4)])
    far = turns([list(range(k, n_src, 4)) for k in range(4)])

    f, g, row, col = sweep(True, [], 0, 0)
    rows = gather_by_permutes(row, "tgt", all_tgt)
    cols = [lax.all_gather(col, "src")]
    f, g, row, col = sweep(False, [f, g, *rows, *cols], len(rows), len(cols))

    rows = [lax.all_gather(row, "tgt")]
    col = log_sum(gather_by_permutes(col, "src", near))
    cols = gather_by_permutes(col, "src", far)
    extra = [f, g, *rows, *cols]
    f_rows, b_rows = blocks * BLK // n_tgt, blocks * BLK // n_src
    forward, backward = pl.pallas_call(
        functools.partial(project_kernel, len(rows), len(cols), scale, blocks),
        out_shape=[shape(n_tgt, f_rows + 8, width), shape(n_src, b_rows + 8, width)],
        in_specs=head + in_vmem(len(extra)),
        out_specs=in_vmem(2),
        scratch_shapes=[pltpu.VMEM((blocks, 8, BLK), jnp.float32)] * 2
        + [pltpu.VMEM((blocks, BLK, width), jnp.float32)] * 2
        + sums_scratch(blocks),
        compiler_params=params,
    )(pair_list, kept, x, y, *extra)

    def merge(parts, rows):
        return pl.pallas_call(
            functools.partial(merge_kernel, rows),
            out_shape=shape(rows, width),
            in_specs=in_vmem(1),
            out_specs=pl.BlockSpec(memory_space=pltpu.VMEM),
            compiler_params=params,
        )(parts)

    forward = lax.all_to_all(forward, "tgt", 0, 0, tiled=True)
    backward = lax.all_to_all(backward, "src", 0, 0, tiled=True)
    return (merge(forward, f_rows), merge(backward, b_rows))


def solution(mesh):
    return jax.shard_map(
        functools.partial(per_device, mesh.shape["src"], mesh.shape["tgt"]),
        mesh=mesh,
        in_specs=(P("src", None), P("tgt", None), P("src", "tgt", None, None), P("src", "tgt")),
        out_specs=(P(("src", "tgt"), None), P(("tgt", "src"), None)),
        check_vma=False,
    )
```

```python
import functools
import math

import jax
import jax.numpy as jnp
from jax import lax
from jax.experimental import pallas as pl
from jax.experimental.pallas import tpu as pltpu
from jax.sharding import PartitionSpec as P

BLK = 256
ITERS = 2
NEG = -1e30
VMEM_BYTES = 24 * 1024 * 1024


def log_sum(parts):
    high = functools.reduce(jnp.maximum, parts)
    total = functools.reduce(jnp.add, [jnp.exp2(part - high) for part in parts])
    return high + jnp.log2(total)


def down_rows(lanes, blocks, wide_ref):
    upright = jnp.transpose(lanes)
    for b in range(blocks):
        wide_ref[b] = jnp.broadcast_to(upright[:, b : b + 1], (BLK, 128))


def norms(z_ref, scale, blocks, wide_ref):
    lane = lax.broadcasted_iota(jnp.int32, (BLK, 128), 1)
    gathered = jnp.zeros((BLK, 128), jnp.float32)
    for b in range(blocks):
        z = z_ref[b].astype(jnp.float32)
        half = jnp.sum(z * z, axis=1, keepdims=True) * (-0.5 * scale)
        wide = jnp.broadcast_to(half, (BLK, 128))
        wide_ref[b] = wide
        gathered = jnp.where(lane == b, wide, gathered)
    return jnp.transpose(gathered)[:8]


def over_pairs(pairs_ref, kept, visit):
    def two(step, carry):
        p = 2 * step
        visit(pairs_ref[2 * p], pairs_ref[2 * p + 1])
        visit(pairs_ref[2 * p + 2], pairs_ref[2 * p + 3])
        return carry

    lax.fori_loop(0, kept // 2, two, 0)

    @pl.when(kept % 2 == 1)
    def _():
        p = kept - 1
        visit(pairs_ref[2 * p], pairs_ref[2 * p + 1])


def cross(a, b):
    return lax.dot_general(a, b, (((1,), (1,)), ((), ())), preferred_element_type=jnp.float32)


def fold(scores, wide, scale, high_ref, sum_ref, b):
    for h in range(2):
        at = slice(128 * h, 128 * h + 128)
        t = (scores[:, at] * scale + wide).reshape(BLK // 8, 8, 128)
        old = high_ref[b, :, at]
        high = jnp.maximum(old, jnp.max(t, axis=0))
        total = jnp.sum(jnp.exp2(t - high[None]), axis=0)
        sum_ref[b, :, at] = sum_ref[b, :, at] * jnp.exp2(old - high) + total
        high_ref[b, :, at] = high


def settle(high_ref, sum_ref, blocks):
    rows = []
    for b in range(blocks):
        high = high_ref[b]
        top = jnp.max(high, axis=0, keepdims=True)
        total = jnp.sum(sum_ref[b] * jnp.exp2(high - top), axis=0, keepdims=True)
        rows.append(top + jnp.log2(total))
    rows += [jnp.zeros((1, BLK), jnp.float32)] * (8 - blocks)
    return jnp.concatenate(rows, axis=0)


def start_potentials(x_ref, y_ref, rest, first, n_row, n_col, scale, blocks, f_wide, g_wide):
    if first:
        return norms(x_ref, scale, blocks, f_wide), norms(y_ref, scale, blocks, g_wide), rest
    f_old, g_old = rest[0][...], rest[1][...]
    rows = [part for r in rest[2 : 2 + n_row] for part in parts_of(r)]
    cols = [part for r in rest[2 + n_row : 2 + n_row + n_col] for part in parts_of(r)]
    f = 0.5 * (f_old - log_sum(rows))
    g = 0.5 * (g_old - log_sum(cols))
    down_rows(f, blocks, f_wide)
    down_rows(g, blocks, g_wide)
    return f, g, rest[2 + n_row + n_col :]


def parts_of(ref):
    if len(ref.shape) == 2:
        return [ref[...]]
    return [ref[k] for k in range(ref.shape[0])]


def pass_sums(pairs_ref, kept, x_ref, y_ref, scale, f_wide, g_wide, row_high, row_sum, col_high, col_sum):
    for ref in (row_high, col_high):
        ref[...] = jnp.full(ref.shape, NEG, jnp.float32)
    for ref in (row_sum, col_sum):
        ref[...] = jnp.zeros(ref.shape, jnp.float32)

    def visit(s, t):
        xs, yt = x_ref[s], y_ref[t]
        fold(cross(yt, xs), g_wide[t], scale, row_high, row_sum, s)
        fold(cross(xs, yt), f_wide[s], scale, col_high, col_sum, t)

    over_pairs(pairs_ref, kept, visit)


def sweep_kernel(first, n_row, n_col, scale, blocks, pairs_ref, count_ref, x_ref, y_ref, *rest):
    scratch = rest[-6:]
    f_wide, g_wide, row_high, row_sum, col_high, col_sum = scratch
    f, g, outs = start_potentials(
        x_ref, y_ref, rest[:-6], first, n_row, n_col, scale, blocks, f_wide, g_wide
    )
    f_out, g_out, row_out, col_out = outs
    f_out[...] = f
    g_out[...] = g
    pass_sums(pairs_ref, count_ref[0], x_ref, y_ref, scale, *scratch)
    row_out[...] = settle(row_high, row_sum, blocks)
    col_out[...] = settle(col_high, col_sum, blocks)


def split_two(w):
    high = w.astype(jnp.bfloat16)
    return high, (w - high.astype(jnp.float32)).astype(jnp.bfloat16)


def weigh(scores, scale, lanes, wide):
    halves = []
    for h in range(2):
        at = slice(128 * h, 128 * h + 128)
        t = (scores[:, at] * scale - wide).reshape(BLK // 8, 8, 128) + lanes[:, at][None]
        halves.append(jnp.exp2(t).reshape(BLK, 128))
    return jnp.concatenate(halves, axis=1)


def receivers_lines(log_sums, n, blocks):
    rows = blocks * BLK // n
    lane = lax.broadcasted_iota(jnp.int32, (1, BLK), 1)
    shifted, lines = {}, []
    for b in range(n):
        k, off = b * rows // BLK, b * rows % BLK
        if off not in shifted:
            shifted[off] = pltpu.roll(log_sums, BLK - off, 1) if off else log_sums
        line = shifted[off][k : k + 1]
        if off and k + 1 < blocks:
            line = jnp.where(lane < BLK - off, line, shifted[off][k + 1 : k + 2])
        lines.append(line)
    return lines


def images(pairs_ref, kept, a_ref, b_ref, scale, lanes, wide, image_ref, turned):
    image_ref[...] = jnp.zeros(image_ref.shape, jnp.float32)

    def visit(s, t):
        a, b = (t, s) if turned else (s, t)
        at, bt = a_ref[a], b_ref[b]
        high, low = split_two(weigh(cross(at, bt), scale, lanes[b], wide[a]))
        rows = pl.ds(pl.multiple_of(a * BLK, BLK), BLK)
        image_ref[rows, :] += jnp.dot(high, bt, preferred_element_type=jnp.float32) + jnp.dot(
            low, bt, preferred_element_type=jnp.float32
        )

    over_pairs(pairs_ref, kept, visit)


def spread_lanes(values, blocks, lanes_ref):
    for b in range(blocks):
        lanes_ref[b] = jnp.broadcast_to(values[b : b + 1], (8, BLK))


def backward_kernel(n_row, n_col, scale, blocks, core_ref, pairs_ref, count_ref, x_ref, y_ref, *rest):
    scratch = rest[-6:]
    f_wide, g_wide, row_high, row_sum, col_high, col_sum = scratch
    lanes, backward = rest[-8:-6]
    f, g, outs = start_potentials(
        x_ref, y_ref, rest[:-8], False, n_row, n_col, scale, blocks, f_wide, g_wide
    )
    g_out, row_out, keep_out, send_out = outs
    kept = count_ref[0]
    pass_sums(pairs_ref, kept, x_ref, y_ref, scale, *scratch)
    g_out[...] = g
    row_out[...] = settle(row_high, row_sum, blocks)
    col = settle(col_high, col_sum, blocks)
    spread_lanes(f, blocks, lanes)
    down_rows(col, blocks, g_wide)
    images(pairs_ref, kept, y_ref, x_ref, scale, lanes, g_wide, backward, True)
    half = keep_out.shape[0]
    rows = blocks * BLK // (2 * half)
    lines = receivers_lines(col, 2 * half, blocks)
    core = core_ref[0]
    for q in range(half):
        for ref, side in ((keep_out, core), (send_out, 1 - core)):
            first = pl.multiple_of((2 * q + side) * rows, 16)
            ref[q, :rows, :] = backward[pl.ds(first, rows), :]
            ref[q, rows : rows + 1, :] = jnp.where(side == 0, lines[2 * q], lines[2 * q + 1])


def forward_kernel(scale, blocks, pairs_ref, count_ref, x_ref, y_ref, g_ref, row_ref, out, lanes, wide, forward):
    row = row_ref[...]
    spread_lanes(g_ref[...], blocks, lanes)
    down_rows(row, blocks, wide)
    images(pairs_ref, count_ref[0], x_ref, y_ref, scale, lanes, wide, forward, False)
    n = out.shape[0]
    rows = blocks * BLK // n
    lines = receivers_lines(row, n, blocks)
    for b in range(n):
        out[b, :rows, :] = forward[b * rows : (b + 1) * rows, :]
        out[b, rows : rows + 1, :] = lines[b]


def pair_kernel(rows, a_ref, b_ref, out_ref):
    n = a_ref.shape[0]
    a = jnp.concatenate([a_ref[q, rows : rows + 1, :] for q in range(n)], axis=0)
    b = jnp.concatenate([b_ref[q, rows : rows + 1, :] for q in range(n)], axis=0)
    high = jnp.maximum(a, b)
    both = jnp.exp2(a - high) + jnp.exp2(b - high)
    merged = high + jnp.log2(both)
    a_part = jnp.transpose(jnp.exp2(a - high) / both)
    b_part = jnp.transpose(jnp.exp2(b - high) / both)
    for q in range(n):
        out_ref[q, :rows, :] = (
            a_part[:rows, q : q + 1] * a_ref[q, :rows, :]
            + b_part[:rows, q : q + 1] * b_ref[q, :rows, :]
        )
        out_ref[q, rows : rows + 1, :] = merged[q : q + 1]


def merge_kernel(rows, parts_ref, out_ref):
    n = parts_ref.shape[0]
    logs = jnp.concatenate([parts_ref[d, rows : rows + 1, :] for d in range(n)], axis=0)
    lifted = jnp.exp2(logs - jnp.max(logs, axis=0, keepdims=True))
    upright = jnp.transpose(lifted / jnp.sum(lifted, axis=0, keepdims=True))
    total = jnp.zeros((rows, BLK), jnp.float32)
    for d in range(n):
        total += upright[:rows, d : d + 1] * parts_ref[d, :rows, :]
    out_ref[...] = total


def in_vmem(n):
    return [pl.BlockSpec(memory_space=pltpu.VMEM)] * n


def shape(*dims):
    return jax.ShapeDtypeStruct(dims, jnp.float32)


def sums_scratch(blocks):
    return [pltpu.VMEM((blocks, BLK, 128), jnp.float32)] * 2 + [
        pltpu.VMEM((blocks, 8, BLK), jnp.float32)
    ] * 4


def per_device(n_src, n_tgt, sources, targets, pairs, counts):
    width = sources.shape[1]
    scale = math.log2(math.e) / (math.sqrt(width) / 4.0)
    blocks = sources.shape[0] // BLK
    x = sources.reshape(blocks, BLK, width)
    y = targets.reshape(blocks, BLK, width)
    pair_list = pairs.reshape(-1)
    kept = counts.reshape(-1)
    head = [pl.BlockSpec(memory_space=pltpu.SMEM)] * 2 + in_vmem(2)
    params = pltpu.CompilerParams(vmem_limit_bytes=VMEM_BYTES)

    def sweep(first, extra, n_row, n_col):
        return pl.pallas_call(
            functools.partial(sweep_kernel, first, n_row, n_col, scale, blocks),
            out_shape=[shape(8, BLK)] * 4,
            in_specs=head + in_vmem(len(extra)),
            out_specs=in_vmem(4),
            scratch_shapes=sums_scratch(blocks),
            compiler_params=params,
        )(pair_list, kept, x, y, *extra)

    def spread(mine, axis, size, groups=None):
        copies = jnp.broadcast_to(mine[None], (size, *mine.shape))
        return lax.all_to_all(copies, axis, 0, 0, axis_index_groups=groups, tiled=True)

    near = [list(range(k, k + 4)) for k in range(0, n_src, 4)]
    far = [list(range(k, n_src, 4)) for k in range(4)]

    f, g, row, col = sweep(True, [], 0, 0)
    rows = spread(row, "tgt", n_tgt)
    cols = spread(col, "src", n_src)
    f, g, row, col = sweep(False, [f, g, rows, cols], 1, 1)

    rows = spread(row, "tgt", n_tgt)
    col = log_sum(list(spread(col, "src", 4, near)))
    cols = spread(col, "src", n_src // 4, far)

    f_rows, b_rows = blocks * BLK // n_tgt, blocks * BLK // n_src
    half = n_src // 2
    core = lax.axis_index("src").astype(jnp.int32) % 2
    g, row, keep, send = pl.pallas_call(
        functools.partial(backward_kernel, 1, 1, scale, blocks),
        out_shape=[shape(8, BLK)] * 2 + [shape(half, b_rows + 8, width)] * 2,
        in_specs=[pl.BlockSpec(memory_space=pltpu.SMEM)] + head + in_vmem(4),
        out_specs=in_vmem(4),
        scratch_shapes=[
            pltpu.VMEM((blocks, 8, BLK), jnp.float32),
            pltpu.VMEM((blocks * BLK, width), jnp.float32),
        ]
        + sums_scratch(blocks),
        compiler_params=params,
    )(core.reshape(1), pair_list, kept, x, y, f, g, rows, cols)
    came = lax.ppermute(send, "src", [(k, k ^ 1) for k in range(n_src)])
    forward = pl.pallas_call(
        functools.partial(forward_kernel, scale, blocks),
        out_shape=shape(n_tgt, f_rows + 8, width),
        in_specs=head + in_vmem(2),
        out_specs=pl.BlockSpec(memory_space=pltpu.VMEM),
        scratch_shapes=[
            pltpu.VMEM((blocks, 8, BLK), jnp.float32),
            pltpu.VMEM((blocks, BLK, 128), jnp.float32),
            pltpu.VMEM((blocks * BLK, width), jnp.float32),
        ],
        compiler_params=params,
        cost_estimate=pl.CostEstimate(flops=3 * 10**9, bytes_accessed=4 * 10**6, transcendentals=0),
    )(pair_list, kept, x, y, g, row)
    backward = pl.pallas_call(
        functools.partial(pair_kernel, b_rows),
        out_shape=shape(half, b_rows + 8, width),
        in_specs=in_vmem(2),
        out_specs=pl.BlockSpec(memory_space=pltpu.VMEM),
        compiler_params=params,
    )(keep, came)

    def merge(parts, rows):
        return pl.pallas_call(
            functools.partial(merge_kernel, rows),
            out_shape=shape(rows, width),
            in_specs=in_vmem(1),
            out_specs=pl.BlockSpec(memory_space=pltpu.VMEM),
            compiler_params=params,
        )(parts)

    same_core = [list(range(k, n_src, 2)) for k in range(2)]
    backward = lax.all_to_all(backward, "src", 0, 0, axis_index_groups=same_core, tiled=True)
    forward = lax.all_to_all(forward, "tgt", 0, 0, tiled=True)
    return (merge(forward, f_rows), merge(backward, b_rows))


def solution(mesh):
    return jax.shard_map(
        functools.partial(per_device, mesh.shape["src"], mesh.shape["tgt"]),
        mesh=mesh,
        in_specs=(P("src", None), P("tgt", None), P("src", "tgt", None, None), P("src", "tgt")),
        out_specs=(P(("src", "tgt"), None), P(("tgt", "src"), None)),
        check_vma=False,
    )
```

```python
import functools
import math

import jax
import jax.numpy as jnp
from jax import lax
from jax.experimental import pallas as pl
from jax.experimental.pallas import tpu as pltpu
from jax.sharding import PartitionSpec as P

BLK = 256
ITERS = 2
NEG = -1e30
VMEM_BYTES = 24 * 1024 * 1024


def log_sum(parts):
    high = functools.reduce(jnp.maximum, parts)
    total = functools.reduce(jnp.add, [jnp.exp2(part - high) for part in parts])
    return high + jnp.log2(total)


def down_rows(lanes, blocks, wide_ref):
    upright = jnp.transpose(lanes)
    for b in range(blocks):
        wide_ref[b] = jnp.broadcast_to(upright[:, b : b + 1], (BLK, 128))


def norms(z_ref, scale, blocks, wide_ref):
    lane = lax.broadcasted_iota(jnp.int32, (BLK, 128), 1)
    gathered = jnp.zeros((BLK, 128), jnp.float32)
    for b in range(blocks):
        z = z_ref[b].astype(jnp.float32)
        half = jnp.sum(z * z, axis=1, keepdims=True) * (-0.5 * scale)
        wide = jnp.broadcast_to(half, (BLK, 128))
        wide_ref[b] = wide
        gathered = jnp.where(lane == b, wide, gathered)
    return jnp.transpose(gathered)[:8]


def over_pairs(pairs_ref, kept, visit):
    def two(step, carry):
        p = 2 * step
        visit(pairs_ref[0, p], pairs_ref[1, p])
        visit(pairs_ref[0, p + 1], pairs_ref[1, p + 1])
        return carry

    lax.fori_loop(0, kept // 2, two, 0)

    @pl.when(kept % 2 == 1)
    def _():
        p = kept - 1
        visit(pairs_ref[0, p], pairs_ref[1, p])


def cross(a, b):
    return lax.dot_general(a, b, (((1,), (1,)), ((), ())), preferred_element_type=jnp.float32)


def fold(scores, wide, scale, high_ref, sum_ref, b):
    for h in range(2):
        at = slice(128 * h, 128 * h + 128)
        t = (scores[:, at] * scale + wide).reshape(BLK // 8, 8, 128)
        old = high_ref[b, :, at]
        high = jnp.maximum(old, jnp.max(t, axis=0))
        total = jnp.sum(jnp.exp2(t - high[None]), axis=0)
        sum_ref[b, :, at] = sum_ref[b, :, at] * jnp.exp2(old - high) + total
        high_ref[b, :, at] = high


def settle(high_ref, sum_ref, blocks):
    rows = []
    for b in range(blocks):
        high = high_ref[b]
        top = jnp.max(high, axis=0, keepdims=True)
        total = jnp.sum(sum_ref[b] * jnp.exp2(high - top), axis=0, keepdims=True)
        rows.append(top + jnp.log2(total))
    rows += [jnp.zeros((1, BLK), jnp.float32)] * (8 - blocks)
    return jnp.concatenate(rows, axis=0)


def start_potentials(x_ref, y_ref, rest, first, n_row, n_col, scale, blocks, f_wide, g_wide):
    if first:
        return norms(x_ref, scale, blocks, f_wide), norms(y_ref, scale, blocks, g_wide), rest
    f_old, g_old = rest[0][...], rest[1][...]
    rows = [part for r in rest[2 : 2 + n_row] for part in parts_of(r)]
    cols = [part for r in rest[2 + n_row : 2 + n_row + n_col] for part in parts_of(r)]
    f = 0.5 * (f_old - log_sum(rows))
    g = 0.5 * (g_old - log_sum(cols))
    down_rows(f, blocks, f_wide)
    down_rows(g, blocks, g_wide)
    return f, g, rest[2 + n_row + n_col :]


def parts_of(ref):
    if len(ref.shape) == 2:
        return [ref[...]]
    return [ref[k] for k in range(ref.shape[0])]


def pass_sums(pairs_ref, kept, x_ref, y_ref, scale, f_wide, g_wide, row_high, row_sum, col_high, col_sum):
    for ref in (row_high, col_high):
        ref[...] = jnp.full(ref.shape, NEG, jnp.float32)
    for ref in (row_sum, col_sum):
        ref[...] = jnp.zeros(ref.shape, jnp.float32)

    def visit(s, t):
        xs, yt = x_ref[s], y_ref[t]
        fold(cross(yt, xs), g_wide[t], scale, row_high, row_sum, s)
        fold(cross(xs, yt), f_wide[s], scale, col_high, col_sum, t)

    over_pairs(pairs_ref, kept, visit)


def sweep_kernel(first, n_row, n_col, scale, blocks, pairs_ref, count_ref, x_ref, y_ref, *rest):
    scratch = rest[-6:]
    f_wide, g_wide, row_high, row_sum, col_high, col_sum = scratch
    f, g, outs = start_potentials(
        x_ref, y_ref, rest[:-6], first, n_row, n_col, scale, blocks, f_wide, g_wide
    )
    f_out, g_out, row_out, col_out = outs
    f_out[...] = f
    g_out[...] = g
    pass_sums(pairs_ref, count_ref[0], x_ref, y_ref, scale, *scratch)
    row_out[...] = settle(row_high, row_sum, blocks)
    col_out[...] = settle(col_high, col_sum, blocks)


def split_two(w):
    high = w.astype(jnp.bfloat16)
    return high, (w - high.astype(jnp.float32)).astype(jnp.bfloat16)


def weigh(scores, scale, lanes, wide):
    halves = []
    for h in range(2):
        at = slice(128 * h, 128 * h + 128)
        t = (scores[:, at] * scale - wide).reshape(BLK // 8, 8, 128) + lanes[:, at][None]
        halves.append(jnp.exp2(t).reshape(BLK, 128))
    return jnp.concatenate(halves, axis=1)


def receivers_lines(log_sums, n, blocks):
    rows = blocks * BLK // n
    lane = lax.broadcasted_iota(jnp.int32, (1, BLK), 1)
    shifted, lines = {}, []
    for b in range(n):
        k, off = b * rows // BLK, b * rows % BLK
        if off not in shifted:
            shifted[off] = pltpu.roll(log_sums, BLK - off, 1) if off else log_sums
        line = shifted[off][k : k + 1]
        if off and k + 1 < blocks:
            line = jnp.where(lane < BLK - off, line, shifted[off][k + 1 : k + 2])
        lines.append(line)
    return lines


def images(pairs_ref, kept, a_ref, b_ref, scale, lanes, wide, image_ref, turned):
    image_ref[...] = jnp.zeros(image_ref.shape, jnp.float32)

    def visit(s, t):
        a, b = (t, s) if turned else (s, t)
        at, bt = a_ref[a], b_ref[b]
        high, low = split_two(weigh(cross(at, bt), scale, lanes[b], wide[a]))
        rows = pl.ds(pl.multiple_of(a * BLK, BLK), BLK)
        image_ref[rows, :] += jnp.dot(high, bt, preferred_element_type=jnp.float32) + jnp.dot(
            low, bt, preferred_element_type=jnp.float32
        )

    over_pairs(pairs_ref, kept, visit)


def spread_lanes(values, blocks, lanes_ref):
    for b in range(blocks):
        lanes_ref[b] = jnp.broadcast_to(values[b : b + 1], (8, BLK))


def backward_kernel(n_row, n_col, scale, blocks, core_ref, pairs_ref, count_ref, x_ref, y_ref, *rest):
    scratch = rest[-6:]
    f_wide, g_wide, row_high, row_sum, col_high, col_sum = scratch
    lanes, backward = rest[-8:-6]
    f, g, outs = start_potentials(
        x_ref, y_ref, rest[:-8], False, n_row, n_col, scale, blocks, f_wide, g_wide
    )
    g_out, row_out, keep_out, send_out = outs
    kept = count_ref[0]
    pass_sums(pairs_ref, kept, x_ref, y_ref, scale, *scratch)
    g_out[...] = g
    row_out[...] = settle(row_high, row_sum, blocks)
    col = settle(col_high, col_sum, blocks)
    spread_lanes(f, blocks, lanes)
    down_rows(col, blocks, g_wide)
    images(pairs_ref, kept, y_ref, x_ref, scale, lanes, g_wide, backward, True)
    half = keep_out.shape[0]
    rows = blocks * BLK // (2 * half)
    lines = receivers_lines(col, 2 * half, blocks)
    core = core_ref[0]
    for q in range(half):
        for ref, side in ((keep_out, core), (send_out, 1 - core)):
            first = pl.multiple_of((2 * q + side) * rows, 16)
            ref[q, :rows, :] = backward[pl.ds(first, rows), :]
            ref[q, rows : rows + 1, :] = jnp.where(side == 0, lines[2 * q], lines[2 * q + 1])


def forward_kernel(
    scale, blocks, place_ref, pairs_ref, count_ref, x_ref, y_ref, g_ref, row_ref, *rest
):
    outs, (lanes, wide, forward, lines_ref) = rest[:-4], rest[-4:]
    row = row_ref[...]
    spread_lanes(g_ref[...], blocks, lanes)
    down_rows(row, blocks, wide)
    images(pairs_ref, count_ref[0], x_ref, y_ref, scale, lanes, wide, forward, False)
    n = len(outs)
    rows = blocks * BLK // n
    for b, line in enumerate(receivers_lines(row, n, blocks)):
        lines_ref[b] = line
    for r, out in enumerate(outs):
        to = place_ref[0] ^ r
        out[:rows, :] = forward[pl.ds(pl.multiple_of(to * rows, 16), rows), :]
        out[rows : rows + 1, :] = lines_ref[to]


def pair_kernel(rows, a_ref, b_ref, out_ref):
    n = a_ref.shape[0]
    a = jnp.concatenate([a_ref[q, rows : rows + 1, :] for q in range(n)], axis=0)
    b = jnp.concatenate([b_ref[q, rows : rows + 1, :] for q in range(n)], axis=0)
    high = jnp.maximum(a, b)
    both = jnp.exp2(a - high) + jnp.exp2(b - high)
    merged = high + jnp.log2(both)
    a_part = jnp.transpose(jnp.exp2(a - high) / both)
    b_part = jnp.transpose(jnp.exp2(b - high) / both)
    for q in range(n):
        out_ref[q, :rows, :] = (
            a_part[:rows, q : q + 1] * a_ref[q, :rows, :]
            + b_part[:rows, q : q + 1] * b_ref[q, :rows, :]
        )
        out_ref[q, rows : rows + 1, :] = merged[q : q + 1]


def merge_kernel(rows, *refs):
    out_ref = refs[-1]
    parts = [p for ref in refs[:-1] for p in ([ref] if len(ref.shape) == 2 else [ref.at[d] for d in range(ref.shape[0])])]
    logs = jnp.concatenate([part[rows : rows + 1, :] for part in parts], axis=0)
    lifted = jnp.exp2(logs - jnp.max(logs, axis=0, keepdims=True))
    upright = jnp.transpose(lifted / jnp.sum(lifted, axis=0, keepdims=True))
    total = jnp.zeros((rows, BLK), jnp.float32)
    for d, part in enumerate(parts):
        total += upright[:rows, d : d + 1] * part[:rows, :]
    out_ref[...] = total


def in_vmem(n):
    return [pl.BlockSpec(memory_space=pltpu.VMEM)] * n


def shape(*dims):
    return jax.ShapeDtypeStruct(dims, jnp.float32)


def sums_scratch(blocks):
    return [pltpu.VMEM((blocks, BLK, 128), jnp.float32)] * 2 + [
        pltpu.VMEM((blocks, 8, BLK), jnp.float32)
    ] * 4


def per_device(n_src, n_tgt, sources, targets, pairs, counts):
    width = sources.shape[1]
    scale = math.log2(math.e) / (math.sqrt(width) / 4.0)
    blocks = sources.shape[0] // BLK
    x = sources.reshape(blocks, BLK, width)
    y = targets.reshape(blocks, BLK, width)
    pair_list = jnp.transpose(pairs[0, 0])
    kept = counts.reshape(-1)
    head = [pl.BlockSpec(memory_space=pltpu.SMEM)] * 2 + in_vmem(2)
    params = pltpu.CompilerParams(vmem_limit_bytes=VMEM_BYTES)

    def sweep(first, extra, n_row, n_col):
        return pl.pallas_call(
            functools.partial(sweep_kernel, first, n_row, n_col, scale, blocks),
            out_shape=[shape(8, BLK)] * 4,
            in_specs=head + in_vmem(len(extra)),
            out_specs=in_vmem(4),
            scratch_shapes=sums_scratch(blocks),
            compiler_params=params,
        )(pair_list, kept, x, y, *extra)

    def swap(value, axis, size, bit):
        return lax.ppermute(value, axis, [(k, k ^ bit) for k in range(size)])

    def butterfly(row, col):
        bit = 1
        while bit < max(n_src, n_tgt):
            row_came = swap(row, "tgt", n_tgt, bit) if bit < n_tgt else None
            col_came = swap(col, "src", n_src, bit) if bit < n_src else None
            if 2 * bit < n_tgt:
                row = log_sum([row, row_came])
            elif 2 * bit == n_tgt:
                rows = [row, row_came]
            if 2 * bit < n_src:
                col = log_sum([col, col_came])
            elif 2 * bit == n_src:
                cols = [col, col_came]
            bit *= 2
        return rows, cols

    f, g, row, col = sweep(True, [], 0, 0)
    rows, cols = butterfly(row, col)
    f, g, row, col = sweep(False, [f, g, *rows, *cols], 2, 2)
    rows, cols = butterfly(row, col)

    f_rows, b_rows = blocks * BLK // n_tgt, blocks * BLK // n_src
    half = n_src // 2
    scalar = pl.BlockSpec(memory_space=pltpu.SMEM)
    core = lax.axis_index("src").astype(jnp.int32) % 2
    g, row, keep, send = pl.pallas_call(
        functools.partial(backward_kernel, 2, 2, scale, blocks),
        out_shape=[shape(8, BLK)] * 2 + [shape(half, b_rows + 8, width)] * 2,
        in_specs=[scalar] + head + in_vmem(6),
        out_specs=in_vmem(4),
        scratch_shapes=[
            pltpu.VMEM((blocks, 8, BLK), jnp.float32),
            pltpu.VMEM((blocks * BLK, width), jnp.float32),
        ]
        + sums_scratch(blocks),
        compiler_params=params,
    )(core.reshape(1), pair_list, kept, x, y, f, g, *rows, *cols)
    came = swap(send, "src", n_src, 1)
    forward = pl.pallas_call(
        functools.partial(forward_kernel, scale, blocks),
        out_shape=[shape(f_rows + 8, width)] * n_tgt,
        in_specs=[scalar] + head + in_vmem(2),
        out_specs=in_vmem(n_tgt),
        scratch_shapes=[
            pltpu.VMEM((blocks, 8, BLK), jnp.float32),
            pltpu.VMEM((blocks, BLK, 128), jnp.float32),
            pltpu.VMEM((blocks * BLK, width), jnp.float32),
            pltpu.VMEM((n_tgt, 1, BLK), jnp.float32),
        ],
        compiler_params=params,
        cost_estimate=pl.CostEstimate(flops=6 * 10**9, bytes_accessed=4 * 10**6, transcendentals=0),
    )(lax.axis_index("tgt").astype(jnp.int32).reshape(1), pair_list, kept, x, y, g, row)
    backward = pl.pallas_call(
        functools.partial(pair_kernel, b_rows),
        out_shape=shape(half, b_rows + 8, width),
        in_specs=in_vmem(2),
        out_specs=pl.BlockSpec(memory_space=pltpu.VMEM),
        compiler_params=params,
    )(keep, came)
    backward, forward = lax.optimization_barrier((backward, forward))

    def merge(parts, rows):
        return pl.pallas_call(
            functools.partial(merge_kernel, rows),
            out_shape=shape(rows, width),
            in_specs=in_vmem(len(parts)),
            out_specs=pl.BlockSpec(memory_space=pltpu.VMEM),
            compiler_params=params,
        )(*parts)

    same_core = [list(range(k, n_src, 2)) for k in range(2)]
    backward = lax.all_to_all(backward, "src", 0, 0, axis_index_groups=same_core, tiled=True)
    forward = [forward[0]] + [swap(forward[r], "tgt", n_tgt, r) for r in range(1, n_tgt)]
    return (merge(forward, f_rows), merge([backward], b_rows))


def solution(mesh):
    return jax.shard_map(
        functools.partial(per_device, mesh.shape["src"], mesh.shape["tgt"]),
        mesh=mesh,
        in_specs=(P("src", None), P("tgt", None), P("src", "tgt", None, None), P("src", "tgt")),
        out_specs=(P(("src", "tgt"), None), P(("tgt", "src"), None)),
        check_vma=False,
    )
```

```python
import functools
import math

import jax
import jax.numpy as jnp
from jax import lax
from jax.experimental import pallas as pl
from jax.experimental.pallas import tpu as pltpu
from jax.sharding import PartitionSpec as P

BLK = 256
ITERS = 2
NEG = -1e30
RING = 4
VMEM_BYTES = 24 * 1024 * 1024


def log_sum(parts):
    high = functools.reduce(jnp.maximum, parts)
    total = functools.reduce(jnp.add, [jnp.exp2(part - high) for part in parts])
    return high + jnp.log2(total)


def down_rows(lanes, blocks, wide_ref):
    upright = jnp.transpose(lanes)
    for b in range(blocks):
        wide_ref[b] = jnp.broadcast_to(upright[:, b : b + 1], (BLK, 128))


def norms(z_ref, scale, blocks, wide_ref):
    lane = lax.broadcasted_iota(jnp.int32, (BLK, 128), 1)
    gathered = jnp.zeros((BLK, 128), jnp.float32)
    for b in range(blocks):
        z = z_ref[b].astype(jnp.float32)
        half = jnp.sum(z * z, axis=1, keepdims=True) * (-0.5 * scale)
        wide = jnp.broadcast_to(half, (BLK, 128))
        wide_ref[b] = wide
        gathered = jnp.where(lane == b, wide, gathered)
    return jnp.transpose(gathered)[:8]


def over_pairs(pairs_ref, kept, visit):
    def two(step, carry):
        p = 2 * step
        visit(pairs_ref[0, p], pairs_ref[1, p])
        visit(pairs_ref[0, p + 1], pairs_ref[1, p + 1])
        return carry

    lax.fori_loop(0, kept // 2, two, 0)

    @pl.when(kept % 2 == 1)
    def _():
        p = kept - 1
        visit(pairs_ref[0, p], pairs_ref[1, p])


def cross(a, b):
    return lax.dot_general(a, b, (((1,), (1,)), ((), ())), preferred_element_type=jnp.float32)


def fold(scores, wide, scale, high_ref, sum_ref, b):
    for h in range(2):
        at = slice(128 * h, 128 * h + 128)
        t = (scores[:, at] * scale + wide).reshape(BLK // 8, 8, 128)
        old = high_ref[b, :, at]
        high = jnp.maximum(old, jnp.max(t, axis=0))
        total = jnp.sum(jnp.exp2(t - high[None]), axis=0)
        sum_ref[b, :, at] = sum_ref[b, :, at] * jnp.exp2(old - high) + total
        high_ref[b, :, at] = high


def settle(high_ref, sum_ref, blocks):
    rows = []
    for b in range(blocks):
        high = high_ref[b]
        top = jnp.max(high, axis=0, keepdims=True)
        total = jnp.sum(sum_ref[b] * jnp.exp2(high - top), axis=0, keepdims=True)
        rows.append(top + jnp.log2(total))
    rows += [jnp.zeros((1, BLK), jnp.float32)] * (8 - blocks)
    return jnp.concatenate(rows, axis=0)


def start_potentials(x_ref, y_ref, rest, first, n_row, n_col, scale, blocks, f_wide, g_wide):
    if first:
        return norms(x_ref, scale, blocks, f_wide), norms(y_ref, scale, blocks, g_wide), rest
    f_old, g_old = rest[0][...], rest[1][...]
    rows = [part for r in rest[2 : 2 + n_row] for part in parts_of(r)]
    cols = [part for r in rest[2 + n_row : 2 + n_row + n_col] for part in parts_of(r)]
    f = 0.5 * (f_old - log_sum(rows))
    g = 0.5 * (g_old - log_sum(cols))
    down_rows(f, blocks, f_wide)
    down_rows(g, blocks, g_wide)
    return f, g, rest[2 + n_row + n_col :]


def parts_of(ref):
    if len(ref.shape) == 2:
        return [ref[...]]
    return [ref[k] for k in range(ref.shape[0])]


def pass_sums(pairs_ref, kept, x_ref, y_ref, scale, f_wide, g_wide, row_high, row_sum, col_high, col_sum):
    for ref in (row_high, col_high):
        ref[...] = jnp.full(ref.shape, NEG, jnp.float32)
    for ref in (row_sum, col_sum):
        ref[...] = jnp.zeros(ref.shape, jnp.float32)

    def visit(s, t):
        xs, yt = x_ref[s], y_ref[t]
        fold(cross(yt, xs), g_wide[t], scale, row_high, row_sum, s)
        fold(cross(xs, yt), f_wide[s], scale, col_high, col_sum, t)

    over_pairs(pairs_ref, kept, visit)


def sweep_kernel(first, n_row, n_col, scale, blocks, pairs_ref, count_ref, x_ref, y_ref, *rest):
    scratch = rest[-6:]
    f_wide, g_wide, row_high, row_sum, col_high, col_sum = scratch
    f, g, outs = start_potentials(
        x_ref, y_ref, rest[:-6], first, n_row, n_col, scale, blocks, f_wide, g_wide
    )
    f_out, g_out, row_out, col_out = outs
    f_out[...] = f
    g_out[...] = g
    pass_sums(pairs_ref, count_ref[0], x_ref, y_ref, scale, *scratch)
    row_out[...] = settle(row_high, row_sum, blocks)
    col_out[...] = settle(col_high, col_sum, blocks)


def split_two(w):
    high = w.astype(jnp.bfloat16)
    return high, (w - high.astype(jnp.float32)).astype(jnp.bfloat16)


def weigh(scores, scale, lanes, wide):
    halves = []
    for h in range(2):
        at = slice(128 * h, 128 * h + 128)
        t = (scores[:, at] * scale - wide).reshape(BLK // 8, 8, 128) + lanes[:, at][None]
        halves.append(jnp.exp2(t).reshape(BLK, 128))
    return jnp.concatenate(halves, axis=1)


def receivers_lines(log_sums, n, blocks):
    rows = blocks * BLK // n
    lane = lax.broadcasted_iota(jnp.int32, (1, BLK), 1)
    shifted, lines = {}, []
    for b in range(n):
        k, off = b * rows // BLK, b * rows % BLK
        if off not in shifted:
            shifted[off] = pltpu.roll(log_sums, BLK - off, 1) if off else log_sums
        line = shifted[off][k : k + 1]
        if off and k + 1 < blocks:
            line = jnp.where(lane < BLK - off, line, shifted[off][k + 1 : k + 2])
        lines.append(line)
    return lines


def images(pairs_ref, kept, a_ref, b_ref, scale, lanes, wide, image_ref, turned):
    image_ref[...] = jnp.zeros(image_ref.shape, jnp.float32)

    def visit(s, t):
        a, b = (t, s) if turned else (s, t)
        at, bt = a_ref[a], b_ref[b]
        high, low = split_two(weigh(cross(at, bt), scale, lanes[b], wide[a]))
        rows = pl.ds(pl.multiple_of(a * BLK, BLK), BLK)
        image_ref[rows, :] += jnp.dot(high, bt, preferred_element_type=jnp.float32) + jnp.dot(
            low, bt, preferred_element_type=jnp.float32
        )

    over_pairs(pairs_ref, kept, visit)


def spread_lanes(values, blocks, lanes_ref):
    for b in range(blocks):
        lanes_ref[b] = jnp.broadcast_to(values[b : b + 1], (8, BLK))


def backward_kernel(n_row, n_col, scale, blocks, core_ref, pairs_ref, count_ref, x_ref, y_ref, *rest):
    scratch = rest[-6:]
    f_wide, g_wide, row_high, row_sum, col_high, col_sum = scratch
    lanes, backward = rest[-8:-6]
    f, g, outs = start_potentials(
        x_ref, y_ref, rest[:-8], False, n_row, n_col, scale, blocks, f_wide, g_wide
    )
    g_out, row_out, keep_out, send_out = outs
    kept = count_ref[0]
    pass_sums(pairs_ref, kept, x_ref, y_ref, scale, *scratch)
    g_out[...] = g
    row_out[...] = settle(row_high, row_sum, blocks)
    col = settle(col_high, col_sum, blocks)
    spread_lanes(f, blocks, lanes)
    down_rows(col, blocks, g_wide)
    images(pairs_ref, kept, y_ref, x_ref, scale, lanes, g_wide, backward, True)
    half = keep_out.shape[0]
    rows = blocks * BLK // (2 * half)
    lines = receivers_lines(col, 2 * half, blocks)
    core = core_ref[0]
    for q in range(half):
        for ref, side in ((keep_out, core), (send_out, 1 - core)):
            first = pl.multiple_of((2 * q + side) * rows, 16)
            ref[q, :rows, :] = backward[pl.ds(first, rows), :]
            ref[q, rows : rows + 1, :] = jnp.where(side == 0, lines[2 * q], lines[2 * q + 1])


def forward_kernel(
    scale, blocks, place_ref, pairs_ref, count_ref, x_ref, y_ref, g_ref, row_ref, *rest
):
    own, up, down, up_next, down_next = rest[:-4]
    lanes, wide, forward, lines_ref = rest[-4:]
    row = row_ref[...]
    spread_lanes(g_ref[...], blocks, lanes)
    down_rows(row, blocks, wide)
    images(pairs_ref, count_ref[0], x_ref, y_ref, scale, lanes, wide, forward, False)
    n = lines_ref.shape[0]
    rows = blocks * BLK // n
    for b, line in enumerate(receivers_lines(row, n, blocks)):
        lines_ref[b] = line
    me = place_ref[0]

    def put(out, r, high):
        to = ((me + r) % RING) + RING * high
        out[:rows, :] = forward[pl.ds(pl.multiple_of(to * rows, 16), rows), :]
        out[rows : rows + 1, :] = lines_ref[to]

    put(up.at[0], 2, 0)
    put(up.at[1], 1, 1)
    put(down.at[0], 2, 1)
    put(down.at[1], 3, 0)
    put(own.at[0], 0, 0)
    put(own.at[1], 0, 1)
    put(up_next, 1, 0)
    put(down_next, 3, 1)


def pair_kernel(rows, a_ref, b_ref, out_ref):
    n = a_ref.shape[0]
    a = jnp.concatenate([a_ref[q, rows : rows + 1, :] for q in range(n)], axis=0)
    b = jnp.concatenate([b_ref[q, rows : rows + 1, :] for q in range(n)], axis=0)
    high = jnp.maximum(a, b)
    both = jnp.exp2(a - high) + jnp.exp2(b - high)
    merged = high + jnp.log2(both)
    a_part = jnp.transpose(jnp.exp2(a - high) / both)
    b_part = jnp.transpose(jnp.exp2(b - high) / both)
    for q in range(n):
        out_ref[q, :rows, :] = (
            a_part[:rows, q : q + 1] * a_ref[q, :rows, :]
            + b_part[:rows, q : q + 1] * b_ref[q, :rows, :]
        )
        out_ref[q, rows : rows + 1, :] = merged[q : q + 1]


def blend(parts, rows):
    logs = jnp.concatenate([part[rows : rows + 1, :] for part in parts], axis=0)
    high = jnp.max(logs, axis=0, keepdims=True)
    lifted = jnp.exp2(logs - high)
    whole = jnp.sum(lifted, axis=0, keepdims=True)
    upright = jnp.transpose(lifted / whole)
    total = jnp.zeros((rows, BLK), jnp.float32)
    for d, part in enumerate(parts):
        total += upright[:rows, d : d + 1] * part[:rows, :]
    return total, high + jnp.log2(whole)


def put_blend(out, blended, rows):
    out[:rows, :] = blended[0]
    if out.shape[0] > rows:
        out[rows : rows + 1, :] = blended[1]


def z_kernel(rows, place_ref, parts_ref, keep_ref, send_ref):
    for out, low in ((keep_ref, place_ref[0]), (send_ref, 1 - place_ref[0])):
        parts = [parts_ref.at[d, low] for d in range(parts_ref.shape[0])]
        put_blend(out, blend(parts, rows), rows)


def relay_kernel(rows, up_next, up_came, down_next, down_came, up_out, down_out):
    put_blend(up_out, blend([up_next, up_came.at[0]], rows), rows)
    put_blend(down_out, blend([down_next, down_came.at[0]], rows), rows)


def x_kernel(rows, place_ref, own, up_came, down_came, up_second, down_second, keep_ref, send_ref):
    low = blend([own.at[0], up_second, down_came.at[1]], rows)
    high = blend([own.at[1], down_second, up_came.at[1]], rows)

    @pl.when(place_ref[0] == 0)
    def _():
        put_blend(keep_ref, low, rows)
        put_blend(send_ref, high, rows)

    @pl.when(place_ref[0] == 1)
    def _():
        put_blend(keep_ref, high, rows)
        put_blend(send_ref, low, rows)


def last_kernel(rows, a_ref, b_ref, out_ref):
    put_blend(out_ref, blend([a_ref, b_ref], rows), rows)


def in_vmem(n):
    return [pl.BlockSpec(memory_space=pltpu.VMEM)] * n


def shape(*dims):
    return jax.ShapeDtypeStruct(dims, jnp.float32)


def sums_scratch(blocks):
    return [pltpu.VMEM((blocks, BLK, 128), jnp.float32)] * 2 + [
        pltpu.VMEM((blocks, 8, BLK), jnp.float32)
    ] * 4


def per_device(n_src, n_tgt, sources, targets, pairs, counts):
    width = sources.shape[1]
    scale = math.log2(math.e) / (math.sqrt(width) / 4.0)
    blocks = sources.shape[0] // BLK
    x = sources.reshape(blocks, BLK, width)
    y = targets.reshape(blocks, BLK, width)
    pair_list = jnp.transpose(pairs[0, 0])
    kept = counts.reshape(-1)
    head = [pl.BlockSpec(memory_space=pltpu.SMEM)] * 2 + in_vmem(2)
    params = pltpu.CompilerParams(vmem_limit_bytes=VMEM_BYTES)

    def sweep(first, extra, n_row, n_col):
        return pl.pallas_call(
            functools.partial(sweep_kernel, first, n_row, n_col, scale, blocks),
            out_shape=[shape(8, BLK)] * 4,
            in_specs=head + in_vmem(len(extra)),
            out_specs=in_vmem(4),
            scratch_shapes=sums_scratch(blocks),
            compiler_params=params,
        )(pair_list, kept, x, y, *extra)

    def swap(value, axis, size, bit):
        return lax.ppermute(value, axis, [(k, k ^ bit) for k in range(size)])

    n_z = n_src // 4
    along_z = [list(range(k, n_src, 4)) for k in range(4)]

    def exchange(row, col):
        col = log_sum([col, swap(col, "src", n_src, 1)])
        row = log_sum([row, swap(row, "tgt", n_tgt, 1)])
        col = log_sum([col, swap(col, "src", n_src, 2)])
        row = log_sum([row, swap(row, "tgt", n_tgt, 2)])
        copies = jnp.broadcast_to(col[None], (n_z, *col.shape))
        cols = lax.all_to_all(copies, "src", 0, 0, axis_index_groups=along_z, tiled=True)
        return [row, swap(row, "tgt", n_tgt, 4)], [cols]

    f, g, row, col = sweep(True, [], 0, 0)
    rows, cols = exchange(row, col)
    f, g, row, col = sweep(False, [f, g, *rows, *cols], 2, 1)
    rows, cols = exchange(row, col)

    f_rows, b_rows = blocks * BLK // n_tgt, blocks * BLK // n_src
    half = n_src // 2
    scalar = pl.BlockSpec(memory_space=pltpu.SMEM)
    s_at = lax.axis_index("src").astype(jnp.int32).reshape(1)
    t_at = lax.axis_index("tgt").astype(jnp.int32).reshape(1)

    def call(kernel, operands, outs, places=()):
        return pl.pallas_call(
            kernel,
            out_shape=outs,
            in_specs=[scalar] * len(places) + in_vmem(len(operands)),
            out_specs=in_vmem(len(outs)),
            compiler_params=params,
        )(*places, *operands)

    g, row, keep, send = pl.pallas_call(
        functools.partial(backward_kernel, 2, 1, scale, blocks),
        out_shape=[shape(8, BLK)] * 2 + [shape(half, b_rows + 8, width)] * 2,
        in_specs=[scalar] + head + in_vmem(5),
        out_specs=in_vmem(4),
        scratch_shapes=[
            pltpu.VMEM((blocks, 8, BLK), jnp.float32),
            pltpu.VMEM((blocks * BLK, width), jnp.float32),
        ]
        + sums_scratch(blocks),
        compiler_params=params,
    )(s_at % 2, pair_list, kept, x, y, f, g, *rows, *cols)
    came = swap(send, "src", n_src, 1)
    block = shape(f_rows + 8, width)
    two = shape(2, f_rows + 8, width)
    forward = pl.pallas_call(
        functools.partial(forward_kernel, scale, blocks),
        out_shape=[two, two, two, block, block],
        in_specs=[scalar] + head + in_vmem(2),
        out_specs=in_vmem(5),
        scratch_shapes=[
            pltpu.VMEM((blocks, 8, BLK), jnp.float32),
            pltpu.VMEM((blocks, BLK, 128), jnp.float32),
            pltpu.VMEM((blocks * BLK, width), jnp.float32),
            pltpu.VMEM((n_tgt, 1, BLK), jnp.float32),
        ],
        compiler_params=params,
        cost_estimate=pl.CostEstimate(flops=6 * 10**9, bytes_accessed=4 * 10**6, transcendentals=0),
    )(t_at % RING, pair_list, kept, x, y, g, row)
    came, forward = lax.optimization_barrier((came, forward))

    (backward,) = call(
        functools.partial(pair_kernel, b_rows), [keep, came], [shape(half, b_rows + 8, width)]
    )
    backward = lax.all_to_all(
        backward.reshape(n_z, 2, b_rows + 8, width),
        "src",
        0,
        0,
        axis_index_groups=along_z,
        tiled=True,
    )
    small = shape(b_rows + 8, width)
    keep, send = call(
        functools.partial(z_kernel, b_rows), [backward], [small, small], [s_at // 2 % 2]
    )
    came = swap(send, "src", n_src, 2)
    (backward,) = call(functools.partial(last_kernel, b_rows), [keep, came], [shape(b_rows, width)])

    ups = [(k, k // RING * RING + (k + 1) % RING) for k in range(n_tgt)]
    downs = [(b, a) for a, b in ups]
    own, up, down, up_next, down_next = forward
    up_came = lax.ppermute(up, "tgt", ups)
    down_came = lax.ppermute(down, "tgt", downs)
    up, down = call(
        functools.partial(relay_kernel, f_rows),
        [up_next, up_came, down_next, down_came],
        [block, block],
    )
    up_second = lax.ppermute(up, "tgt", ups)
    down_second = lax.ppermute(down, "tgt", downs)
    keep, send = call(
        functools.partial(x_kernel, f_rows),
        [own, up_came, down_came, up_second, down_second],
        [block, block],
        [t_at // RING],
    )
    came = swap(send, "tgt", n_tgt, RING)
    (forward,) = call(functools.partial(last_kernel, f_rows), [keep, came], [shape(f_rows, width)])
    return (forward, backward)


def solution(mesh):
    return jax.shard_map(
        functools.partial(per_device, mesh.shape["src"], mesh.shape["tgt"]),
        mesh=mesh,
        in_specs=(P("src", None), P("tgt", None), P("src", "tgt", None, None), P("src", "tgt")),
        out_specs=(P(("src", "tgt"), None), P(("tgt", "src"), None)),
        check_vma=False,
    )
```

```python
import functools
import math

import jax
import jax.numpy as jnp
from jax import lax
from jax.experimental import pallas as pl
from jax.experimental.pallas import tpu as pltpu
from jax.sharding import PartitionSpec as P

BLK = 256
ITERS = 2
NEG = -1e30
RING = 4


def log_sum(parts):
    high = functools.reduce(jnp.maximum, parts)
    total = functools.reduce(jnp.add, [jnp.exp2(part - high) for part in parts])
    return high + jnp.log2(total)


def down_rows(lanes, blocks, wide_ref):
    upright = jnp.transpose(lanes)
    for b in range(blocks):
        wide_ref[b] = jnp.broadcast_to(upright[:, b : b + 1], (BLK, 128))


def norm(z, scale):
    z = z.astype(jnp.float32)
    return jnp.sum(z * z, axis=1, keepdims=True) * (-0.5 * scale)


def across(columns):
    lane = lax.broadcasted_iota(jnp.int32, (BLK, 128), 1)
    gathered = jnp.zeros((BLK, 128), jnp.float32)
    for b, column in enumerate(columns):
        gathered = jnp.where(lane == b, jnp.broadcast_to(column, (BLK, 128)), gathered)
    return jnp.transpose(gathered)[:8]


def over_pairs(pairs_ref, kept, visit):
    def two(step, carry):
        p = 2 * step
        visit(pairs_ref[0, p], pairs_ref[1, p])
        visit(pairs_ref[0, p + 1], pairs_ref[1, p + 1])
        return carry

    lax.fori_loop(0, kept // 2, two, 0)

    @pl.when(kept % 2 == 1)
    def _():
        p = kept - 1
        visit(pairs_ref[0, p], pairs_ref[1, p])


def cross(a, b):
    return lax.dot_general(a, b, (((1,), (1,)), ((), ())), preferred_element_type=jnp.float32)


def fold(scores, wide, scale, high_ref, sum_ref, b):
    for h in range(2):
        at = slice(128 * h, 128 * h + 128)
        t = (scores[:, at] * scale + wide).reshape(BLK // 8, 8, 128)
        old = high_ref[b, :, at]
        high = jnp.maximum(old, jnp.max(t, axis=0))
        total = jnp.sum(jnp.exp2(t - high[None]), axis=0)
        sum_ref[b, :, at] = sum_ref[b, :, at] * jnp.exp2(old - high) + total
        high_ref[b, :, at] = high


def settle(high_ref, sum_ref, blocks):
    rows = []
    for b in range(blocks):
        high = high_ref[b]
        top = jnp.max(high, axis=0, keepdims=True)
        total = jnp.sum(sum_ref[b] * jnp.exp2(high - top), axis=0, keepdims=True)
        rows.append(top + jnp.log2(total))
    rows += [jnp.zeros((1, BLK), jnp.float32)] * (8 - blocks)
    return jnp.concatenate(rows, axis=0)


def new_potential(old_ref, refs):
    parts = [part for r in refs for part in ([r[...]] if len(r.shape) == 2 else [r[k] for k in range(r.shape[0])])]
    return 0.5 * (old_ref[...] - log_sum(parts))


def exponentials(scores, scale, wide, lanes):
    halves = []
    for h in range(2):
        at = slice(128 * h, 128 * h + 128)
        t = (scores[:, at] * scale + wide).reshape(BLK // 8, 8, 128) + lanes[:, at][None]
        halves.append(jnp.exp2(t))
    return halves


def add_sums(halves, row_acc, col_acc, s, t):
    for h, e in enumerate(halves):
        col_acc[t, :, 128 * h : 128 * h + 128] += jnp.sum(e, axis=0)
    row_acc[s] += (halves[0] + halves[1]).reshape(BLK, 128)


def totals(row_acc, col_acc, blocks):
    columns = [jnp.sum(row_acc[b], axis=1, keepdims=True) for b in range(blocks)]
    below = lax.broadcasted_iota(jnp.int32, (8, BLK), 0) >= blocks
    row = jnp.where(below, 1.0, across(columns))
    col = [jnp.sum(col_acc[b], axis=0, keepdims=True) for b in range(blocks)]
    col = jnp.concatenate(col + [jnp.ones((8 - blocks, BLK), jnp.float32)], axis=0)
    low = jnp.minimum(jnp.min(row), jnp.min(col))
    high = jnp.maximum(jnp.max(row), jnp.max(col))
    return columns, row, col, (low >= 2.0**-60) & (high <= 2.0**100)


def clear(*refs):
    for ref in refs:
        ref[...] = jnp.zeros(ref.shape, jnp.float32)


def pass_sums(pairs_ref, kept, x_ref, y_ref, scale, f_wide, g_wide, row_high, row_sum, col_high, col_sum):
    for ref in (row_high, col_high):
        ref[...] = jnp.full(ref.shape, NEG, jnp.float32)
    clear(row_sum, col_sum)

    def visit(s, t):
        xs, yt = x_ref[s], y_ref[t]
        fold(cross(yt, xs), g_wide[t], scale, row_high, row_sum, s)
        fold(cross(xs, yt), f_wide[s], scale, col_high, col_sum, t)

    over_pairs(pairs_ref, kept, visit)


def sweep(pairs_ref, kept, x_ref, y_ref, f, g, shift, scale, blocks, outs, scratch):
    row_out, col_out = outs
    f_wide, g_wide, row_high, row_sum, col_high, col_sum, lanes, row_acc, col_acc = scratch
    spread_lanes(g + shift, blocks, lanes)
    clear(row_acc, col_acc)

    def visit(s, t):
        halves = exponentials(cross(x_ref[s], y_ref[t]), scale, f_wide[s], lanes[t])
        add_sums(halves, row_acc, col_acc, s, t)

    over_pairs(pairs_ref, kept, visit)
    _, row, col, good = totals(row_acc, col_acc, blocks)
    row_out[...] = jnp.log2(row) - (f + shift)
    col_out[...] = jnp.log2(col) - (g + shift)

    @pl.when(jnp.logical_not(good))
    def _():
        down_rows(g, blocks, g_wide)
        pass_sums(pairs_ref, kept, x_ref, y_ref, scale, *scratch[:6])
        row_out[...] = settle(row_high, row_sum, blocks)
        col_out[...] = settle(col_high, col_sum, blocks)


def first_kernel(scale, blocks, pairs_ref, count_ref, x_hbm, y_hbm, *rest):
    f_out, g_out, row_out, col_out = rest[:4]
    scratch, (x_ref, y_ref, arrived) = rest[4:-3], rest[-3:]
    f_wide, g_wide = scratch[:2]
    copies = [
        pltpu.make_async_copy(far.at[b], near.at[b], arrived.at[k, b])
        for b in range(blocks)
        for k, (far, near) in enumerate(((x_hbm, x_ref), (y_hbm, y_ref)))
    ]
    for copy in copies:
        copy.start()
    f_columns, g_columns = [], []
    for b in range(blocks):
        copies[2 * b].wait()
        f_columns.append(norm(x_ref[b], scale))
        f_wide[b] = jnp.broadcast_to(f_columns[b], (BLK, 128))
        copies[2 * b + 1].wait()
        g_columns.append(norm(y_ref[b], scale))
    f, g = across(f_columns), across(g_columns)
    f_out[...] = f
    g_out[...] = g
    shift = -(jnp.sum(f) + jnp.sum(g)) / (blocks * BLK)
    sweep(pairs_ref, count_ref[0], x_ref, y_ref, f, g, shift, scale, blocks, (row_out, col_out), scratch)


def second_kernel(n_row, scale, blocks, pairs_ref, count_ref, x_ref, y_ref, f_old, g_old, *rest):
    parts, rest = rest[: n_row + 1], rest[n_row + 1 :]
    f_out, g_out, row_out, col_out = rest[:4]
    scratch = rest[4:]
    f = new_potential(f_old, parts[:n_row])
    g = new_potential(g_old, parts[n_row:])
    f_out[...] = f
    g_out[...] = g
    down_rows(f, blocks, scratch[0])
    sweep(pairs_ref, count_ref[0], x_ref, y_ref, f, g, 0.0, scale, blocks, (row_out, col_out), scratch)


def split_two(w):
    high = w.astype(jnp.bfloat16)
    return high, (w - high.astype(jnp.float32)).astype(jnp.bfloat16)


def weigh(scores, scale, lanes, wide):
    halves = []
    for h in range(2):
        at = slice(128 * h, 128 * h + 128)
        t = (scores[:, at] * scale - wide).reshape(BLK // 8, 8, 128) + lanes[:, at][None]
        halves.append(jnp.exp2(t).reshape(BLK, 128))
    return jnp.concatenate(halves, axis=1)


def receivers_lines(log_sums, n, blocks):
    rows = blocks * BLK // n
    lane = lax.broadcasted_iota(jnp.int32, (1, BLK), 1)
    shifted, lines = {}, []
    for b in range(n):
        k, off = b * rows // BLK, b * rows % BLK
        if off not in shifted:
            shifted[off] = pltpu.roll(log_sums, BLK - off, 1) if off else log_sums
        line = shifted[off][k : k + 1]
        if off and k + 1 < blocks:
            line = jnp.where(lane < BLK - off, line, shifted[off][k + 1 : k + 2])
        lines.append(line)
    return lines


def images(pairs_ref, kept, a_ref, b_ref, scale, lanes, wide, image_ref, turned):
    image_ref[...] = jnp.zeros(image_ref.shape, jnp.float32)

    def visit(s, t):
        a, b = (t, s) if turned else (s, t)
        at, bt = a_ref[a], b_ref[b]
        high, low = split_two(weigh(cross(at, bt), scale, lanes[b], wide[a]))
        rows = pl.ds(pl.multiple_of(a * BLK, BLK), BLK)
        image_ref[rows, :] += jnp.dot(high, bt, preferred_element_type=jnp.float32) + jnp.dot(
            low, bt, preferred_element_type=jnp.float32
        )

    over_pairs(pairs_ref, kept, visit)


def spread_lanes(values, blocks, lanes_ref):
    for b in range(blocks):
        lanes_ref[b] = jnp.broadcast_to(values[b : b + 1], (8, BLK))


def maps_kernel(n_row, scale, blocks, place_ref, pairs_ref, count_ref, x_ref, y_ref, f_old, g_old, *rest):
    parts, rest = rest[: n_row + 1], rest[n_row + 1 :]
    keep_out, send_out, own, up, down, up_next, down_next = rest[:7]
    scratch = rest[7:16]
    f_wide, g_wide, row_high, row_sum, col_high, col_sum, lanes, row_acc, col_acc = scratch
    x_turned, forward, backward, turned, logs, lines_ref = rest[16:]
    kept = count_ref[0]
    f = new_potential(f_old, parts[:n_row])
    g = new_potential(g_old, parts[n_row:])
    down_rows(f, blocks, f_wide)
    spread_lanes(g, blocks, lanes)
    clear(row_acc, col_acc, forward, turned)
    diagonal = lax.broadcasted_iota(jnp.int32, (BLK, BLK), 0) == lax.broadcasted_iota(jnp.int32, (BLK, BLK), 1)
    unit = jnp.where(diagonal, 1.0, 0.0).astype(jnp.bfloat16)
    for b in range(blocks):
        x_turned[b] = cross(unit, x_ref[b]).astype(jnp.bfloat16)

    def visit(s, t):
        xs, yt, xt = x_ref[s], y_ref[t], x_turned[s]
        halves = exponentials(cross(xs, yt), scale, f_wide[s], lanes[t])
        add_sums(halves, row_acc, col_acc, s, t)
        e = jnp.concatenate([half.reshape(BLK, 128) for half in halves], axis=1)
        high, low = split_two(e)
        rows = pl.ds(pl.multiple_of(s * BLK, BLK), BLK)
        forward[rows, :] += jnp.dot(
            jnp.concatenate([high, low], axis=1),
            jnp.concatenate([yt, yt], axis=0),
            preferred_element_type=jnp.float32,
        )
        turned[t] += jnp.dot(
            jnp.concatenate([xt, xt], axis=1),
            jnp.concatenate([high, low], axis=0),
            preferred_element_type=jnp.float32,
        )

    over_pairs(pairs_ref, kept, visit)
    columns, row, col, good = totals(row_acc, col_acc, blocks)

    @pl.when(good)
    def _():
        logs[0] = jnp.log2(row) - f
        logs[1] = jnp.log2(col) - g
        inverse = 1.0 / col
        for b in range(blocks):
            rows = slice(b * BLK, b * BLK + BLK)
            forward[rows, :] = forward[rows, :] * (1.0 / columns[b])
            backward[rows, :] = jnp.transpose(turned[b] * inverse[b : b + 1])

    @pl.when(jnp.logical_not(good))
    def _():
        down_rows(g, blocks, g_wide)
        pass_sums(pairs_ref, kept, x_ref, y_ref, scale, *scratch[:6])
        row_log = settle(row_high, row_sum, blocks)
        col_log = settle(col_high, col_sum, blocks)
        logs[0] = row_log
        logs[1] = col_log
        down_rows(row_log, blocks, f_wide)
        images(pairs_ref, kept, x_ref, y_ref, scale, lanes, f_wide, forward, False)
        spread_lanes(f, blocks, lanes)
        down_rows(col_log, blocks, g_wide)
        images(pairs_ref, kept, y_ref, x_ref, scale, lanes, g_wide, backward, True)

    n = lines_ref.shape[0]
    rows = blocks * BLK // n
    for b, line in enumerate(receivers_lines(logs[0], n, blocks)):
        lines_ref[b] = line
    me = place_ref[1]

    def put(out, r, high):
        to = ((me + r) % RING) + RING * high
        out[:rows, :] = forward[pl.ds(pl.multiple_of(to * rows, 16), rows), :]
        out[rows : rows + 1, :] = lines_ref[to]

    put(up.at[0], 2, 0)
    put(up.at[1], 1, 1)
    put(down.at[0], 2, 1)
    put(down.at[1], 3, 0)
    put(own.at[0], 0, 0)
    put(own.at[1], 0, 1)
    put(up_next, 1, 0)
    put(down_next, 3, 1)

    half = keep_out.shape[0]
    small = blocks * BLK // (2 * half)
    lines = receivers_lines(logs[1], 2 * half, blocks)
    core = place_ref[0]
    for q in range(half):
        for ref, side in ((keep_out, core), (send_out, 1 - core)):
            first = pl.multiple_of((2 * q + side) * small, 16)
            ref[q, :small, :] = backward[pl.ds(first, small), :]
            ref[q, small : small + 1, :] = jnp.where(side == 0, lines[2 * q], lines[2 * q + 1])


def pair_kernel(rows, a_ref, b_ref, out_ref):
    n = a_ref.shape[0]
    a = jnp.concatenate([a_ref[q, rows : rows + 1, :] for q in range(n)], axis=0)
    b = jnp.concatenate([b_ref[q, rows : rows + 1, :] for q in range(n)], axis=0)
    high = jnp.maximum(a, b)
    both = jnp.exp2(a - high) + jnp.exp2(b - high)
    merged = high + jnp.log2(both)
    a_part = jnp.transpose(jnp.exp2(a - high) / both)
    b_part = jnp.transpose(jnp.exp2(b - high) / both)
    for q in range(n):
        out_ref[q, :rows, :] = (
            a_part[:rows, q : q + 1] * a_ref[q, :rows, :]
            + b_part[:rows, q : q + 1] * b_ref[q, :rows, :]
        )
        out_ref[q, rows : rows + 1, :] = merged[q : q + 1]


def blend(parts, rows):
    logs = jnp.concatenate([part[rows : rows + 1, :] for part in parts], axis=0)
    high = jnp.max(logs, axis=0, keepdims=True)
    lifted = jnp.exp2(logs - high)
    whole = jnp.sum(lifted, axis=0, keepdims=True)
    upright = jnp.transpose(lifted / whole)
    total = jnp.zeros((rows, BLK), jnp.float32)
    for d, part in enumerate(parts):
        total += upright[:rows, d : d + 1] * part[:rows, :]
    return total, high + jnp.log2(whole)


def put_blend(out, blended, rows):
    out[:rows, :] = blended[0]
    if out.shape[0] > rows:
        out[rows : rows + 1, :] = blended[1]


def z_kernel(rows, place_ref, parts_ref, keep_ref, send_ref):
    for out, low in ((keep_ref, place_ref[0]), (send_ref, 1 - place_ref[0])):
        parts = [parts_ref.at[d, low] for d in range(parts_ref.shape[0])]
        put_blend(out, blend(parts, rows), rows)


def relay_kernel(rows, up_next, up_came, down_next, down_came, up_out, down_out):
    put_blend(up_out, blend([up_next, up_came.at[0]], rows), rows)
    put_blend(down_out, blend([down_next, down_came.at[0]], rows), rows)


def x_kernel(rows, place_ref, own, up_came, down_came, up_second, down_second, keep_ref, send_ref):
    low = blend([own.at[0], up_second, down_came.at[1]], rows)
    high = blend([own.at[1], down_second, up_came.at[1]], rows)

    @pl.when(place_ref[0] == 0)
    def _():
        put_blend(keep_ref, low, rows)
        put_blend(send_ref, high, rows)

    @pl.when(place_ref[0] == 1)
    def _():
        put_blend(keep_ref, high, rows)
        put_blend(send_ref, low, rows)


def last_kernel(rows, a_ref, b_ref, out_ref):
    put_blend(out_ref, blend([a_ref, b_ref], rows), rows)


def in_vmem(n):
    return [pl.BlockSpec(memory_space=pltpu.VMEM)] * n


def shape(*dims):
    return jax.ShapeDtypeStruct(dims, jnp.float32)


def sums_scratch(blocks):
    wide = pltpu.VMEM((blocks, BLK, 128), jnp.float32)
    deep = pltpu.VMEM((blocks, 8, BLK), jnp.float32)
    return [wide] * 2 + [deep] * 5 + [wide, deep]


def per_device(n_src, n_tgt, sources, targets, pairs, counts):
    width = sources.shape[1]
    scale = math.log2(math.e) / (math.sqrt(width) / 4.0)
    blocks = sources.shape[0] // BLK
    x = sources.reshape(blocks, BLK, width)
    y = targets.reshape(blocks, BLK, width)
    pair_list = jnp.transpose(pairs[0, 0])
    kept = counts.reshape(-1)
    smem = pl.BlockSpec(memory_space=pltpu.SMEM)
    hbm = pl.BlockSpec(memory_space=pltpu.HBM)
    large = pltpu.CompilerParams(vmem_limit_bytes=24 * 1024 * 1024)
    little = pltpu.CompilerParams(vmem_limit_bytes=8 * 1024 * 1024)

    def swap(value, axis, size, bit):
        return lax.ppermute(value, axis, [(k, k ^ bit) for k in range(size)])

    n_z = n_src // 4
    along_z = [list(range(k, n_src, 4)) for k in range(4)]

    def exchange(row, col):
        col = log_sum([col, swap(col, "src", n_src, 1)])
        row = log_sum([row, swap(row, "tgt", n_tgt, RING)])
        col = log_sum([col, swap(col, "src", n_src, 2)])
        row = log_sum([row, swap(row, "tgt", n_tgt, 2)])
        copies = jnp.broadcast_to(col[None], (n_z, *col.shape))
        cols = lax.all_to_all(copies, "src", 0, 0, axis_index_groups=along_z, tiled=True)
        return [row, swap(row, "tgt", n_tgt, 1), cols]

    latents = pltpu.VMEM((blocks, BLK, width), jnp.bfloat16)
    f, g, row, col = pl.pallas_call(
        functools.partial(first_kernel, scale, blocks),
        out_shape=[shape(8, BLK)] * 4,
        in_specs=[smem] * 2 + [hbm] * 2,
        out_specs=in_vmem(4),
        scratch_shapes=sums_scratch(blocks)
        + [latents] * 2
        + [pltpu.SemaphoreType.DMA((2, blocks))],
        compiler_params=pltpu.CompilerParams(vmem_limit_bytes=60 * 1024 * 1024),
    )(pair_list, kept, x, y)
    parts = exchange(row, col)
    f, g, row, col = pl.pallas_call(
        functools.partial(second_kernel, 2, scale, blocks),
        out_shape=[shape(8, BLK)] * 4,
        in_specs=[smem] * 2 + in_vmem(7),
        out_specs=in_vmem(4),
        scratch_shapes=sums_scratch(blocks),
        compiler_params=large,
    )(pair_list, kept, x, y, f, g, *parts)
    parts = exchange(row, col)

    f_rows, b_rows = blocks * BLK // n_tgt, blocks * BLK // n_src
    half = n_src // 2
    s_at = lax.axis_index("src").astype(jnp.int32)
    t_at = lax.axis_index("tgt").astype(jnp.int32)

    def call(kernel, operands, outs, places=()):
        return pl.pallas_call(
            kernel,
            out_shape=outs,
            in_specs=[smem] * len(places) + in_vmem(len(operands)),
            out_specs=in_vmem(len(outs)),
            compiler_params=little,
        )(*places, *operands)

    block = shape(f_rows + 8, width)
    two = shape(2, f_rows + 8, width)
    keep, send, own, up, down, up_next, down_next = pl.pallas_call(
        functools.partial(maps_kernel, 2, scale, blocks),
        out_shape=[shape(half, b_rows + 8, width)] * 2 + [two, two, two, block, block],
        in_specs=[smem] * 3 + in_vmem(7),
        out_specs=in_vmem(7),
        scratch_shapes=sums_scratch(blocks)
        + [
            pltpu.VMEM((blocks, width, BLK), jnp.bfloat16),
            pltpu.VMEM((blocks * BLK, width), jnp.float32),
            pltpu.VMEM((blocks * BLK, width), jnp.float32),
            pltpu.VMEM((blocks, width, BLK), jnp.float32),
            pltpu.VMEM((2, 8, BLK), jnp.float32),
            pltpu.VMEM((n_tgt, 1, BLK), jnp.float32),
        ],
        compiler_params=large,
    )(jnp.stack([s_at % 2, t_at % RING]), pair_list, kept, x, y, f, g, *parts)
    came = swap(send, "src", n_src, 1)

    (paired,) = call(
        functools.partial(pair_kernel, b_rows), [keep, came], [shape(half, b_rows + 8, width)]
    )
    backward = lax.all_to_all(
        paired.reshape(n_z, 2, b_rows + 8, width),
        "src",
        0,
        0,
        axis_index_groups=along_z,
        tiled=True,
    )
    small = shape(b_rows + 8, width)
    keep, send = call(
        functools.partial(z_kernel, b_rows), [backward], [small, small], [(s_at // 2 % 2).reshape(1)]
    )
    came = swap(send, "src", n_src, 2)
    (backward,) = call(functools.partial(last_kernel, b_rows), [keep, came], [shape(b_rows, width)])

    ups = [(k, k // RING * RING + (k + 1) % RING) for k in range(n_tgt)]
    downs = [(b, a) for a, b in ups]
    up_came = lax.ppermute(up, "tgt", ups)
    down_came = lax.ppermute(down, "tgt", downs)
    up_came, down_came, _ = lax.optimization_barrier((up_came, down_came, paired))
    up, down = call(
        functools.partial(relay_kernel, f_rows),
        [up_next, up_came, down_next, down_came],
        [block, block],
    )
    up_second = lax.ppermute(up, "tgt", ups)
    down_second = lax.ppermute(down, "tgt", downs)
    keep, send = call(
        functools.partial(x_kernel, f_rows),
        [own, up_came, down_came, up_second, down_second],
        [block, block],
        [(t_at // RING).reshape(1)],
    )
    came = swap(send, "tgt", n_tgt, RING)
    (forward,) = call(functools.partial(last_kernel, f_rows), [keep, came], [shape(f_rows, width)])
    return (forward, backward)


def solution(mesh):
    return jax.shard_map(
        functools.partial(per_device, mesh.shape["src"], mesh.shape["tgt"]),
        mesh=mesh,
        in_specs=(P("src", None), P("tgt", None), P("src", "tgt", None, None), P("src", "tgt")),
        out_specs=(P(("src", "tgt"), None), P(("tgt", "src"), None)),
        check_vma=False,
    )
```

```python
import functools
import math

import jax
import jax.numpy as jnp
from jax import lax
from jax.experimental import pallas as pl
from jax.experimental.pallas import tpu as pltpu
from jax.sharding import PartitionSpec as P

BLK = 256
ITERS = 2
NEG = -1e30
RING = 4


def log_sum(parts):
    high = functools.reduce(jnp.maximum, parts)
    total = functools.reduce(jnp.add, [jnp.exp2(part - high) for part in parts])
    return high + jnp.log2(total)


def down_rows(lanes, blocks, wide_ref):
    upright = jnp.transpose(lanes)
    for b in range(blocks):
        wide_ref[b] = jnp.broadcast_to(upright[:, b : b + 1], (BLK, 128))


def norm(z, scale):
    z = z.astype(jnp.float32)
    return jnp.sum(z * z, axis=1, keepdims=True) * (-0.5 * scale)


def across(columns):
    lane = lax.broadcasted_iota(jnp.int32, (BLK, 128), 1)
    gathered = jnp.zeros((BLK, 128), jnp.float32)
    for b, column in enumerate(columns):
        gathered = jnp.where(lane == b, jnp.broadcast_to(column, (BLK, 128)), gathered)
    return jnp.transpose(gathered)[:8]


def over_pairs(pairs_ref, kept, visit):
    def two(step, carry):
        p = 2 * step
        visit(pairs_ref[0, p], pairs_ref[1, p])
        visit(pairs_ref[0, p + 1], pairs_ref[1, p + 1])
        return carry

    lax.fori_loop(0, kept // 2, two, 0)

    @pl.when(kept % 2 == 1)
    def _():
        p = kept - 1
        visit(pairs_ref[0, p], pairs_ref[1, p])


def cross(a, b):
    return lax.dot_general(a, b, (((1,), (1,)), ((), ())), preferred_element_type=jnp.float32)


def fold(scores, wide, scale, high_ref, sum_ref, b):
    for h in range(2):
        at = slice(128 * h, 128 * h + 128)
        t = (scores[:, at] * scale + wide).reshape(BLK // 8, 8, 128)
        old = high_ref[b, :, at]
        high = jnp.maximum(old, jnp.max(t, axis=0))
        total = jnp.sum(jnp.exp2(t - high[None]), axis=0)
        sum_ref[b, :, at] = sum_ref[b, :, at] * jnp.exp2(old - high) + total
        high_ref[b, :, at] = high


def settle(high_ref, sum_ref, blocks):
    rows = []
    for b in range(blocks):
        high = high_ref[b]
        top = jnp.max(high, axis=0, keepdims=True)
        total = jnp.sum(sum_ref[b] * jnp.exp2(high - top), axis=0, keepdims=True)
        rows.append(top + jnp.log2(total))
    rows += [jnp.zeros((1, BLK), jnp.float32)] * (8 - blocks)
    return jnp.concatenate(rows, axis=0)


def new_potential(old_ref, refs):
    parts = [part for r in refs for part in ([r[...]] if len(r.shape) == 2 else [r[k] for k in range(r.shape[0])])]
    return 0.5 * (old_ref[...] - log_sum(parts))


def exponentials(scores_ref, wide, lanes):
    halves = []
    for h in range(2):
        at = slice(128 * h, 128 * h + 128)
        t = (scores_ref[:, at] + wide).reshape(BLK // 8, 8, 128) + lanes[:, at][None]
        halves.append(jnp.exp2(t))
    return halves


def add_sums(halves, row_acc, col_acc, s, t):
    for h, e in enumerate(halves):
        col_acc[t, :, 128 * h : 128 * h + 128] += jnp.sum(e, axis=0)
    row_acc[s] += (halves[0] + halves[1]).reshape(BLK, 128)


def totals(row_acc, col_acc, blocks):
    columns = [jnp.sum(row_acc[b], axis=1, keepdims=True) for b in range(blocks)]
    below = lax.broadcasted_iota(jnp.int32, (8, BLK), 0) >= blocks
    row = jnp.where(below, 1.0, across(columns))
    col = [jnp.sum(col_acc[b], axis=0, keepdims=True) for b in range(blocks)]
    col = jnp.concatenate(col + [jnp.ones((8 - blocks, BLK), jnp.float32)], axis=0)
    low = jnp.minimum(jnp.min(row), jnp.min(col))
    high = jnp.maximum(jnp.max(row), jnp.max(col))
    return columns, row, col, (low >= 2.0**-60) & (high <= 2.0**100)


def clear(*refs):
    for ref in refs:
        ref[...] = jnp.zeros(ref.shape, jnp.float32)


def pass_sums(pairs_ref, kept, x_ref, y_ref, scale, f_wide, g_wide, row_high, row_sum, col_high, col_sum):
    for ref in (row_high, col_high):
        ref[...] = jnp.full(ref.shape, NEG, jnp.float32)
    clear(row_sum, col_sum)

    def visit(s, t):
        xs, yt = x_ref[s], y_ref[t]
        fold(cross(yt, xs), g_wide[t], scale, row_high, row_sum, s)
        fold(cross(xs, yt), f_wide[s], scale, col_high, col_sum, t)

    over_pairs(pairs_ref, kept, visit)


def sweep(pairs_ref, kept, x_ref, y_ref, scores_ref, f, g, shift, scale, blocks, outs, scratch):
    row_out, col_out = outs
    f_wide, g_wide, row_high, row_sum, col_high, col_sum, lanes, row_acc, col_acc = scratch
    spread_lanes(g + shift, blocks, lanes)
    clear(row_acc, col_acc)

    def visit(s, t):
        halves = exponentials(scores_ref.at[t, s], f_wide[s], lanes[t])
        add_sums(halves, row_acc, col_acc, s, t)

    over_pairs(pairs_ref, kept, visit)
    _, row, col, good = totals(row_acc, col_acc, blocks)
    row_out[...] = jnp.log2(row) - (f + shift)
    col_out[...] = jnp.log2(col) - (g + shift)

    @pl.when(jnp.logical_not(good))
    def _():
        down_rows(g, blocks, g_wide)
        pass_sums(pairs_ref, kept, x_ref, y_ref, scale, *scratch[:6])
        row_out[...] = settle(row_high, row_sum, blocks)
        col_out[...] = settle(col_high, col_sum, blocks)


def first_kernel(scale, blocks, pairs_ref, count_ref, x_ref, y_ref, *rest):
    scores_ref, f_out, g_out, row_out, col_out = rest[:5]
    scratch = rest[5:]
    f_wide, g_wide = scratch[:2]
    f_columns, g_columns = [], []
    for b in range(blocks):
        f_columns.append(norm(x_ref[b], scale))
        f_wide[b] = jnp.broadcast_to(f_columns[b], (BLK, 128))
    everything = x_ref[...].reshape(blocks * BLK, BLK)
    for b in range(blocks):
        scores = cross(everything, y_ref[b]) * scale
        scores_ref[b] = scores.reshape(blocks, BLK, BLK)
        g_columns.append(norm(y_ref[b], scale))
    f, g = across(f_columns), across(g_columns)
    f_out[...] = f
    g_out[...] = g
    shift = -(jnp.sum(f) + jnp.sum(g)) / (blocks * BLK)
    outs = (row_out, col_out)
    sweep(pairs_ref, count_ref[0], x_ref, y_ref, scores_ref, f, g, shift, scale, blocks, outs, scratch)


def second_kernel(n_row, scale, blocks, pairs_ref, count_ref, x_ref, y_ref, scores_ref, f_old, g_old, *rest):
    parts, rest = rest[: n_row + 1], rest[n_row + 1 :]
    f_out, g_out, row_out, col_out = rest[:4]
    scratch = rest[4:]
    f = new_potential(f_old, parts[:n_row])
    g = new_potential(g_old, parts[n_row:])
    f_out[...] = f
    g_out[...] = g
    down_rows(f, blocks, scratch[0])
    outs = (row_out, col_out)
    sweep(pairs_ref, count_ref[0], x_ref, y_ref, scores_ref, f, g, 0.0, scale, blocks, outs, scratch)


def split_two(w):
    high = w.astype(jnp.bfloat16)
    return high, (w - high.astype(jnp.float32)).astype(jnp.bfloat16)


def weigh(scores, scale, lanes, wide):
    halves = []
    for h in range(2):
        at = slice(128 * h, 128 * h + 128)
        t = (scores[:, at] * scale - wide).reshape(BLK // 8, 8, 128) + lanes[:, at][None]
        halves.append(jnp.exp2(t).reshape(BLK, 128))
    return jnp.concatenate(halves, axis=1)


def receivers_lines(log_sums, n, blocks):
    rows = blocks * BLK // n
    lane = lax.broadcasted_iota(jnp.int32, (1, BLK), 1)
    shifted, lines = {}, []
    for b in range(n):
        k, off = b * rows // BLK, b * rows % BLK
        if off not in shifted:
            shifted[off] = pltpu.roll(log_sums, BLK - off, 1) if off else log_sums
        line = shifted[off][k : k + 1]
        if off and k + 1 < blocks:
            line = jnp.where(lane < BLK - off, line, shifted[off][k + 1 : k + 2])
        lines.append(line)
    return lines


def images(pairs_ref, kept, a_ref, b_ref, scale, lanes, wide, image_ref, turned):
    image_ref[...] = jnp.zeros(image_ref.shape, jnp.float32)

    def visit(s, t):
        a, b = (t, s) if turned else (s, t)
        at, bt = a_ref[a], b_ref[b]
        high, low = split_two(weigh(cross(at, bt), scale, lanes[b], wide[a]))
        rows = pl.ds(pl.multiple_of(a * BLK, BLK), BLK)
        image_ref[rows, :] += jnp.dot(high, bt, preferred_element_type=jnp.float32) + jnp.dot(
            low, bt, preferred_element_type=jnp.float32
        )

    over_pairs(pairs_ref, kept, visit)


def spread_lanes(values, blocks, lanes_ref):
    for b in range(blocks):
        lanes_ref[b] = jnp.broadcast_to(values[b : b + 1], (8, BLK))


def maps_kernel(n_row, scale, blocks, place_ref, pairs_ref, count_ref, x_ref, y_ref, scores_ref, f_old, g_old, *rest):
    parts, rest = rest[: n_row + 1], rest[n_row + 1 :]
    keep_out, send_out, own, up, down, up_next, down_next = rest[:7]
    scratch = rest[7:16]
    f_wide, g_wide, row_high, row_sum, col_high, col_sum, lanes, row_acc, col_acc = scratch
    x_turned, forward, backward, turned, logs, lines_ref, *weights = rest[16:]
    kept = count_ref[0]
    f = new_potential(f_old, parts[:n_row])
    g = new_potential(g_old, parts[n_row:])
    down_rows(f, blocks, f_wide)
    spread_lanes(g, blocks, lanes)
    clear(row_acc, col_acc, forward, turned)
    diagonal = lax.broadcasted_iota(jnp.int32, (BLK, BLK), 0) == lax.broadcasted_iota(jnp.int32, (BLK, BLK), 1)
    unit = jnp.where(diagonal, 1.0, 0.0).astype(jnp.bfloat16)
    for b in range(blocks):
        x_turned[b] = cross(unit, x_ref[b]).astype(jnp.bfloat16)

    def weigh_pair(p, buffer):
        at = jnp.minimum(p, kept - 1)
        s, t = pairs_ref[0, at], pairs_ref[1, at]
        halves = exponentials(scores_ref.at[t, s], f_wide[s], lanes[t])
        counted = jnp.where(p < kept, 1.0, 0.0)
        for h, e in enumerate(halves):
            cols = slice(128 * h, 128 * h + 128)
            col_acc[t, :, cols] += jnp.sum(e, axis=0) * counted
            high, low = split_two(e.reshape(BLK, 128))
            buffer[0, :, cols] = high
            buffer[1, :, cols] = low
        row_acc[s] += (halves[0] + halves[1]).reshape(BLK, 128) * counted

    def add_pair(p, buffer):
        s, t = pairs_ref[0, p], pairs_ref[1, p]
        yt, xt = y_ref[t], x_turned[s]
        high, low = buffer[0], buffer[1]
        rows = pl.ds(pl.multiple_of(s * BLK, BLK), BLK)
        forward[rows, :] += jnp.dot(
            jnp.concatenate([high, low], axis=1),
            jnp.concatenate([yt, yt], axis=0),
            preferred_element_type=jnp.float32,
        )
        turned[t] += jnp.dot(
            jnp.concatenate([xt, xt], axis=1),
            jnp.concatenate([high, low], axis=0),
            preferred_element_type=jnp.float32,
        )

    weigh_pair(0, weights[0])

    def two(step, carry):
        p = 2 * step
        weigh_pair(p + 1, weights[1])
        add_pair(p, weights[0])
        weigh_pair(p + 2, weights[0])
        add_pair(p + 1, weights[1])
        return carry

    lax.fori_loop(0, kept // 2, two, 0)

    @pl.when(kept % 2 == 1)
    def _():
        add_pair(kept - 1, weights[0])

    columns, row, col, good = totals(row_acc, col_acc, blocks)

    @pl.when(good)
    def _():
        logs[0] = jnp.log2(row) - f
        logs[1] = jnp.log2(col) - g
        inverse = 1.0 / col
        for b in range(blocks):
            rows = slice(b * BLK, b * BLK + BLK)
            forward[rows, :] = forward[rows, :] * (1.0 / columns[b])
            backward[rows, :] = jnp.transpose(turned[b] * inverse[b : b + 1])

    @pl.when(jnp.logical_not(good))
    def _():
        down_rows(g, blocks, g_wide)
        pass_sums(pairs_ref, kept, x_ref, y_ref, scale, *scratch[:6])
        row_log = settle(row_high, row_sum, blocks)
        col_log = settle(col_high, col_sum, blocks)
        logs[0] = row_log
        logs[1] = col_log
        down_rows(row_log, blocks, f_wide)
        images(pairs_ref, kept, x_ref, y_ref, scale, lanes, f_wide, forward, False)
        spread_lanes(f, blocks, lanes)
        down_rows(col_log, blocks, g_wide)
        images(pairs_ref, kept, y_ref, x_ref, scale, lanes, g_wide, backward, True)

    n = lines_ref.shape[0]
    rows = blocks * BLK // n
    for b, line in enumerate(receivers_lines(logs[0], n, blocks)):
        lines_ref[b] = line
    me = place_ref[1]

    def put(out, r, high):
        to = ((me + r) % RING) + RING * high
        out[:rows, :] = forward[pl.ds(pl.multiple_of(to * rows, 16), rows), :]
        out[rows : rows + 1, :] = lines_ref[to]

    put(up.at[0], 2, 0)
    put(up.at[1], 1, 1)
    put(down.at[0], 2, 1)
    put(down.at[1], 3, 0)
    put(own.at[0], 0, 0)
    put(own.at[1], 0, 1)
    put(up_next, 1, 0)
    put(down_next, 3, 1)

    half = keep_out.shape[0]
    small = blocks * BLK // (2 * half)
    lines = receivers_lines(logs[1], 2 * half, blocks)
    core = place_ref[0]
    for q in range(half):
        for ref, side in ((keep_out, core), (send_out, 1 - core)):
            first = pl.multiple_of((2 * q + side) * small, 16)
            ref[q, :small, :] = backward[pl.ds(first, small), :]
            ref[q, small : small + 1, :] = jnp.where(side == 0, lines[2 * q], lines[2 * q + 1])


def pair_kernel(rows, a_ref, b_ref, out_ref):
    n = a_ref.shape[0]
    a = jnp.concatenate([a_ref[q, rows : rows + 1, :] for q in range(n)], axis=0)
    b = jnp.concatenate([b_ref[q, rows : rows + 1, :] for q in range(n)], axis=0)
    high = jnp.maximum(a, b)
    both = jnp.exp2(a - high) + jnp.exp2(b - high)
    merged = high + jnp.log2(both)
    a_part = jnp.transpose(jnp.exp2(a - high) / both)
    b_part = jnp.transpose(jnp.exp2(b - high) / both)
    for q in range(n):
        out_ref[q, :rows, :] = (
            a_part[:rows, q : q + 1] * a_ref[q, :rows, :]
            + b_part[:rows, q : q + 1] * b_ref[q, :rows, :]
        )
        out_ref[q, rows : rows + 1, :] = merged[q : q + 1]


def blend(parts, rows):
    logs = jnp.concatenate([part[rows : rows + 1, :] for part in parts], axis=0)
    high = jnp.max(logs, axis=0, keepdims=True)
    lifted = jnp.exp2(logs - high)
    whole = jnp.sum(lifted, axis=0, keepdims=True)
    upright = jnp.transpose(lifted / whole)
    total = jnp.zeros((rows, BLK), jnp.float32)
    for d, part in enumerate(parts):
        total += upright[:rows, d : d + 1] * part[:rows, :]
    return total, high + jnp.log2(whole)


def put_blend(out, blended, rows):
    out[:rows, :] = blended[0]
    if out.shape[0] > rows:
        out[rows : rows + 1, :] = blended[1]


def z_kernel(rows, place_ref, parts_ref, keep_ref, send_ref):
    for out, low in ((keep_ref, place_ref[0]), (send_ref, 1 - place_ref[0])):
        parts = [parts_ref.at[d, low] for d in range(parts_ref.shape[0])]
        put_blend(out, blend(parts, rows), rows)


def relay_kernel(rows, up_next, up_came, down_next, down_came, up_out, down_out):
    put_blend(up_out, blend([up_next, up_came.at[0]], rows), rows)
    put_blend(down_out, blend([down_next, down_came.at[0]], rows), rows)


def x_kernel(rows, place_ref, own, up_came, down_came, up_second, down_second, keep_ref, send_ref):
    low = blend([own.at[0], up_second, down_came.at[1]], rows)
    high = blend([own.at[1], down_second, up_came.at[1]], rows)

    @pl.when(place_ref[0] == 0)
    def _():
        put_blend(keep_ref, low, rows)
        put_blend(send_ref, high, rows)

    @pl.when(place_ref[0] == 1)
    def _():
        put_blend(keep_ref, high, rows)
        put_blend(send_ref, low, rows)


def last_kernel(rows, a_ref, b_ref, out_ref):
    put_blend(out_ref, blend([a_ref, b_ref], rows), rows)


def in_vmem(n):
    return [pl.BlockSpec(memory_space=pltpu.VMEM)] * n


def shape(*dims):
    return jax.ShapeDtypeStruct(dims, jnp.float32)


def sums_scratch(blocks):
    wide = pltpu.VMEM((blocks, BLK, 128), jnp.float32)
    deep = pltpu.VMEM((blocks, 8, BLK), jnp.float32)
    return [wide] * 2 + [deep] * 5 + [wide, deep]


def per_device(n_src, n_tgt, sources, targets, pairs, counts):
    width = sources.shape[1]
    scale = math.log2(math.e) / (math.sqrt(width) / 4.0)
    blocks = sources.shape[0] // BLK
    x = sources.reshape(blocks, BLK, width)
    y = targets.reshape(blocks, BLK, width)
    pair_list = jnp.transpose(pairs[0, 0])
    kept = counts.reshape(-1)
    smem = pl.BlockSpec(memory_space=pltpu.SMEM)
    large = pltpu.CompilerParams(vmem_limit_bytes=24 * 1024 * 1024)
    little = pltpu.CompilerParams(vmem_limit_bytes=8 * 1024 * 1024)

    def swap(value, axis, size, bit):
        return lax.ppermute(value, axis, [(k, k ^ bit) for k in range(size)])

    n_z = n_src // 4
    along_z = [list(range(k, n_src, 4)) for k in range(4)]

    def exchange(row, col):
        col = log_sum([col, swap(col, "src", n_src, 1)])
        row = log_sum([row, swap(row, "tgt", n_tgt, RING)])
        col = log_sum([col, swap(col, "src", n_src, 2)])
        row = log_sum([row, swap(row, "tgt", n_tgt, 2)])
        copies = jnp.broadcast_to(col[None], (n_z, *col.shape))
        cols = lax.all_to_all(copies, "src", 0, 0, axis_index_groups=along_z, tiled=True)
        return [row, swap(row, "tgt", n_tgt, 1), cols]

    scores, f, g, row, col = pl.pallas_call(
        functools.partial(first_kernel, scale, blocks),
        out_shape=[shape(blocks, blocks, BLK, BLK)] + [shape(8, BLK)] * 4,
        in_specs=[smem] * 2 + in_vmem(2),
        out_specs=in_vmem(5),
        scratch_shapes=sums_scratch(blocks),
        compiler_params=large,
    )(pair_list, kept, x, y)
    parts = exchange(row, col)
    f, g, row, col = pl.pallas_call(
        functools.partial(second_kernel, 2, scale, blocks),
        out_shape=[shape(8, BLK)] * 4,
        in_specs=[smem] * 2 + in_vmem(8),
        out_specs=in_vmem(4),
        scratch_shapes=sums_scratch(blocks),
        compiler_params=large,
    )(pair_list, kept, x, y, scores, f, g, *parts)
    parts = exchange(row, col)

    f_rows, b_rows = blocks * BLK // n_tgt, blocks * BLK // n_src
    half = n_src // 2
    s_at = lax.axis_index("src").astype(jnp.int32)
    t_at = lax.axis_index("tgt").astype(jnp.int32)

    def call(kernel, operands, outs, places=(), cost=None):
        return pl.pallas_call(
            kernel,
            out_shape=outs,
            in_specs=[smem] * len(places) + in_vmem(len(operands)),
            out_specs=in_vmem(len(outs)),
            compiler_params=little,
            cost_estimate=cost,
        )(*places, *operands)

    block = shape(f_rows + 8, width)
    two = shape(2, f_rows + 8, width)
    keep, send, own, up, down, up_next, down_next = pl.pallas_call(
        functools.partial(maps_kernel, 2, scale, blocks),
        out_shape=[shape(half, b_rows + 8, width)] * 2 + [two, two, two, block, block],
        in_specs=[smem] * 3 + in_vmem(8),
        out_specs=in_vmem(7),
        scratch_shapes=sums_scratch(blocks)
        + [
            pltpu.VMEM((blocks, width, BLK), jnp.bfloat16),
            pltpu.VMEM((blocks * BLK, width), jnp.float32),
            pltpu.VMEM((blocks * BLK, width), jnp.float32),
            pltpu.VMEM((blocks, width, BLK), jnp.float32),
            pltpu.VMEM((2, 8, BLK), jnp.float32),
            pltpu.VMEM((n_tgt, 1, BLK), jnp.float32),
            pltpu.VMEM((2, BLK, BLK), jnp.bfloat16),
            pltpu.VMEM((2, BLK, BLK), jnp.bfloat16),
        ],
        compiler_params=large,
    )(jnp.stack([s_at % 2, t_at % RING]), pair_list, kept, x, y, scores, f, g, *parts)
    came = swap(send, "src", n_src, 1)

    (paired,) = call(
        functools.partial(pair_kernel, b_rows),
        [keep, came],
        [shape(half, b_rows + 8, width)],
        cost=pl.CostEstimate(flops=10**10, bytes_accessed=3 * 10**7, transcendentals=0),
    )
    backward = lax.all_to_all(
        paired.reshape(n_z, 2, b_rows + 8, width),
        "src",
        0,
        0,
        axis_index_groups=along_z,
        tiled=True,
    )
    small = shape(b_rows + 8, width)
    keep, send = call(
        functools.partial(z_kernel, b_rows), [backward], [small, small], [(s_at // 2 % 2).reshape(1)]
    )
    came = swap(send, "src", n_src, 2)
    (backward,) = call(functools.partial(last_kernel, b_rows), [keep, came], [shape(b_rows, width)])

    ups = [(k, k // RING * RING + (k + 1) % RING) for k in range(n_tgt)]
    downs = [(b, a) for a, b in ups]
    up_came = lax.ppermute(up, "tgt", ups)
    down_came = lax.ppermute(down, "tgt", downs)
    up_came, down_came, _ = lax.optimization_barrier((up_came, down_came, paired))
    up, down = call(
        functools.partial(relay_kernel, f_rows),
        [up_next, up_came, down_next, down_came],
        [block, block],
    )
    up_second = lax.ppermute(up, "tgt", ups)
    down_second = lax.ppermute(down, "tgt", downs)
    keep, send = call(
        functools.partial(x_kernel, f_rows),
        [own, up_came, down_came, up_second, down_second],
        [block, block],
        [(t_at // RING).reshape(1)],
    )
    came = swap(send, "tgt", n_tgt, RING)
    (forward,) = call(functools.partial(last_kernel, f_rows), [keep, came], [shape(f_rows, width)])
    return (forward, backward)


def solution(mesh):
    return jax.shard_map(
        functools.partial(per_device, mesh.shape["src"], mesh.shape["tgt"]),
        mesh=mesh,
        in_specs=(P("src", None), P("tgt", None), P("src", "tgt", None, None), P("src", "tgt")),
        out_specs=(P(("src", "tgt"), None), P(("tgt", "src"), None)),
        check_vma=False,
    )
```

```python
import functools
import math

import jax
import jax.numpy as jnp
from jax import lax
from jax.experimental import pallas as pl
from jax.experimental.pallas import tpu as pltpu
from jax.sharding import PartitionSpec as P

BLK = 256
ITERS = 2
NEG = -1e30
RING = 4


def log_sum(parts):
    high = functools.reduce(jnp.maximum, parts)
    total = functools.reduce(jnp.add, [jnp.exp2(part - high) for part in parts])
    return high + jnp.log2(total)


def down_rows(lanes, blocks, wide_ref):
    upright = jnp.transpose(lanes)
    for b in range(blocks):
        wide_ref[b] = jnp.broadcast_to(upright[:, b : b + 1], (BLK, 128))


def norm(z, scale):
    z = z.astype(jnp.float32)
    return jnp.sum(z * z, axis=1, keepdims=True) * (-0.5 * scale)


def across(columns):
    lane = lax.broadcasted_iota(jnp.int32, (BLK, 128), 1)
    gathered = jnp.zeros((BLK, 128), jnp.float32)
    for b, column in enumerate(columns):
        gathered = jnp.where(lane == b, jnp.broadcast_to(column, (BLK, 128)), gathered)
    return jnp.transpose(gathered)[:8]


def over_pairs(pairs_ref, kept, visit):
    def two(step, carry):
        p = 2 * step
        visit(pairs_ref[0, p], pairs_ref[1, p])
        visit(pairs_ref[0, p + 1], pairs_ref[1, p + 1])
        return carry

    lax.fori_loop(0, kept // 2, two, 0)

    @pl.when(kept % 2 == 1)
    def _():
        p = kept - 1
        visit(pairs_ref[0, p], pairs_ref[1, p])


def cross(a, b):
    return lax.dot_general(a, b, (((1,), (1,)), ((), ())), preferred_element_type=jnp.float32)


def fold(scores, wide, scale, high_ref, sum_ref, b):
    for h in range(2):
        at = slice(128 * h, 128 * h + 128)
        t = (scores[:, at] * scale + wide).reshape(BLK // 8, 8, 128)
        old = high_ref[b, :, at]
        high = jnp.maximum(old, jnp.max(t, axis=0))
        total = jnp.sum(jnp.exp2(t - high[None]), axis=0)
        sum_ref[b, :, at] = sum_ref[b, :, at] * jnp.exp2(old - high) + total
        high_ref[b, :, at] = high


def settle(high_ref, sum_ref, blocks):
    rows = []
    for b in range(blocks):
        high = high_ref[b]
        top = jnp.max(high, axis=0, keepdims=True)
        total = jnp.sum(sum_ref[b] * jnp.exp2(high - top), axis=0, keepdims=True)
        rows.append(top + jnp.log2(total))
    rows += [jnp.zeros((1, BLK), jnp.float32)] * (8 - blocks)
    return jnp.concatenate(rows, axis=0)


def new_potential(old_ref, refs):
    parts = [part for r in refs for part in ([r[...]] if len(r.shape) == 2 else [r[k] for k in range(r.shape[0])])]
    return 0.5 * (old_ref[...] - log_sum(parts))


def exponentials(scores_ref, wide, lanes):
    halves = []
    for h in range(2):
        at = slice(128 * h, 128 * h + 128)
        t = (scores_ref[:, at] + wide).reshape(BLK // 8, 8, 128) + lanes[:, at][None]
        halves.append(jnp.exp2(t))
    return halves


def add_sums(halves, row_acc, col_acc, s, t):
    for h, e in enumerate(halves):
        col_acc[t, :, 128 * h : 128 * h + 128] += jnp.sum(e, axis=0)
    row_acc[s] += (halves[0] + halves[1]).reshape(BLK, 128)


def totals(row_acc, col_acc, blocks):
    columns = [jnp.sum(row_acc[b], axis=1, keepdims=True) for b in range(blocks)]
    below = lax.broadcasted_iota(jnp.int32, (8, BLK), 0) >= blocks
    row = jnp.where(below, 1.0, across(columns))
    col = [jnp.sum(col_acc[b], axis=0, keepdims=True) for b in range(blocks)]
    col = jnp.concatenate(col + [jnp.ones((8 - blocks, BLK), jnp.float32)], axis=0)
    low = jnp.minimum(jnp.min(row), jnp.min(col))
    high = jnp.maximum(jnp.max(row), jnp.max(col))
    return columns, row, col, (low >= 2.0**-60) & (high <= 2.0**100)


def clear(*refs):
    for ref in refs:
        ref[...] = jnp.zeros(ref.shape, jnp.float32)


def pass_sums(pairs_ref, kept, x_ref, y_ref, scale, f_wide, g_wide, row_high, row_sum, col_high, col_sum):
    for ref in (row_high, col_high):
        ref[...] = jnp.full(ref.shape, NEG, jnp.float32)
    clear(row_sum, col_sum)

    def visit(s, t):
        xs, yt = x_ref[s], y_ref[t]
        fold(cross(yt, xs), g_wide[t], scale, row_high, row_sum, s)
        fold(cross(xs, yt), f_wide[s], scale, col_high, col_sum, t)

    over_pairs(pairs_ref, kept, visit)


def sweep(pairs_ref, kept, x_ref, y_ref, scores_ref, f, g, shift, scale, blocks, outs, scratch):
    row_out, col_out = outs
    f_wide, g_wide, row_high, row_sum, col_high, col_sum, lanes, row_acc, col_acc = scratch
    spread_lanes(g + shift, blocks, lanes)
    clear(row_acc, col_acc)

    def visit(s, t):
        halves = exponentials(scores_ref.at[t, s], f_wide[s], lanes[t])
        add_sums(halves, row_acc, col_acc, s, t)

    over_pairs(pairs_ref, kept, visit)
    _, row, col, good = totals(row_acc, col_acc, blocks)
    row_out[...] = jnp.log2(row) - (f + shift)
    col_out[...] = jnp.log2(col) - (g + shift)

    @pl.when(jnp.logical_not(good))
    def _():
        down_rows(g, blocks, g_wide)
        pass_sums(pairs_ref, kept, x_ref, y_ref, scale, *scratch[:6])
        row_out[...] = settle(row_high, row_sum, blocks)
        col_out[...] = settle(col_high, col_sum, blocks)


def all_scores(x_ref, y_ref, scale, blocks, scores_ref):
    everything = x_ref[...].reshape(blocks * BLK, BLK)
    for t in range(blocks):
        scores_ref[t] = (cross(everything, y_ref[t]) * scale).reshape(blocks, BLK, BLK)


def first_kernel(scale, blocks, pairs_ref, count_ref, x_ref, y_ref, *rest):
    f_out, g_out, row_out, col_out = rest[:4]
    scratch, scores_ref = rest[4:-1], rest[-1]
    all_scores(x_ref, y_ref, scale, blocks, scores_ref)
    f_wide, g_wide = scratch[:2]
    f_columns, g_columns = [], []
    for b in range(blocks):
        f_columns.append(norm(x_ref[b], scale))
        f_wide[b] = jnp.broadcast_to(f_columns[b], (BLK, 128))
        g_columns.append(norm(y_ref[b], scale))
    f, g = across(f_columns), across(g_columns)
    f_out[...] = f
    g_out[...] = g
    shift = -(jnp.sum(f) + jnp.sum(g)) / (blocks * BLK)
    outs = (row_out, col_out)
    sweep(pairs_ref, count_ref[0], x_ref, y_ref, scores_ref, f, g, shift, scale, blocks, outs, scratch)


def second_kernel(n_row, scale, blocks, pairs_ref, count_ref, x_ref, y_ref, f_old, g_old, *rest):
    parts, rest = rest[: n_row + 1], rest[n_row + 1 :]
    f_out, g_out, row_out, col_out = rest[:4]
    scratch, scores_ref = rest[4:-1], rest[-1]
    all_scores(x_ref, y_ref, scale, blocks, scores_ref)
    f = new_potential(f_old, parts[:n_row])
    g = new_potential(g_old, parts[n_row:])
    f_out[...] = f
    g_out[...] = g
    down_rows(f, blocks, scratch[0])
    outs = (row_out, col_out)
    sweep(pairs_ref, count_ref[0], x_ref, y_ref, scores_ref, f, g, 0.0, scale, blocks, outs, scratch)


def split_two(w):
    high = w.astype(jnp.bfloat16)
    return high, (w - high.astype(jnp.float32)).astype(jnp.bfloat16)


def weigh(scores, scale, lanes, wide):
    halves = []
    for h in range(2):
        at = slice(128 * h, 128 * h + 128)
        t = (scores[:, at] * scale - wide).reshape(BLK // 8, 8, 128) + lanes[:, at][None]
        halves.append(jnp.exp2(t).reshape(BLK, 128))
    return jnp.concatenate(halves, axis=1)


def receivers_lines(log_sums, n, blocks):
    rows = blocks * BLK // n
    lane = lax.broadcasted_iota(jnp.int32, (1, BLK), 1)
    shifted, lines = {}, []
    for b in range(n):
        k, off = b * rows // BLK, b * rows % BLK
        if off not in shifted:
            shifted[off] = pltpu.roll(log_sums, BLK - off, 1) if off else log_sums
        line = shifted[off][k : k + 1]
        if off and k + 1 < blocks:
            line = jnp.where(lane < BLK - off, line, shifted[off][k + 1 : k + 2])
        lines.append(line)
    return lines


def images(pairs_ref, kept, a_ref, b_ref, scale, lanes, wide, image_ref, turned):
    image_ref[...] = jnp.zeros(image_ref.shape, jnp.float32)

    def visit(s, t):
        a, b = (t, s) if turned else (s, t)
        at, bt = a_ref[a], b_ref[b]
        high, low = split_two(weigh(cross(at, bt), scale, lanes[b], wide[a]))
        rows = pl.ds(pl.multiple_of(a * BLK, BLK), BLK)
        image_ref[rows, :] += jnp.dot(high, bt, preferred_element_type=jnp.float32) + jnp.dot(
            low, bt, preferred_element_type=jnp.float32
        )

    over_pairs(pairs_ref, kept, visit)


def spread_lanes(values, blocks, lanes_ref):
    for b in range(blocks):
        lanes_ref[b] = jnp.broadcast_to(values[b : b + 1], (8, BLK))


def maps_kernel(n_row, scale, blocks, place_ref, pairs_ref, count_ref, x_ref, y_ref, f_old, g_old, *rest):
    parts, rest = rest[: n_row + 1], rest[n_row + 1 :]
    keep_out, send_out, own, up_first, down_first, up_own, down_own = rest[:7]
    scratch = rest[7:16]
    f_wide, g_wide, row_high, row_sum, col_high, col_sum, lanes, row_acc, col_acc = scratch
    scores_ref, x_turned, forward, backward, turned, logs, lines_ref, *weights = rest[16:]
    all_scores(x_ref, y_ref, scale, blocks, scores_ref)
    kept = count_ref[0]
    f = new_potential(f_old, parts[:n_row])
    g = new_potential(g_old, parts[n_row:])
    down_rows(f, blocks, f_wide)
    spread_lanes(g, blocks, lanes)
    clear(row_acc, col_acc, forward, turned)
    diagonal = lax.broadcasted_iota(jnp.int32, (BLK, BLK), 0) == lax.broadcasted_iota(jnp.int32, (BLK, BLK), 1)
    unit = jnp.where(diagonal, 1.0, 0.0).astype(jnp.bfloat16)
    for b in range(blocks):
        x_turned[b] = cross(unit, x_ref[b]).astype(jnp.bfloat16)

    def weigh_pair(p, buffer):
        at = jnp.minimum(p, kept - 1)
        s, t = pairs_ref[0, at], pairs_ref[1, at]
        halves = exponentials(scores_ref.at[t, s], f_wide[s], lanes[t])
        counted = jnp.where(p < kept, 1.0, 0.0)
        for h, e in enumerate(halves):
            cols = slice(128 * h, 128 * h + 128)
            col_acc[t, :, cols] += jnp.sum(e, axis=0) * counted
            high, low = split_two(e.reshape(BLK, 128))
            buffer[0, :, cols] = high
            buffer[1, :, cols] = low
        row_acc[s] += (halves[0] + halves[1]).reshape(BLK, 128) * counted

    def add_pair(p, buffer):
        s, t = pairs_ref[0, p], pairs_ref[1, p]
        yt, xt = y_ref[t], x_turned[s]
        high, low = buffer[0], buffer[1]
        rows = pl.ds(pl.multiple_of(s * BLK, BLK), BLK)
        forward[rows, :] += jnp.dot(
            jnp.concatenate([high, low], axis=1),
            jnp.concatenate([yt, yt], axis=0),
            preferred_element_type=jnp.float32,
        )
        turned[t] += jnp.dot(
            jnp.concatenate([xt, xt], axis=1),
            jnp.concatenate([high, low], axis=0),
            preferred_element_type=jnp.float32,
        )

    weigh_pair(0, weights[0])

    def two(step, carry):
        p = 2 * step
        weigh_pair(p + 1, weights[1])
        add_pair(p, weights[0])
        weigh_pair(p + 2, weights[0])
        add_pair(p + 1, weights[1])
        return carry

    lax.fori_loop(0, kept // 2, two, 0)

    @pl.when(kept % 2 == 1)
    def _():
        add_pair(kept - 1, weights[0])

    columns, row, col, good = totals(row_acc, col_acc, blocks)

    @pl.when(good)
    def _():
        logs[0] = jnp.log2(row) - f
        logs[1] = jnp.log2(col) - g
        inverse = 1.0 / col
        for b in range(blocks):
            rows = slice(b * BLK, b * BLK + BLK)
            forward[rows, :] = forward[rows, :] * (1.0 / columns[b])
            backward[rows, :] = jnp.transpose(turned[b] * inverse[b : b + 1])

    @pl.when(jnp.logical_not(good))
    def _():
        down_rows(g, blocks, g_wide)
        pass_sums(pairs_ref, kept, x_ref, y_ref, scale, *scratch[:6])
        row_log = settle(row_high, row_sum, blocks)
        col_log = settle(col_high, col_sum, blocks)
        logs[0] = row_log
        logs[1] = col_log
        down_rows(row_log, blocks, f_wide)
        images(pairs_ref, kept, x_ref, y_ref, scale, lanes, f_wide, forward, False)
        spread_lanes(f, blocks, lanes)
        down_rows(col_log, blocks, g_wide)
        images(pairs_ref, kept, y_ref, x_ref, scale, lanes, g_wide, backward, True)

    n = lines_ref.shape[0]
    rows = blocks * BLK // n
    for b, line in enumerate(receivers_lines(logs[0], n, blocks)):
        lines_ref[b] = line
    me = place_ref[1]

    def put(out, r, high):
        to = ((me + r) % RING) + RING * high
        out[:rows, :] = forward[pl.ds(pl.multiple_of(to * rows, 16), rows), :]
        out[rows : rows + 1, :] = lines_ref[to]

    put(up_first, 2, 0)
    put(down_first, 2, 1)
    put(own.at[0], 0, 0)
    put(own.at[1], 0, 1)
    put(up_own.at[0], 1, 0)
    put(up_own.at[1], 1, 1)
    put(down_own.at[0], 3, 1)
    put(down_own.at[1], 3, 0)

    half = keep_out.shape[0]
    small = blocks * BLK // (2 * half)
    lines = receivers_lines(logs[1], 2 * half, blocks)
    core = place_ref[0]
    for q in range(half):
        for ref, side in ((keep_out, core), (send_out, 1 - core)):
            first = pl.multiple_of((2 * q + side) * small, 16)
            ref[q, :small, :] = backward[pl.ds(first, small), :]
            ref[q, small : small + 1, :] = jnp.where(side == 0, lines[2 * q], lines[2 * q + 1])


def pair_kernel(rows, a_ref, b_ref, out_ref):
    n = a_ref.shape[0]
    a = jnp.concatenate([a_ref[q, rows : rows + 1, :] for q in range(n)], axis=0)
    b = jnp.concatenate([b_ref[q, rows : rows + 1, :] for q in range(n)], axis=0)
    high = jnp.maximum(a, b)
    both = jnp.exp2(a - high) + jnp.exp2(b - high)
    merged = high + jnp.log2(both)
    a_part = jnp.transpose(jnp.exp2(a - high) / both)
    b_part = jnp.transpose(jnp.exp2(b - high) / both)
    for q in range(n):
        out_ref[q, :rows, :] = (
            a_part[:rows, q : q + 1] * a_ref[q, :rows, :]
            + b_part[:rows, q : q + 1] * b_ref[q, :rows, :]
        )
        out_ref[q, rows : rows + 1, :] = merged[q : q + 1]


def blend(parts, rows):
    logs = jnp.concatenate([part[rows : rows + 1, :] for part in parts], axis=0)
    high = jnp.max(logs, axis=0, keepdims=True)
    lifted = jnp.exp2(logs - high)
    whole = jnp.sum(lifted, axis=0, keepdims=True)
    upright = jnp.transpose(lifted / whole)
    total = jnp.zeros((rows, BLK), jnp.float32)
    for d, part in enumerate(parts):
        total += upright[:rows, d : d + 1] * part[:rows, :]
    return total, high + jnp.log2(whole)


def put_blend(out, blended, rows):
    out[:rows, :] = blended[0]
    if out.shape[0] > rows:
        out[rows : rows + 1, :] = blended[1]


def z_kernel(rows, place_ref, parts_ref, keep_ref, send_ref):
    for out, low in ((keep_ref, place_ref[0]), (send_ref, 1 - place_ref[0])):
        parts = [parts_ref.at[d, low] for d in range(parts_ref.shape[0])]
        put_blend(out, blend(parts, rows), rows)


def relay_kernel(
    f_rows, b_rows, keep, came, up_own, up_came, down_own, down_came, paired, up_out, down_out
):
    pair_kernel(b_rows, keep, came, paired)
    for own, relayed, out in ((up_own, up_came, up_out), (down_own, down_came, down_out)):
        put_blend(out.at[0], blend([own.at[0], relayed], f_rows), f_rows)
        out[1] = own[1]


def x_kernel(rows, place_ref, own, up_came, down_came, keep_ref, send_ref):
    low = blend([own.at[0], up_came.at[0], down_came.at[1]], rows)
    high = blend([own.at[1], down_came.at[0], up_came.at[1]], rows)

    @pl.when(place_ref[0] == 0)
    def _():
        put_blend(keep_ref, low, rows)
        put_blend(send_ref, high, rows)

    @pl.when(place_ref[0] == 1)
    def _():
        put_blend(keep_ref, high, rows)
        put_blend(send_ref, low, rows)


def last_kernel(rows, a_ref, b_ref, out_ref):
    put_blend(out_ref, blend([a_ref, b_ref], rows), rows)


def in_vmem(n):
    return [pl.BlockSpec(memory_space=pltpu.VMEM)] * n


def shape(*dims):
    return jax.ShapeDtypeStruct(dims, jnp.float32)


def sums_scratch(blocks):
    wide = pltpu.VMEM((blocks, BLK, 128), jnp.float32)
    deep = pltpu.VMEM((blocks, 8, BLK), jnp.float32)
    return [wide] * 2 + [deep] * 5 + [wide, deep, pltpu.VMEM((blocks, blocks, BLK, BLK), jnp.float32)]


def per_device(n_src, n_tgt, sources, targets, pairs, counts):
    width = sources.shape[1]
    scale = math.log2(math.e) / (math.sqrt(width) / 4.0)
    blocks = sources.shape[0] // BLK
    x = sources.reshape(blocks, BLK, width)
    y = targets.reshape(blocks, BLK, width)
    pair_list = jnp.transpose(pairs[0, 0])
    kept = counts.reshape(-1)
    smem = pl.BlockSpec(memory_space=pltpu.SMEM)
    large = pltpu.CompilerParams(vmem_limit_bytes=36 * 1024 * 1024)
    little = pltpu.CompilerParams(vmem_limit_bytes=8 * 1024 * 1024)

    def swap(value, axis, size, bit):
        return lax.ppermute(value, axis, [(k, k ^ bit) for k in range(size)])

    n_z = n_src // 4
    along_z = [list(range(k, n_src, 4)) for k in range(4)]

    def exchange(row, col):
        row = log_sum([row, swap(row, "tgt", n_tgt, RING)])
        col = log_sum([col] + [swap(col, "src", n_src, bits) for bits in (1, 2, 3)])
        row = log_sum([row, swap(row, "tgt", n_tgt, 2)])
        copies = jnp.broadcast_to(col[None], (n_z, *col.shape))
        cols = lax.all_to_all(copies, "src", 0, 0, axis_index_groups=along_z, tiled=True)
        return [row, swap(row, "tgt", n_tgt, 1), cols]

    f, g, row, col = pl.pallas_call(
        functools.partial(first_kernel, scale, blocks),
        out_shape=[shape(8, BLK)] * 4,
        in_specs=[smem] * 2 + in_vmem(2),
        out_specs=in_vmem(4),
        scratch_shapes=sums_scratch(blocks),
        compiler_params=large,
    )(pair_list, kept, x, y)
    parts = exchange(row, col)
    f, g, row, col = pl.pallas_call(
        functools.partial(second_kernel, 2, scale, blocks),
        out_shape=[shape(8, BLK)] * 4,
        in_specs=[smem] * 2 + in_vmem(7),
        out_specs=in_vmem(4),
        scratch_shapes=sums_scratch(blocks),
        compiler_params=large,
    )(pair_list, kept, x, y, f, g, *parts)
    parts = exchange(row, col)

    f_rows, b_rows = blocks * BLK // n_tgt, blocks * BLK // n_src
    half = n_src // 2
    s_at = lax.axis_index("src").astype(jnp.int32)
    t_at = lax.axis_index("tgt").astype(jnp.int32)

    def call(kernel, operands, outs, places=()):
        return pl.pallas_call(
            kernel,
            out_shape=outs,
            in_specs=[smem] * len(places) + in_vmem(len(operands)),
            out_specs=in_vmem(len(outs)),
            compiler_params=little,
        )(*places, *operands)

    block = shape(f_rows + 8, width)
    two = shape(2, f_rows + 8, width)
    keep, send, own, up_first, down_first, up_own, down_own = pl.pallas_call(
        functools.partial(maps_kernel, 2, scale, blocks),
        out_shape=[shape(half, b_rows + 8, width)] * 2 + [two, block, block, two, two],
        in_specs=[smem] * 3 + in_vmem(7),
        out_specs=in_vmem(7),
        scratch_shapes=sums_scratch(blocks)
        + [
            pltpu.VMEM((blocks, width, BLK), jnp.bfloat16),
            pltpu.VMEM((blocks * BLK, width), jnp.float32),
            pltpu.VMEM((blocks * BLK, width), jnp.float32),
            pltpu.VMEM((blocks, width, BLK), jnp.float32),
            pltpu.VMEM((2, 8, BLK), jnp.float32),
            pltpu.VMEM((n_tgt, 1, BLK), jnp.float32),
            pltpu.VMEM((2, BLK, BLK), jnp.bfloat16),
            pltpu.VMEM((2, BLK, BLK), jnp.bfloat16),
        ],
        compiler_params=large,
    )(jnp.stack([s_at % 2, t_at % RING]), pair_list, kept, x, y, f, g, *parts)
    came = swap(send, "src", n_src, 1)

    ups = [(k, k // RING * RING + (k + 1) % RING) for k in range(n_tgt)]
    downs = [(b, a) for a, b in ups]
    up_came = lax.ppermute(up_first, "tgt", ups)
    down_came = lax.ppermute(down_first, "tgt", downs)
    paired, up, down = call(
        functools.partial(relay_kernel, f_rows, b_rows),
        [keep, came, up_own, up_came, down_own, down_came],
        [shape(half, b_rows + 8, width), two, two],
    )
    backward = lax.all_to_all(
        paired.reshape(n_z, 2, b_rows + 8, width),
        "src",
        0,
        0,
        axis_index_groups=along_z,
        tiled=True,
    )
    small = shape(b_rows + 8, width)
    keep, send = call(
        functools.partial(z_kernel, b_rows), [backward], [small, small], [(s_at // 2 % 2).reshape(1)]
    )
    came = swap(send, "src", n_src, 2)
    (backward,) = call(functools.partial(last_kernel, b_rows), [keep, came], [shape(b_rows, width)])

    up_came = lax.ppermute(up, "tgt", ups)
    down_came = lax.ppermute(down, "tgt", downs)
    keep, send = call(
        functools.partial(x_kernel, f_rows),
        [own, up_came, down_came],
        [block, block],
        [(t_at // RING).reshape(1)],
    )
    came = swap(send, "tgt", n_tgt, RING)
    (forward,) = call(functools.partial(last_kernel, f_rows), [keep, came], [shape(f_rows, width)])
    return (forward, backward)


def solution(mesh):
    return jax.shard_map(
        functools.partial(per_device, mesh.shape["src"], mesh.shape["tgt"]),
        mesh=mesh,
        in_specs=(P("src", None), P("tgt", None), P("src", "tgt", None, None), P("src", "tgt")),
        out_specs=(P(("src", "tgt"), None), P(("tgt", "src"), None)),
        check_vma=False,
    )
```

```python
import functools
import math

import jax
import jax.numpy as jnp
from jax import lax
from jax.experimental import pallas as pl
from jax.experimental.pallas import tpu as pltpu
from jax.sharding import PartitionSpec as P

BLK = 256
ITERS = 2
NEG = -1e30
RING = 4


def log_sum(parts):
    high = functools.reduce(jnp.maximum, parts)
    total = functools.reduce(jnp.add, [jnp.exp2(part - high) for part in parts])
    return high + jnp.log2(total)


def down_rows(lanes, blocks, wide_ref):
    upright = jnp.transpose(lanes)
    for b in range(blocks):
        wide_ref[b] = jnp.broadcast_to(upright[:, b : b + 1], (BLK, 128))


def norm(z, scale):
    z = z.astype(jnp.float32)
    return jnp.sum(z * z, axis=1, keepdims=True) * (-0.5 * scale)


def across(columns):
    lane = lax.broadcasted_iota(jnp.int32, (BLK, 128), 1)
    gathered = jnp.zeros((BLK, 128), jnp.float32)
    for b, column in enumerate(columns):
        gathered = jnp.where(lane == b, jnp.broadcast_to(column, (BLK, 128)), gathered)
    return jnp.transpose(gathered)[:8]


def over_pairs(pairs_ref, kept, visit):
    def two(step, carry):
        p = 2 * step
        visit(pairs_ref[0, p], pairs_ref[1, p])
        visit(pairs_ref[0, p + 1], pairs_ref[1, p + 1])
        return carry

    lax.fori_loop(0, kept // 2, two, 0)

    @pl.when(kept % 2 == 1)
    def _():
        p = kept - 1
        visit(pairs_ref[0, p], pairs_ref[1, p])


def cross(a, b):
    return lax.dot_general(a, b, (((1,), (1,)), ((), ())), preferred_element_type=jnp.float32)


def fold(scores, wide, scale, high_ref, sum_ref, b):
    for h in range(2):
        at = slice(128 * h, 128 * h + 128)
        t = (scores[:, at] * scale + wide).reshape(BLK // 8, 8, 128)
        old = high_ref[b, :, at]
        high = jnp.maximum(old, jnp.max(t, axis=0))
        total = jnp.sum(jnp.exp2(t - high[None]), axis=0)
        sum_ref[b, :, at] = sum_ref[b, :, at] * jnp.exp2(old - high) + total
        high_ref[b, :, at] = high


def settle(high_ref, sum_ref, blocks):
    rows = []
    for b in range(blocks):
        high = high_ref[b]
        top = jnp.max(high, axis=0, keepdims=True)
        total = jnp.sum(sum_ref[b] * jnp.exp2(high - top), axis=0, keepdims=True)
        rows.append(top + jnp.log2(total))
    rows += [jnp.zeros((1, BLK), jnp.float32)] * (8 - blocks)
    return jnp.concatenate(rows, axis=0)


def new_potential(old_ref, refs):
    parts = [part for r in refs for part in ([r[...]] if len(r.shape) == 2 else [r[k] for k in range(r.shape[0])])]
    return 0.5 * (old_ref[...] - log_sum(parts))


def exponentials(scores_ref, wide, lanes):
    halves = []
    for h in range(2):
        at = slice(128 * h, 128 * h + 128)
        t = (scores_ref[:, at] + wide).reshape(BLK // 8, 8, 128) + lanes[:, at][None]
        halves.append(jnp.exp2(t))
    return halves


def add_sums(halves, row_acc, col_acc, s, t):
    for h, e in enumerate(halves):
        col_acc[t, :, 128 * h : 128 * h + 128] += jnp.sum(e, axis=0)
    row_acc[s] += (halves[0] + halves[1]).reshape(BLK, 128)


def totals(row_acc, col_acc, blocks):
    columns = [jnp.sum(row_acc[b], axis=1, keepdims=True) for b in range(blocks)]
    below = lax.broadcasted_iota(jnp.int32, (8, BLK), 0) >= blocks
    row = jnp.where(below, 1.0, across(columns))
    col = [jnp.sum(col_acc[b], axis=0, keepdims=True) for b in range(blocks)]
    col = jnp.concatenate(col + [jnp.ones((8 - blocks, BLK), jnp.float32)], axis=0)
    low = jnp.minimum(jnp.min(row), jnp.min(col))
    high = jnp.maximum(jnp.max(row), jnp.max(col))
    return columns, row, col, (low >= 2.0**-60) & (high <= 2.0**100)


def clear(*refs):
    for ref in refs:
        ref[...] = jnp.zeros(ref.shape, jnp.float32)


def pass_sums(pairs_ref, kept, x_ref, y_ref, scale, f_wide, g_wide, row_high, row_sum, col_high, col_sum):
    for ref in (row_high, col_high):
        ref[...] = jnp.full(ref.shape, NEG, jnp.float32)
    clear(row_sum, col_sum)

    def visit(s, t):
        xs, yt = x_ref[s], y_ref[t]
        fold(cross(yt, xs), g_wide[t], scale, row_high, row_sum, s)
        fold(cross(xs, yt), f_wide[s], scale, col_high, col_sum, t)

    over_pairs(pairs_ref, kept, visit)


def sweep(pairs_ref, kept, x_ref, y_ref, scores_ref, f, g, shift, scale, blocks, outs, scratch):
    row_out, col_out = outs
    f_wide, g_wide, row_high, row_sum, col_high, col_sum, lanes, row_acc, col_acc = scratch
    spread_lanes(g + shift, blocks, lanes)
    clear(row_acc, col_acc)

    def visit(s, t):
        halves = exponentials(scores_ref.at[t, s], f_wide[s], lanes[t])
        add_sums(halves, row_acc, col_acc, s, t)

    over_pairs(pairs_ref, kept, visit)
    _, row, col, good = totals(row_acc, col_acc, blocks)
    row_out[...] = jnp.log2(row) - (f + shift)
    col_out[...] = jnp.log2(col) - (g + shift)

    @pl.when(jnp.logical_not(good))
    def _():
        down_rows(g, blocks, g_wide)
        pass_sums(pairs_ref, kept, x_ref, y_ref, scale, *scratch[:6])
        row_out[...] = settle(row_high, row_sum, blocks)
        col_out[...] = settle(col_high, col_sum, blocks)


def all_scores(x_ref, y_ref, scale, blocks, scores_ref):
    everything = x_ref[...].reshape(blocks * BLK, BLK)
    for t in range(blocks):
        scores_ref[t] = (cross(everything, y_ref[t]) * scale).reshape(blocks, BLK, BLK)


def first_kernel(scale, blocks, pairs_ref, count_ref, x_ref, y_ref, *rest):
    f_out, g_out, row_out, col_out = rest[:4]
    scratch, scores_ref = rest[4:-1], rest[-1]
    all_scores(x_ref, y_ref, scale, blocks, scores_ref)
    f_wide, g_wide = scratch[:2]
    f_columns, g_columns = [], []
    for b in range(blocks):
        f_columns.append(norm(x_ref[b], scale))
        f_wide[b] = jnp.broadcast_to(f_columns[b], (BLK, 128))
        g_columns.append(norm(y_ref[b], scale))
    f, g = across(f_columns), across(g_columns)
    f_out[...] = f
    g_out[...] = g
    shift = -(jnp.sum(f) + jnp.sum(g)) / (blocks * BLK)
    outs = (row_out, col_out)
    sweep(pairs_ref, count_ref[0], x_ref, y_ref, scores_ref, f, g, shift, scale, blocks, outs, scratch)


def second_kernel(n_row, scale, blocks, pairs_ref, count_ref, x_ref, y_ref, f_old, g_old, *rest):
    parts, rest = rest[: n_row + 1], rest[n_row + 1 :]
    f_out, g_out, row_out, col_out = rest[:4]
    scratch, scores_ref = rest[4:-1], rest[-1]
    all_scores(x_ref, y_ref, scale, blocks, scores_ref)
    f = new_potential(f_old, parts[:n_row])
    g = new_potential(g_old, parts[n_row:])
    f_out[...] = f
    g_out[...] = g
    down_rows(f, blocks, scratch[0])
    outs = (row_out, col_out)
    sweep(pairs_ref, count_ref[0], x_ref, y_ref, scores_ref, f, g, 0.0, scale, blocks, outs, scratch)


def split_two(w):
    high = w.astype(jnp.bfloat16)
    return high, (w - high.astype(jnp.float32)).astype(jnp.bfloat16)


def weigh(scores, scale, lanes, wide):
    halves = []
    for h in range(2):
        at = slice(128 * h, 128 * h + 128)
        t = (scores[:, at] * scale - wide).reshape(BLK // 8, 8, 128) + lanes[:, at][None]
        halves.append(jnp.exp2(t).reshape(BLK, 128))
    return jnp.concatenate(halves, axis=1)


def receivers_lines(log_sums, n, blocks):
    rows = blocks * BLK // n
    lane = lax.broadcasted_iota(jnp.int32, (1, BLK), 1)
    shifted, lines = {}, []
    for b in range(n):
        k, off = b * rows // BLK, b * rows % BLK
        if off not in shifted:
            shifted[off] = pltpu.roll(log_sums, BLK - off, 1) if off else log_sums
        line = shifted[off][k : k + 1]
        if off and k + 1 < blocks:
            line = jnp.where(lane < BLK - off, line, shifted[off][k + 1 : k + 2])
        lines.append(line)
    return lines


def images(pairs_ref, kept, a_ref, b_ref, scale, lanes, wide, image_ref, turned):
    image_ref[...] = jnp.zeros(image_ref.shape, jnp.float32)

    def visit(s, t):
        a, b = (t, s) if turned else (s, t)
        at, bt = a_ref[a], b_ref[b]
        high, low = split_two(weigh(cross(at, bt), scale, lanes[b], wide[a]))
        rows = pl.ds(pl.multiple_of(a * BLK, BLK), BLK)
        image_ref[rows, :] += jnp.dot(high, bt, preferred_element_type=jnp.float32) + jnp.dot(
            low, bt, preferred_element_type=jnp.float32
        )

    over_pairs(pairs_ref, kept, visit)


def spread_lanes(values, blocks, lanes_ref):
    for b in range(blocks):
        lanes_ref[b] = jnp.broadcast_to(values[b : b + 1], (8, BLK))


def maps_kernel(n_row, scale, blocks, place_ref, pairs_ref, count_ref, x_ref, y_ref, f_old, g_old, *rest):
    parts, rest = rest[: n_row + 1], rest[n_row + 1 :]
    keep_out, send_out, own, up_first, down_first, up_own, down_own = rest[:7]
    scratch = rest[7:16]
    f_wide, g_wide, row_high, row_sum, col_high, col_sum, lanes, row_acc, col_acc = scratch
    scores_ref, x_turned, forward, backward, turned, logs, lines_ref, *weights = rest[16:]
    all_scores(x_ref, y_ref, scale, blocks, scores_ref)
    kept = count_ref[0]
    f = new_potential(f_old, parts[:n_row])
    g = new_potential(g_old, parts[n_row:])
    down_rows(f, blocks, f_wide)
    spread_lanes(g, blocks, lanes)
    clear(row_acc, col_acc, forward, turned)
    diagonal = lax.broadcasted_iota(jnp.int32, (BLK, BLK), 0) == lax.broadcasted_iota(jnp.int32, (BLK, BLK), 1)
    unit = jnp.where(diagonal, 1.0, 0.0).astype(jnp.bfloat16)
    for b in range(blocks):
        x_turned[b] = cross(unit, x_ref[b]).astype(jnp.bfloat16)

    def weigh_pair(p, buffer):
        at = jnp.minimum(p, kept - 1)
        s, t = pairs_ref[0, at], pairs_ref[1, at]
        halves = exponentials(scores_ref.at[t, s], f_wide[s], lanes[t])
        counted = jnp.where(p < kept, 1.0, 0.0)
        for h, e in enumerate(halves):
            cols = slice(128 * h, 128 * h + 128)
            col_acc[t, :, cols] += jnp.sum(e, axis=0) * counted
            high, low = split_two(e.reshape(BLK, 128))
            buffer[0, :, cols] = high
            buffer[1, :, cols] = low
        row_acc[s] += (halves[0] + halves[1]).reshape(BLK, 128) * counted

    def add_pair(p, buffer):
        s, t = pairs_ref[0, p], pairs_ref[1, p]
        yt, xt = y_ref[t], x_turned[s]
        high, low = buffer[0], buffer[1]
        rows = pl.ds(pl.multiple_of(s * BLK, BLK), BLK)
        forward[rows, :] += jnp.dot(
            jnp.concatenate([high, low], axis=1),
            jnp.concatenate([yt, yt], axis=0),
            preferred_element_type=jnp.float32,
        )
        turned[t] += jnp.dot(
            jnp.concatenate([xt, xt], axis=1),
            jnp.concatenate([high, low], axis=0),
            preferred_element_type=jnp.float32,
        )

    weigh_pair(0, weights[0])

    def two(step, carry):
        p = 2 * step
        weigh_pair(p + 1, weights[1])
        add_pair(p, weights[0])
        weigh_pair(p + 2, weights[0])
        add_pair(p + 1, weights[1])
        return carry

    lax.fori_loop(0, kept // 2, two, 0)

    @pl.when(kept % 2 == 1)
    def _():
        add_pair(kept - 1, weights[0])

    columns, row, col, good = totals(row_acc, col_acc, blocks)

    @pl.when(good)
    def _():
        logs[0] = jnp.log2(row) - f
        logs[1] = jnp.log2(col) - g
        inverse = 1.0 / col
        for b in range(blocks):
            rows = slice(b * BLK, b * BLK + BLK)
            forward[rows, :] = forward[rows, :] * (1.0 / columns[b])
            backward[rows, :] = jnp.transpose(turned[b] * inverse[b : b + 1])

    @pl.when(jnp.logical_not(good))
    def _():
        down_rows(g, blocks, g_wide)
        pass_sums(pairs_ref, kept, x_ref, y_ref, scale, *scratch[:6])
        row_log = settle(row_high, row_sum, blocks)
        col_log = settle(col_high, col_sum, blocks)
        logs[0] = row_log
        logs[1] = col_log
        down_rows(row_log, blocks, f_wide)
        images(pairs_ref, kept, x_ref, y_ref, scale, lanes, f_wide, forward, False)
        spread_lanes(f, blocks, lanes)
        down_rows(col_log, blocks, g_wide)
        images(pairs_ref, kept, y_ref, x_ref, scale, lanes, g_wide, backward, True)

    n = lines_ref.shape[0]
    rows = blocks * BLK // n
    for b, line in enumerate(receivers_lines(logs[0], n, blocks)):
        lines_ref[b] = line
    me = place_ref[1]

    def put(out, r, high):
        to = ((me + r) % RING) + RING * high
        out[:rows, :] = forward[pl.ds(pl.multiple_of(to * rows, 16), rows), :]
        out[rows : rows + 1, :] = lines_ref[to]

    put(up_first, 2, 0)
    put(down_first, 2, 1)
    put(own.at[0], 0, 0)
    put(own.at[1], 0, 1)
    put(up_own.at[0], 1, 0)
    put(up_own.at[1], 1, 1)
    put(down_own.at[0], 3, 1)
    put(down_own.at[1], 3, 0)

    half = keep_out.shape[0]
    small = blocks * BLK // (2 * half)
    lines = receivers_lines(logs[1], 2 * half, blocks)
    core = place_ref[0]
    for q in range(half):
        for ref, side in ((keep_out, core), (send_out, 1 - core)):
            first = pl.multiple_of((2 * q + side) * small, 16)
            ref[q, :small, :] = backward[pl.ds(first, small), :]
            ref[q, small : small + 1, :] = jnp.where(side == 0, lines[2 * q], lines[2 * q + 1])


def pair_kernel(rows, a_ref, b_ref, out_ref):
    n = a_ref.shape[0]
    a = jnp.concatenate([a_ref[q, rows : rows + 1, :] for q in range(n)], axis=0)
    b = jnp.concatenate([b_ref[q, rows : rows + 1, :] for q in range(n)], axis=0)
    high = jnp.maximum(a, b)
    both = jnp.exp2(a - high) + jnp.exp2(b - high)
    merged = high + jnp.log2(both)
    a_part = jnp.transpose(jnp.exp2(a - high) / both)
    b_part = jnp.transpose(jnp.exp2(b - high) / both)
    for q in range(n):
        out_ref[q, :rows, :] = (
            a_part[:rows, q : q + 1] * a_ref[q, :rows, :]
            + b_part[:rows, q : q + 1] * b_ref[q, :rows, :]
        )
        out_ref[q, rows : rows + 1, :] = merged[q : q + 1]


def blend(parts, rows):
    logs = jnp.concatenate([part[rows : rows + 1, :] for part in parts], axis=0)
    high = jnp.max(logs, axis=0, keepdims=True)
    lifted = jnp.exp2(logs - high)
    whole = jnp.sum(lifted, axis=0, keepdims=True)
    upright = jnp.transpose(lifted / whole)
    total = jnp.zeros((rows, BLK), jnp.float32)
    for d, part in enumerate(parts):
        total += upright[:rows, d : d + 1] * part[:rows, :]
    return total, high + jnp.log2(whole)


def put_blend(out, blended, rows):
    out[:rows, :] = blended[0]
    if out.shape[0] > rows:
        out[rows : rows + 1, :] = blended[1]


def z_kernel(rows, place_ref, paired, up_came, down_came, keep_ref, send_ref):
    here = 2 * place_ref[0]
    for out, low in ((keep_ref, place_ref[1]), (send_ref, 1 - place_ref[1])):
        parts = [paired.at[here + low], up_came.at[low], down_came.at[low]]
        put_blend(out, blend(parts, rows), rows)


def relay_kernel(rows, up_own, up_came, down_own, down_came, up_out, down_out):
    for own, relayed, out in ((up_own, up_came, up_out), (down_own, down_came, down_out)):
        put_blend(out.at[0], blend([own.at[0], relayed], rows), rows)
        out[1] = own[1]


def core_kernel(rows, place_ref, keep, came, paired, up_out, down_out):
    pair_kernel(rows, keep, came, paired)
    n = paired.shape[0] // 2
    far = 2 * ((place_ref[0] + n // 2) % n)
    up_out[...] = paired[far]
    down_out[...] = paired[far + 1]


def ring_kernel(rows, away, place_ref, paired, up_came, down_came, up_out, down_out):
    n = paired.shape[0] // 2
    up_at = 2 * ((place_ref[0] + away) % n)
    down_at = 2 * ((place_ref[0] + n - away) % n)
    for low in range(2):
        for at, came, out, whole in ((up_at, up_came, up_out, 0), (down_at, down_came, down_out, 1)):
            own = paired.at[at + low]
            if len(came.shape) == 3:
                put_blend(out.at[low], blend([own, came.at[low]], rows), rows)
            elif low == whole:
                put_blend(out.at[low], blend([own, came], rows), rows)
            else:
                out[low] = own[...]


def x_kernel(rows, place_ref, own, up_came, down_came, keep_ref, send_ref):
    low = blend([own.at[0], up_came.at[0], down_came.at[1]], rows)
    high = blend([own.at[1], down_came.at[0], up_came.at[1]], rows)

    @pl.when(place_ref[0] == 0)
    def _():
        put_blend(keep_ref, low, rows)
        put_blend(send_ref, high, rows)

    @pl.when(place_ref[0] == 1)
    def _():
        put_blend(keep_ref, high, rows)
        put_blend(send_ref, low, rows)


def last_kernel(rows, a_ref, b_ref, out_ref):
    put_blend(out_ref, blend([a_ref, b_ref], rows), rows)


def in_vmem(n):
    return [pl.BlockSpec(memory_space=pltpu.VMEM)] * n


def shape(*dims):
    return jax.ShapeDtypeStruct(dims, jnp.float32)


def sums_scratch(blocks):
    wide = pltpu.VMEM((blocks, BLK, 128), jnp.float32)
    deep = pltpu.VMEM((blocks, 8, BLK), jnp.float32)
    return [wide] * 2 + [deep] * 5 + [wide, deep, pltpu.VMEM((blocks, blocks, BLK, BLK), jnp.float32)]


def per_device(n_src, n_tgt, sources, targets, pairs, counts):
    width = sources.shape[1]
    scale = math.log2(math.e) / (math.sqrt(width) / 4.0)
    blocks = sources.shape[0] // BLK
    x = sources.reshape(blocks, BLK, width)
    y = targets.reshape(blocks, BLK, width)
    pair_list = jnp.transpose(pairs[0, 0])
    kept = counts.reshape(-1)
    smem = pl.BlockSpec(memory_space=pltpu.SMEM)
    large = pltpu.CompilerParams(vmem_limit_bytes=36 * 1024 * 1024)
    little = pltpu.CompilerParams(vmem_limit_bytes=8 * 1024 * 1024)

    def swap(value, axis, size, bit):
        return lax.ppermute(value, axis, [(k, k ^ bit) for k in range(size)])

    n_z = n_src // 4
    along_z = [list(range(k, n_src, 4)) for k in range(4)]

    def exchange(row, col):
        row = log_sum([row, swap(row, "tgt", n_tgt, RING)])
        col = log_sum([col] + [swap(col, "src", n_src, bits) for bits in (1, 2, 3)])
        row = log_sum([row, swap(row, "tgt", n_tgt, 2)])
        copies = jnp.broadcast_to(col[None], (n_z, *col.shape))
        cols = lax.all_to_all(copies, "src", 0, 0, axis_index_groups=along_z, tiled=True)
        return [row, swap(row, "tgt", n_tgt, 1), cols]

    f, g, row, col = pl.pallas_call(
        functools.partial(first_kernel, scale, blocks),
        out_shape=[shape(8, BLK)] * 4,
        in_specs=[smem] * 2 + in_vmem(2),
        out_specs=in_vmem(4),
        scratch_shapes=sums_scratch(blocks),
        compiler_params=large,
    )(pair_list, kept, x, y)
    parts = exchange(row, col)
    f, g, row, col = pl.pallas_call(
        functools.partial(second_kernel, 2, scale, blocks),
        out_shape=[shape(8, BLK)] * 4,
        in_specs=[smem] * 2 + in_vmem(7),
        out_specs=in_vmem(4),
        scratch_shapes=sums_scratch(blocks),
        compiler_params=large,
    )(pair_list, kept, x, y, f, g, *parts)
    parts = exchange(row, col)

    f_rows, b_rows = blocks * BLK // n_tgt, blocks * BLK // n_src
    half = n_src // 2
    s_at = lax.axis_index("src").astype(jnp.int32)
    t_at = lax.axis_index("tgt").astype(jnp.int32)

    def call(kernel, operands, outs, places=()):
        return pl.pallas_call(
            kernel,
            out_shape=outs,
            in_specs=[smem] * len(places) + in_vmem(len(operands)),
            out_specs=in_vmem(len(outs)),
            compiler_params=little,
        )(*places, *operands)

    block = shape(f_rows + 8, width)
    two = shape(2, f_rows + 8, width)
    keep, send, own, up_first, down_first, up_own, down_own = pl.pallas_call(
        functools.partial(maps_kernel, 2, scale, blocks),
        out_shape=[shape(half, b_rows + 8, width)] * 2 + [two, block, block, two, two],
        in_specs=[smem] * 3 + in_vmem(7),
        out_specs=in_vmem(7),
        scratch_shapes=sums_scratch(blocks)
        + [
            pltpu.VMEM((blocks, width, BLK), jnp.bfloat16),
            pltpu.VMEM((blocks * BLK, width), jnp.float32),
            pltpu.VMEM((blocks * BLK, width), jnp.float32),
            pltpu.VMEM((blocks, width, BLK), jnp.float32),
            pltpu.VMEM((2, 8, BLK), jnp.float32),
            pltpu.VMEM((n_tgt, 1, BLK), jnp.float32),
            pltpu.VMEM((2, BLK, BLK), jnp.bfloat16),
            pltpu.VMEM((2, BLK, BLK), jnp.bfloat16),
        ],
        compiler_params=large,
    )(jnp.stack([s_at % 2, t_at % RING]), pair_list, kept, x, y, f, g, *parts)
    came = swap(send, "src", n_src, 1)

    ups = [(k, k // RING * RING + (k + 1) % RING) for k in range(n_tgt)]
    downs = [(b, a) for a, b in ups]
    up_came = lax.ppermute(up_first, "tgt", ups)
    down_came = lax.ppermute(down_first, "tgt", downs)
    small = shape(b_rows + 8, width)
    small_two = shape(2, b_rows + 8, width)
    z_at = (s_at // 4).reshape(1)
    paired, z_up, z_down = call(
        functools.partial(core_kernel, b_rows),
        [keep, came],
        [shape(half, b_rows + 8, width), small, small],
        [z_at],
    )
    z_ups = [(k, (k + 4) % n_src) for k in range(n_src)]
    z_downs = [(b, a) for a, b in z_ups]
    for away in range(n_z // 2 - 1, -1, -1):
        z_up = lax.ppermute(z_up, "src", z_ups)
        z_down = lax.ppermute(z_down, "src", z_downs)
        if away:
            z_up, z_down = call(
                functools.partial(ring_kernel, b_rows, away),
                [paired, z_up, z_down],
                [small_two, small_two],
                [z_at],
            )
    keep, send = call(
        functools.partial(z_kernel, b_rows),
        [paired, z_up, z_down],
        [small, small],
        [jnp.stack([s_at // 4, s_at // 2 % 2])],
    )
    came = swap(send, "src", n_src, 2)
    (backward,) = call(functools.partial(last_kernel, b_rows), [keep, came], [shape(b_rows, width)])

    up, down = call(
        functools.partial(relay_kernel, f_rows),
        [up_own, up_came, down_own, down_came],
        [two, two],
    )
    up_came = lax.ppermute(up, "tgt", ups)
    down_came = lax.ppermute(down, "tgt", downs)
    keep, send = call(
        functools.partial(x_kernel, f_rows),
        [own, up_came, down_came],
        [block, block],
        [(t_at // RING).reshape(1)],
    )
    came = swap(send, "tgt", n_tgt, RING)
    (forward,) = call(functools.partial(last_kernel, f_rows), [keep, came], [shape(f_rows, width)])
    return (forward, backward)


def solution(mesh):
    return jax.shard_map(
        functools.partial(per_device, mesh.shape["src"], mesh.shape["tgt"]),
        mesh=mesh,
        in_specs=(P("src", None), P("tgt", None), P("src", "tgt", None, None), P("src", "tgt")),
        out_specs=(P(("src", "tgt"), None), P(("tgt", "src"), None)),
        check_vma=False,
    )
```

```python
import functools
import math

import jax
import jax.numpy as jnp
from jax import lax
from jax.experimental import pallas as pl
from jax.experimental.pallas import tpu as pltpu
from jax.sharding import PartitionSpec as P

BLK = 256
ITERS = 2
NEG = -1e30
RING = 4


def log_sum(parts):
    high = functools.reduce(jnp.maximum, parts)
    total = functools.reduce(jnp.add, [jnp.exp2(part - high) for part in parts])
    return high + jnp.log2(total)


def down_rows(lanes, blocks, wide_ref):
    upright = jnp.transpose(lanes)
    for b in range(blocks):
        wide_ref[b] = jnp.broadcast_to(upright[:, b : b + 1], (BLK, 128))


def norm(z, scale):
    z = z.astype(jnp.float32)
    return jnp.sum(z * z, axis=1, keepdims=True) * (-0.5 * scale)


def across(columns):
    lane = lax.broadcasted_iota(jnp.int32, (BLK, 128), 1)
    gathered = jnp.zeros((BLK, 128), jnp.float32)
    for b, column in enumerate(columns):
        gathered = jnp.where(lane == b, jnp.broadcast_to(column, (BLK, 128)), gathered)
    return jnp.transpose(gathered)[:8]


def over_pairs(pairs_ref, kept, visit):
    def two(step, carry):
        p = 2 * step
        visit(pairs_ref[0, p], pairs_ref[1, p])
        visit(pairs_ref[0, p + 1], pairs_ref[1, p + 1])
        return carry

    lax.fori_loop(0, kept // 2, two, 0)

    @pl.when(kept % 2 == 1)
    def _():
        p = kept - 1
        visit(pairs_ref[0, p], pairs_ref[1, p])


def cross(a, b):
    return lax.dot_general(a, b, (((1,), (1,)), ((), ())), preferred_element_type=jnp.float32)


def fold(scores, wide, scale, high_ref, sum_ref, b):
    for h in range(2):
        at = slice(128 * h, 128 * h + 128)
        t = (scores[:, at] * scale + wide).reshape(BLK // 8, 8, 128)
        old = high_ref[b, :, at]
        high = jnp.maximum(old, jnp.max(t, axis=0))
        total = jnp.sum(jnp.exp2(t - high[None]), axis=0)
        sum_ref[b, :, at] = sum_ref[b, :, at] * jnp.exp2(old - high) + total
        high_ref[b, :, at] = high


def settle(high_ref, sum_ref, blocks):
    rows = []
    for b in range(blocks):
        high = high_ref[b]
        top = jnp.max(high, axis=0, keepdims=True)
        total = jnp.sum(sum_ref[b] * jnp.exp2(high - top), axis=0, keepdims=True)
        rows.append(top + jnp.log2(total))
    rows += [jnp.zeros((1, BLK), jnp.float32)] * (8 - blocks)
    return jnp.concatenate(rows, axis=0)


def new_potential(old_ref, refs):
    parts = [part for r in refs for part in ([r[...]] if len(r.shape) == 2 else [r[k] for k in range(r.shape[0])])]
    return 0.5 * (old_ref[...] - log_sum(parts))


def exponentials(scores_ref, wide, lanes):
    halves = []
    for h in range(2):
        at = slice(128 * h, 128 * h + 128)
        t = (scores_ref[:, at] + wide).reshape(BLK // 8, 8, 128) + lanes[:, at][None]
        halves.append(jnp.exp2(t))
    return halves


def add_sums(halves, row_acc, col_acc, s, t):
    for h, e in enumerate(halves):
        col_acc[t, :, 128 * h : 128 * h + 128] += jnp.sum(e, axis=0)
    row_acc[s] += (halves[0] + halves[1]).reshape(BLK, 128)


def totals(row_acc, col_acc, blocks):
    columns = [jnp.sum(row_acc[b], axis=1, keepdims=True) for b in range(blocks)]
    below = lax.broadcasted_iota(jnp.int32, (8, BLK), 0) >= blocks
    row = jnp.where(below, 1.0, across(columns))
    col = [jnp.sum(col_acc[b], axis=0, keepdims=True) for b in range(blocks)]
    col = jnp.concatenate(col + [jnp.ones((8 - blocks, BLK), jnp.float32)], axis=0)
    low = jnp.minimum(jnp.min(row), jnp.min(col))
    high = jnp.maximum(jnp.max(row), jnp.max(col))
    return columns, row, col, (low >= 2.0**-60) & (high <= 2.0**100)


def clear(*refs):
    for ref in refs:
        ref[...] = jnp.zeros(ref.shape, jnp.float32)


def pass_sums(pairs_ref, kept, x_ref, y_ref, scale, f_wide, g_wide, row_high, row_sum, col_high, col_sum):
    for ref in (row_high, col_high):
        ref[...] = jnp.full(ref.shape, NEG, jnp.float32)
    clear(row_sum, col_sum)

    def visit(s, t):
        xs, yt = x_ref[s], y_ref[t]
        fold(cross(yt, xs), g_wide[t], scale, row_high, row_sum, s)
        fold(cross(xs, yt), f_wide[s], scale, col_high, col_sum, t)

    over_pairs(pairs_ref, kept, visit)


def sweep(pairs_ref, kept, x_ref, y_ref, scores_ref, f, g, shift, scale, blocks, outs, scratch):
    row_out, col_out = outs
    f_wide, g_wide, row_high, row_sum, col_high, col_sum, lanes, row_acc, col_acc = scratch
    spread_lanes(g + shift, blocks, lanes)
    clear(row_acc, col_acc)

    def visit(s, t):
        halves = exponentials(scores_ref.at[t, s], f_wide[s], lanes[t])
        add_sums(halves, row_acc, col_acc, s, t)

    over_pairs(pairs_ref, kept, visit)
    _, row, col, good = totals(row_acc, col_acc, blocks)
    row_out[...] = jnp.log2(row) - (f + shift)
    col_out[...] = jnp.log2(col) - (g + shift)

    @pl.when(jnp.logical_not(good))
    def _():
        down_rows(g, blocks, g_wide)
        pass_sums(pairs_ref, kept, x_ref, y_ref, scale, *scratch[:6])
        row_out[...] = settle(row_high, row_sum, blocks)
        col_out[...] = settle(col_high, col_sum, blocks)


def all_scores(x_ref, y_ref, scale, blocks, scores_ref):
    everything = x_ref[...].reshape(blocks * BLK, BLK)
    for t in range(blocks):
        scores_ref[t] = (cross(everything, y_ref[t]) * scale).reshape(blocks, BLK, BLK)


def first_kernel(scale, blocks, pairs_ref, count_ref, x_ref, y_ref, *rest):
    f_out, g_out, row_out, col_out = rest[:4]
    scratch, scores_ref = rest[4:-1], rest[-1]
    all_scores(x_ref, y_ref, scale, blocks, scores_ref)
    f_wide, g_wide = scratch[:2]
    f_columns, g_columns = [], []
    for b in range(blocks):
        f_columns.append(norm(x_ref[b], scale))
        f_wide[b] = jnp.broadcast_to(f_columns[b], (BLK, 128))
        g_columns.append(norm(y_ref[b], scale))
    f, g = across(f_columns), across(g_columns)
    f_out[...] = f
    g_out[...] = g
    shift = -(jnp.sum(f) + jnp.sum(g)) / (blocks * BLK)
    outs = (row_out, col_out)
    sweep(pairs_ref, count_ref[0], x_ref, y_ref, scores_ref, f, g, shift, scale, blocks, outs, scratch)


def second_kernel(n_row, scale, blocks, pairs_ref, count_ref, x_ref, y_ref, f_old, g_old, *rest):
    parts, rest = rest[: n_row + 1], rest[n_row + 1 :]
    f_out, g_out, row_out, col_out = rest[:4]
    scratch, scores_ref = rest[4:-1], rest[-1]
    all_scores(x_ref, y_ref, scale, blocks, scores_ref)
    f = new_potential(f_old, parts[:n_row])
    g = new_potential(g_old, parts[n_row:])
    f_out[...] = f
    g_out[...] = g
    down_rows(f, blocks, scratch[0])
    outs = (row_out, col_out)
    sweep(pairs_ref, count_ref[0], x_ref, y_ref, scores_ref, f, g, 0.0, scale, blocks, outs, scratch)


def split_two(w):
    high = w.astype(jnp.bfloat16)
    return high, (w - high.astype(jnp.float32)).astype(jnp.bfloat16)


def weigh(scores, scale, lanes, wide):
    halves = []
    for h in range(2):
        at = slice(128 * h, 128 * h + 128)
        t = (scores[:, at] * scale - wide).reshape(BLK // 8, 8, 128) + lanes[:, at][None]
        halves.append(jnp.exp2(t).reshape(BLK, 128))
    return jnp.concatenate(halves, axis=1)


def receivers_lines(log_sums, n, blocks):
    rows = blocks * BLK // n
    lane = lax.broadcasted_iota(jnp.int32, (1, BLK), 1)
    shifted, lines = {}, []
    for b in range(n):
        k, off = b * rows // BLK, b * rows % BLK
        if off not in shifted:
            shifted[off] = pltpu.roll(log_sums, BLK - off, 1) if off else log_sums
        line = shifted[off][k : k + 1]
        if off and k + 1 < blocks:
            line = jnp.where(lane < BLK - off, line, shifted[off][k + 1 : k + 2])
        lines.append(line)
    return lines


def images(pairs_ref, kept, a_ref, b_ref, scale, lanes, wide, image_ref, turned):
    image_ref[...] = jnp.zeros(image_ref.shape, jnp.float32)

    def visit(s, t):
        a, b = (t, s) if turned else (s, t)
        at, bt = a_ref[a], b_ref[b]
        high, low = split_two(weigh(cross(at, bt), scale, lanes[b], wide[a]))
        rows = pl.ds(pl.multiple_of(a * BLK, BLK), BLK)
        image_ref[rows, :] += jnp.dot(high, bt, preferred_element_type=jnp.float32) + jnp.dot(
            low, bt, preferred_element_type=jnp.float32
        )

    over_pairs(pairs_ref, kept, visit)


def spread_lanes(values, blocks, lanes_ref):
    for b in range(blocks):
        lanes_ref[b] = jnp.broadcast_to(values[b : b + 1], (8, BLK))


def maps_kernel(n_row, scale, blocks, place_ref, pairs_ref, count_ref, x_ref, y_ref, f_old, g_old, *rest):
    parts, rest = rest[: n_row + 1], rest[n_row + 1 :]
    keep_out, send_out, own, up_first, down_first, up_own, down_own = rest[:7]
    scratch = rest[7:16]
    f_wide, g_wide, row_high, row_sum, col_high, col_sum, lanes, row_acc, col_acc = scratch
    scores_ref, x_turned, forward, backward, turned, logs, lines_ref, *weights = rest[16:]
    all_scores(x_ref, y_ref, scale, blocks, scores_ref)
    kept = count_ref[0]
    f = new_potential(f_old, parts[:n_row])
    g = new_potential(g_old, parts[n_row:])
    down_rows(f, blocks, f_wide)
    spread_lanes(g, blocks, lanes)
    clear(row_acc, col_acc, forward, turned)
    diagonal = lax.broadcasted_iota(jnp.int32, (BLK, BLK), 0) == lax.broadcasted_iota(jnp.int32, (BLK, BLK), 1)
    unit = jnp.where(diagonal, 1.0, 0.0).astype(jnp.bfloat16)
    for b in range(blocks):
        x_turned[b] = cross(unit, x_ref[b]).astype(jnp.bfloat16)

    def weigh_pair(p, buffer):
        at = jnp.minimum(p, kept - 1)
        s, t = pairs_ref[0, at], pairs_ref[1, at]
        halves = exponentials(scores_ref.at[t, s], f_wide[s], lanes[t])
        counted = jnp.where(p < kept, 1.0, 0.0)
        for h, e in enumerate(halves):
            cols = slice(128 * h, 128 * h + 128)
            col_acc[t, :, cols] += jnp.sum(e, axis=0) * counted
            high, low = split_two(e.reshape(BLK, 128))
            buffer[0, :, cols] = high
            buffer[1, :, cols] = low
        row_acc[s] += (halves[0] + halves[1]).reshape(BLK, 128) * counted

    def add_pair(p, buffer):
        s, t = pairs_ref[0, p], pairs_ref[1, p]
        yt, xt = y_ref[t], x_turned[s]
        high, low = buffer[0], buffer[1]
        rows = pl.ds(pl.multiple_of(s * BLK, BLK), BLK)
        forward[rows, :] += jnp.dot(
            jnp.concatenate([high, low], axis=1),
            jnp.concatenate([yt, yt], axis=0),
            preferred_element_type=jnp.float32,
        )
        turned[t] += jnp.dot(
            jnp.concatenate([xt, xt], axis=1),
            jnp.concatenate([high, low], axis=0),
            preferred_element_type=jnp.float32,
        )

    weigh_pair(0, weights[0])

    def two(step, carry):
        p = 2 * step
        weigh_pair(p + 1, weights[1])
        add_pair(p, weights[0])
        weigh_pair(p + 2, weights[0])
        add_pair(p + 1, weights[1])
        return carry

    lax.fori_loop(0, kept // 2, two, 0)

    @pl.when(kept % 2 == 1)
    def _():
        add_pair(kept - 1, weights[0])

    columns, row, col, good = totals(row_acc, col_acc, blocks)

    @pl.when(good)
    def _():
        logs[0] = jnp.log2(row) - f
        logs[1] = jnp.log2(col) - g
        inverse = 1.0 / col
        for b in range(blocks):
            rows = slice(b * BLK, b * BLK + BLK)
            forward[rows, :] = forward[rows, :] * (1.0 / columns[b])
            backward[rows, :] = jnp.transpose(turned[b] * inverse[b : b + 1])

    @pl.when(jnp.logical_not(good))
    def _():
        down_rows(g, blocks, g_wide)
        pass_sums(pairs_ref, kept, x_ref, y_ref, scale, *scratch[:6])
        row_log = settle(row_high, row_sum, blocks)
        col_log = settle(col_high, col_sum, blocks)
        logs[0] = row_log
        logs[1] = col_log
        down_rows(row_log, blocks, f_wide)
        images(pairs_ref, kept, x_ref, y_ref, scale, lanes, f_wide, forward, False)
        spread_lanes(f, blocks, lanes)
        down_rows(col_log, blocks, g_wide)
        images(pairs_ref, kept, y_ref, x_ref, scale, lanes, g_wide, backward, True)

    n = lines_ref.shape[0]
    rows = blocks * BLK // n
    for b, line in enumerate(receivers_lines(logs[0], n, blocks)):
        lines_ref[b] = line
    me = place_ref[1]

    def put(out, r, high):
        to = ((me + r) % RING) + RING * high
        out[:rows, :] = forward[pl.ds(pl.multiple_of(to * rows, 16), rows), :]
        out[rows : rows + 1, :] = lines_ref[to]

    put(up_first, 2, 0)
    put(down_first, 2, 1)
    put(own.at[0], 0, 0)
    put(own.at[1], 0, 1)
    put(up_own.at[0], 1, 0)
    put(up_own.at[1], 1, 1)
    put(down_own.at[0], 3, 1)
    put(down_own.at[1], 3, 0)

    half = keep_out.shape[0]
    small = blocks * BLK // (2 * half)
    lines = receivers_lines(logs[1], 2 * half, blocks)
    core = place_ref[0]
    for q in range(half):
        for ref, side in ((keep_out, core), (send_out, 1 - core)):
            first = pl.multiple_of((2 * q + side) * small, 16)
            ref[q, :small, :] = backward[pl.ds(first, small), :]
            ref[q, small : small + 1, :] = jnp.where(side == 0, lines[2 * q], lines[2 * q + 1])


def pair_kernel(rows, a_ref, b_ref, out_ref):
    n = a_ref.shape[0]
    a = jnp.concatenate([a_ref[q, rows : rows + 1, :] for q in range(n)], axis=0)
    b = jnp.concatenate([b_ref[q, rows : rows + 1, :] for q in range(n)], axis=0)
    high = jnp.maximum(a, b)
    both = jnp.exp2(a - high) + jnp.exp2(b - high)
    merged = high + jnp.log2(both)
    a_part = jnp.transpose(jnp.exp2(a - high) / both)
    b_part = jnp.transpose(jnp.exp2(b - high) / both)
    for q in range(n):
        out_ref[q, :rows, :] = (
            a_part[:rows, q : q + 1] * a_ref[q, :rows, :]
            + b_part[:rows, q : q + 1] * b_ref[q, :rows, :]
        )
        out_ref[q, rows : rows + 1, :] = merged[q : q + 1]


def blend(parts, rows):
    logs = jnp.concatenate([part[rows : rows + 1, :] for part in parts], axis=0)
    high = jnp.max(logs, axis=0, keepdims=True)
    lifted = jnp.exp2(logs - high)
    whole = jnp.sum(lifted, axis=0, keepdims=True)
    upright = jnp.transpose(lifted / whole)
    total = jnp.zeros((rows, BLK), jnp.float32)
    for d, part in enumerate(parts):
        total += upright[:rows, d : d + 1] * part[:rows, :]
    return total, high + jnp.log2(whole)


def put_blend(out, blended, rows):
    out[:rows, :] = blended[0]
    if out.shape[0] > rows:
        out[rows : rows + 1, :] = blended[1]


def z_kernel(rows, place_ref, paired, up_came, down_came, keep_ref, send_ref):
    here = 2 * place_ref[0]
    for out, low in ((keep_ref, place_ref[1]), (send_ref, 1 - place_ref[1])):
        parts = [paired.at[here + low], up_came.at[low], down_came.at[low]]
        put_blend(out, blend(parts, rows), rows)


def relay_kernel(rows, up_own, up_came, down_own, down_came, up_out, down_out):
    for own, relayed, out in ((up_own, up_came, up_out), (down_own, down_came, down_out)):
        put_blend(out.at[0], blend([own.at[0], relayed], rows), rows)
        out[1] = own[1]


def core_kernel(rows, place_ref, keep, came, paired, up_out, down_out):
    pair_kernel(rows, keep, came, paired)
    n = paired.shape[0] // 2
    far = 2 * ((place_ref[0] + n // 2) % n)
    up_out[...] = paired[far]
    down_out[...] = paired[far + 1]


def ring_kernel(rows, away, place_ref, paired, up_came, down_came, up_out, down_out):
    n = paired.shape[0] // 2
    up_at = 2 * ((place_ref[0] + away) % n)
    down_at = 2 * ((place_ref[0] + n - away) % n)
    for low in range(2):
        for at, came, out, whole in ((up_at, up_came, up_out, 0), (down_at, down_came, down_out, 1)):
            own = paired.at[at + low]
            if len(came.shape) == 3:
                put_blend(out.at[low], blend([own, came.at[low]], rows), rows)
            elif low == whole:
                put_blend(out.at[low], blend([own, came], rows), rows)
            else:
                out[low] = own[...]


def x_kernel(rows, place_ref, own, up_came, down_came, keep_ref, send_ref):
    low = blend([own.at[0], up_came.at[0], down_came.at[1]], rows)
    high = blend([own.at[1], down_came.at[0], up_came.at[1]], rows)

    @pl.when(place_ref[0] == 0)
    def _():
        put_blend(keep_ref, low, rows)
        put_blend(send_ref, high, rows)

    @pl.when(place_ref[0] == 1)
    def _():
        put_blend(keep_ref, high, rows)
        put_blend(send_ref, low, rows)


def last_kernel(rows, a_ref, b_ref, out_ref):
    put_blend(out_ref, blend([a_ref, b_ref], rows), rows)


def in_vmem(n):
    return [pl.BlockSpec(memory_space=pltpu.VMEM)] * n


def shape(*dims):
    return jax.ShapeDtypeStruct(dims, jnp.float32)


def sums_scratch(blocks):
    wide = pltpu.VMEM((blocks, BLK, 128), jnp.float32)
    deep = pltpu.VMEM((blocks, 8, BLK), jnp.float32)
    return [wide] * 2 + [deep] * 5 + [wide, deep, pltpu.VMEM((blocks, blocks, BLK, BLK), jnp.float32)]


def per_device(n_src, n_tgt, sources, targets, pairs, counts):
    width = sources.shape[1]
    scale = math.log2(math.e) / (math.sqrt(width) / 4.0)
    blocks = sources.shape[0] // BLK
    x = sources.reshape(blocks, BLK, width)
    y = targets.reshape(blocks, BLK, width)
    pair_list = jnp.transpose(pairs[0, 0])
    kept = counts.reshape(-1)
    smem = pl.BlockSpec(memory_space=pltpu.SMEM)
    large = pltpu.CompilerParams(vmem_limit_bytes=26 * 1024 * 1024)
    little = pltpu.CompilerParams(vmem_limit_bytes=8 * 1024 * 1024)

    def swap(value, axis, size, bit):
        return lax.ppermute(value, axis, [(k, k ^ bit) for k in range(size)])

    n_z = n_src // 4
    along_z = [list(range(k, n_src, 4)) for k in range(4)]

    def exchange(row, col):
        row = log_sum([row, swap(row, "tgt", n_tgt, RING)])
        col = log_sum([col] + [swap(col, "src", n_src, bits) for bits in (1, 2, 3)])
        row = log_sum([row, swap(row, "tgt", n_tgt, 2)])
        copies = jnp.broadcast_to(col[None], (n_z, *col.shape))
        cols = lax.all_to_all(copies, "src", 0, 0, axis_index_groups=along_z, tiled=True)
        return [row, swap(row, "tgt", n_tgt, 1), cols]

    f, g, row, col = pl.pallas_call(
        functools.partial(first_kernel, scale, blocks),
        out_shape=[shape(8, BLK)] * 4,
        in_specs=[smem] * 2 + in_vmem(2),
        out_specs=in_vmem(4),
        scratch_shapes=sums_scratch(blocks),
        compiler_params=large,
    )(pair_list, kept, x, y)
    parts = exchange(row, col)
    f, g, row, col = pl.pallas_call(
        functools.partial(second_kernel, 2, scale, blocks),
        out_shape=[shape(8, BLK)] * 4,
        in_specs=[smem] * 2 + in_vmem(7),
        out_specs=in_vmem(4),
        scratch_shapes=sums_scratch(blocks),
        compiler_params=large,
    )(pair_list, kept, x, y, f, g, *parts)
    parts = exchange(row, col)

    f_rows, b_rows = blocks * BLK // n_tgt, blocks * BLK // n_src
    half = n_src // 2
    s_at = lax.axis_index("src").astype(jnp.int32)
    t_at = lax.axis_index("tgt").astype(jnp.int32)

    def call(kernel, operands, outs, places=()):
        return pl.pallas_call(
            kernel,
            out_shape=outs,
            in_specs=[smem] * len(places) + in_vmem(len(operands)),
            out_specs=in_vmem(len(outs)),
            compiler_params=little,
        )(*places, *operands)

    block = shape(f_rows + 8, width)
    two = shape(2, f_rows + 8, width)
    keep, send, own, up_first, down_first, up_own, down_own = pl.pallas_call(
        functools.partial(maps_kernel, 2, scale, blocks),
        out_shape=[shape(half, b_rows + 8, width)] * 2 + [two, block, block, two, two],
        in_specs=[smem] * 3 + in_vmem(7),
        out_specs=in_vmem(7),
        scratch_shapes=sums_scratch(blocks)
        + [
            pltpu.VMEM((blocks, width, BLK), jnp.bfloat16),
            pltpu.VMEM((blocks * BLK, width), jnp.float32),
            pltpu.VMEM((blocks * BLK, width), jnp.float32),
            pltpu.VMEM((blocks, width, BLK), jnp.float32),
            pltpu.VMEM((2, 8, BLK), jnp.float32),
            pltpu.VMEM((n_tgt, 1, BLK), jnp.float32),
            pltpu.VMEM((2, BLK, BLK), jnp.bfloat16),
            pltpu.VMEM((2, BLK, BLK), jnp.bfloat16),
        ],
        compiler_params=large,
    )(jnp.stack([s_at % 2, t_at % RING]), pair_list, kept, x, y, f, g, *parts)
    came = swap(send, "src", n_src, 1)

    ups = [(k, k // RING * RING + (k + 1) % RING) for k in range(n_tgt)]
    downs = [(b, a) for a, b in ups]
    up_came = lax.ppermute(up_first, "tgt", ups)
    down_came = lax.ppermute(down_first, "tgt", downs)
    small = shape(b_rows + 8, width)
    small_two = shape(2, b_rows + 8, width)
    z_at = (s_at // 4).reshape(1)
    paired, z_up, z_down = call(
        functools.partial(core_kernel, b_rows),
        [keep, came],
        [shape(half, b_rows + 8, width), small, small],
        [z_at],
    )
    z_ups = [(k, (k + 4) % n_src) for k in range(n_src)]
    z_downs = [(b, a) for a, b in z_ups]
    for away in range(n_z // 2 - 1, -1, -1):
        z_up = lax.ppermute(z_up, "src", z_ups)
        z_down = lax.ppermute(z_down, "src", z_downs)
        if away == n_z // 2 - 1:
            up_came, down_came, z_up, z_down = lax.optimization_barrier(
                (up_came, down_came, z_up, z_down)
            )
        if away:
            z_up, z_down = call(
                functools.partial(ring_kernel, b_rows, away),
                [paired, z_up, z_down],
                [small_two, small_two],
                [z_at],
            )
    keep, send = call(
        functools.partial(z_kernel, b_rows),
        [paired, z_up, z_down],
        [small, small],
        [jnp.stack([s_at // 4, s_at // 2 % 2])],
    )
    came = swap(send, "src", n_src, 2)
    (backward,) = call(functools.partial(last_kernel, b_rows), [keep, came], [shape(b_rows, width)])

    up, down = call(
        functools.partial(relay_kernel, f_rows),
        [up_own, up_came, down_own, down_came],
        [two, two],
    )
    up_came = lax.ppermute(up, "tgt", ups)
    down_came = lax.ppermute(down, "tgt", downs)
    keep, send = call(
        functools.partial(x_kernel, f_rows),
        [own, up_came, down_came],
        [block, block],
        [(t_at // RING).reshape(1)],
    )
    came = swap(send, "tgt", n_tgt, RING)
    (forward,) = call(functools.partial(last_kernel, f_rows), [keep, came], [shape(f_rows, width)])
    return (forward, backward)


def solution(mesh):
    return jax.shard_map(
        functools.partial(per_device, mesh.shape["src"], mesh.shape["tgt"]),
        mesh=mesh,
        in_specs=(P("src", None), P("tgt", None), P("src", "tgt", None, None), P("src", "tgt")),
        out_specs=(P(("src", "tgt"), None), P(("tgt", "src"), None)),
        check_vma=False,
    )
```

```python
import functools
import math

import jax
import jax.numpy as jnp
from jax import lax
from jax.experimental import pallas as pl
from jax.experimental.pallas import tpu as pltpu
from jax.sharding import PartitionSpec as P

BLK = 256
ITERS = 2
NEG = -1e30
RING = 4


def log_sum(parts):
    high = functools.reduce(jnp.maximum, parts)
    total = functools.reduce(jnp.add, [jnp.exp2(part - high) for part in parts])
    return high + jnp.log2(total)


def down_rows(lanes, blocks, wide_ref):
    upright = jnp.transpose(lanes)
    for b in range(blocks):
        wide_ref[b] = jnp.broadcast_to(upright[:, b : b + 1], (BLK, 128))


def norm(z, scale):
    z = z.astype(jnp.float32)
    return jnp.sum(z * z, axis=1, keepdims=True) * (-0.5 * scale)


def across(columns):
    lane = lax.broadcasted_iota(jnp.int32, (BLK, 128), 1)
    gathered = jnp.zeros((BLK, 128), jnp.float32)
    for b, column in enumerate(columns):
        gathered = jnp.where(lane == b, jnp.broadcast_to(column, (BLK, 128)), gathered)
    return jnp.transpose(gathered)[:8]


def over_pairs(pairs_ref, kept, visit):
    def two(step, carry):
        p = 2 * step
        visit(pairs_ref[0, p], pairs_ref[1, p])
        visit(pairs_ref[0, p + 1], pairs_ref[1, p + 1])
        return carry

    lax.fori_loop(0, kept // 2, two, 0)

    @pl.when(kept % 2 == 1)
    def _():
        p = kept - 1
        visit(pairs_ref[0, p], pairs_ref[1, p])


def cross(a, b):
    return lax.dot_general(a, b, (((1,), (1,)), ((), ())), preferred_element_type=jnp.float32)


def fold(scores, wide, scale, high_ref, sum_ref, b):
    for h in range(2):
        at = slice(128 * h, 128 * h + 128)
        t = (scores[:, at] * scale + wide).reshape(BLK // 8, 8, 128)
        old = high_ref[b, :, at]
        high = jnp.maximum(old, jnp.max(t, axis=0))
        total = jnp.sum(jnp.exp2(t - high[None]), axis=0)
        sum_ref[b, :, at] = sum_ref[b, :, at] * jnp.exp2(old - high) + total
        high_ref[b, :, at] = high


def settle(high_ref, sum_ref, blocks):
    rows = []
    for b in range(blocks):
        high = high_ref[b]
        top = jnp.max(high, axis=0, keepdims=True)
        total = jnp.sum(sum_ref[b] * jnp.exp2(high - top), axis=0, keepdims=True)
        rows.append(top + jnp.log2(total))
    rows += [jnp.zeros((1, BLK), jnp.float32)] * (8 - blocks)
    return jnp.concatenate(rows, axis=0)


def new_potential(old_ref, refs):
    parts = [part for r in refs for part in ([r[...]] if len(r.shape) == 2 else [r[k] for k in range(r.shape[0])])]
    return 0.5 * (old_ref[...] - log_sum(parts))


def exponentials(scores_ref, wide, lanes):
    halves = []
    for h in range(2):
        at = slice(128 * h, 128 * h + 128)
        t = (scores_ref[:, at] + wide).reshape(BLK // 8, 8, 128) + lanes[:, at][None]
        halves.append(jnp.exp2(t))
    return halves


def add_sums(halves, row_acc, col_acc, s, t):
    for h, e in enumerate(halves):
        col_acc[t, :, 128 * h : 128 * h + 128] += jnp.sum(e, axis=0)
    row_acc[s] += (halves[0] + halves[1]).reshape(BLK, 128)


def totals(row_acc, col_acc, blocks):
    columns = [jnp.sum(row_acc[b], axis=1, keepdims=True) for b in range(blocks)]
    below = lax.broadcasted_iota(jnp.int32, (8, BLK), 0) >= blocks
    row = jnp.where(below, 1.0, across(columns))
    col = [jnp.sum(col_acc[b], axis=0, keepdims=True) for b in range(blocks)]
    col = jnp.concatenate(col + [jnp.ones((8 - blocks, BLK), jnp.float32)], axis=0)
    low = jnp.minimum(jnp.min(row), jnp.min(col))
    high = jnp.maximum(jnp.max(row), jnp.max(col))
    return columns, row, col, (low >= 2.0**-60) & (high <= 2.0**100)


def clear(*refs):
    for ref in refs:
        ref[...] = jnp.zeros(ref.shape, jnp.float32)


def pass_sums(pairs_ref, kept, x_ref, y_ref, scale, f_wide, g_wide, row_high, row_sum, col_high, col_sum):
    for ref in (row_high, col_high):
        ref[...] = jnp.full(ref.shape, NEG, jnp.float32)
    clear(row_sum, col_sum)

    def visit(s, t):
        xs, yt = x_ref[s], y_ref[t]
        fold(cross(yt, xs), g_wide[t], scale, row_high, row_sum, s)
        fold(cross(xs, yt), f_wide[s], scale, col_high, col_sum, t)

    over_pairs(pairs_ref, kept, visit)


def sweep(pairs_ref, kept, x_ref, y_ref, scores_ref, f, g, shift, scale, blocks, outs, scratch):
    row_out, col_out = outs
    f_wide, g_wide, row_high, row_sum, col_high, col_sum, lanes, row_acc, col_acc = scratch
    spread_lanes(g + shift, blocks, lanes)
    clear(row_acc, col_acc)

    def visit(s, t):
        halves = exponentials(scores_ref.at[t, s], f_wide[s], lanes[t])
        add_sums(halves, row_acc, col_acc, s, t)

    over_pairs(pairs_ref, kept, visit)
    _, row, col, good = totals(row_acc, col_acc, blocks)
    row_out[...] = jnp.log2(row) - (f + shift)
    col_out[...] = jnp.log2(col) - (g + shift)

    @pl.when(jnp.logical_not(good))
    def _():
        down_rows(g, blocks, g_wide)
        pass_sums(pairs_ref, kept, x_ref, y_ref, scale, *scratch[:6])
        row_out[...] = settle(row_high, row_sum, blocks)
        col_out[...] = settle(col_high, col_sum, blocks)


def all_scores(x_ref, y_ref, scale, blocks, scores_ref):
    everything = x_ref[...].reshape(blocks * BLK, BLK)
    for t in range(blocks):
        scores_ref[t] = (cross(everything, y_ref[t]) * scale).reshape(blocks, BLK, BLK)


def first_kernel(scale, blocks, pairs_ref, count_ref, x_ref, y_ref, *rest):
    f_out, g_out, row_out, col_out = rest[:4]
    scratch, scores_ref = rest[4:-1], rest[-1]
    all_scores(x_ref, y_ref, scale, blocks, scores_ref)
    f_wide, g_wide = scratch[:2]
    f_columns, g_columns = [], []
    for b in range(blocks):
        f_columns.append(norm(x_ref[b], scale))
        f_wide[b] = jnp.broadcast_to(f_columns[b], (BLK, 128))
        g_columns.append(norm(y_ref[b], scale))
    f, g = across(f_columns), across(g_columns)
    f_out[...] = f
    g_out[...] = g
    shift = -(jnp.sum(f) + jnp.sum(g)) / (blocks * BLK)
    outs = (row_out, col_out)
    sweep(pairs_ref, count_ref[0], x_ref, y_ref, scores_ref, f, g, shift, scale, blocks, outs, scratch)


def second_kernel(n_row, scale, blocks, pairs_ref, count_ref, x_ref, y_ref, f_old, g_old, *rest):
    parts, rest = rest[: n_row + 1], rest[n_row + 1 :]
    f_out, g_out, row_out, col_out = rest[:4]
    scratch, scores_ref = rest[4:-1], rest[-1]
    all_scores(x_ref, y_ref, scale, blocks, scores_ref)
    f = new_potential(f_old, parts[:n_row])
    g = new_potential(g_old, parts[n_row:])
    f_out[...] = f
    g_out[...] = g
    down_rows(f, blocks, scratch[0])
    outs = (row_out, col_out)
    sweep(pairs_ref, count_ref[0], x_ref, y_ref, scores_ref, f, g, 0.0, scale, blocks, outs, scratch)


def split_two(w):
    high = w.astype(jnp.bfloat16)
    return high, (w - high.astype(jnp.float32)).astype(jnp.bfloat16)


def weigh(scores, scale, lanes, wide):
    halves = []
    for h in range(2):
        at = slice(128 * h, 128 * h + 128)
        t = (scores[:, at] * scale - wide).reshape(BLK // 8, 8, 128) + lanes[:, at][None]
        halves.append(jnp.exp2(t).reshape(BLK, 128))
    return jnp.concatenate(halves, axis=1)


def receivers_lines(log_sums, n, blocks):
    rows = blocks * BLK // n
    lane = lax.broadcasted_iota(jnp.int32, (1, BLK), 1)
    shifted, lines = {}, []
    for b in range(n):
        k, off = b * rows // BLK, b * rows % BLK
        if off not in shifted:
            shifted[off] = pltpu.roll(log_sums, BLK - off, 1) if off else log_sums
        line = shifted[off][k : k + 1]
        if off and k + 1 < blocks:
            line = jnp.where(lane < BLK - off, line, shifted[off][k + 1 : k + 2])
        lines.append(line)
    return lines


def images(pairs_ref, kept, a_ref, b_ref, scale, lanes, wide, image_ref, turned):
    image_ref[...] = jnp.zeros(image_ref.shape, jnp.float32)

    def visit(s, t):
        a, b = (t, s) if turned else (s, t)
        at, bt = a_ref[a], b_ref[b]
        high, low = split_two(weigh(cross(at, bt), scale, lanes[b], wide[a]))
        rows = pl.ds(pl.multiple_of(a * BLK, BLK), BLK)
        image_ref[rows, :] += jnp.dot(high, bt, preferred_element_type=jnp.float32) + jnp.dot(
            low, bt, preferred_element_type=jnp.float32
        )

    over_pairs(pairs_ref, kept, visit)


def spread_lanes(values, blocks, lanes_ref):
    for b in range(blocks):
        lanes_ref[b] = jnp.broadcast_to(values[b : b + 1], (8, BLK))


def maps_kernel(n_row, scale, blocks, place_ref, pairs_ref, count_ref, x_ref, y_ref, f_old, g_old, *rest):
    parts, rest = rest[: n_row + 1], rest[n_row + 1 :]
    keep_out, send_out, own, up_first, down_first, up_own, down_own = rest[:7]
    scratch = rest[7:16]
    f_wide, g_wide, row_high, row_sum, col_high, col_sum, lanes, row_acc, col_acc = scratch
    scores_ref, x_turned, forward, backward, turned, logs, lines_ref, *weights = rest[16:]
    all_scores(x_ref, y_ref, scale, blocks, scores_ref)
    kept = count_ref[0]
    f = new_potential(f_old, parts[:n_row])
    g = new_potential(g_old, parts[n_row:])
    down_rows(f, blocks, f_wide)
    spread_lanes(g, blocks, lanes)
    clear(row_acc, col_acc, forward, turned)
    diagonal = lax.broadcasted_iota(jnp.int32, (BLK, BLK), 0) == lax.broadcasted_iota(jnp.int32, (BLK, BLK), 1)
    unit = jnp.where(diagonal, 1.0, 0.0).astype(jnp.bfloat16)
    for b in range(blocks):
        x_turned[b] = cross(unit, x_ref[b]).astype(jnp.bfloat16)

    def weigh_pair(p, buffer):
        at = jnp.minimum(p, kept - 1)
        s, t = pairs_ref[0, at], pairs_ref[1, at]
        halves = exponentials(scores_ref.at[t, s], f_wide[s], lanes[t])
        counted = jnp.where(p < kept, 1.0, 0.0)
        for h, e in enumerate(halves):
            cols = slice(128 * h, 128 * h + 128)
            col_acc[t, :, cols] += jnp.sum(e, axis=0) * counted
            high, low = split_two(e.reshape(BLK, 128))
            buffer[0, :, cols] = high
            buffer[1, :, cols] = low
        row_acc[s] += (halves[0] + halves[1]).reshape(BLK, 128) * counted

    def add_pair(p, buffer):
        s, t = pairs_ref[0, p], pairs_ref[1, p]
        yt, xt = y_ref[t], x_turned[s]
        high, low = buffer[0], buffer[1]
        rows = pl.ds(pl.multiple_of(s * BLK, BLK), BLK)
        forward[rows, :] += jnp.dot(
            jnp.concatenate([high, low], axis=1),
            jnp.concatenate([yt, yt], axis=0),
            preferred_element_type=jnp.float32,
        )
        turned[t] += jnp.dot(
            jnp.concatenate([xt, xt], axis=1),
            jnp.concatenate([high, low], axis=0),
            preferred_element_type=jnp.float32,
        )

    weigh_pair(0, weights[0])

    def two(step, carry):
        p = 2 * step
        weigh_pair(p + 1, weights[1])
        add_pair(p, weights[0])
        weigh_pair(p + 2, weights[0])
        add_pair(p + 1, weights[1])
        return carry

    lax.fori_loop(0, kept // 2, two, 0)

    @pl.when(kept % 2 == 1)
    def _():
        add_pair(kept - 1, weights[0])

    columns, row, col, good = totals(row_acc, col_acc, blocks)

    @pl.when(good)
    def _():
        logs[0] = jnp.log2(row) - f
        logs[1] = jnp.log2(col) - g
        inverse = 1.0 / col
        for b in range(blocks):
            rows = slice(b * BLK, b * BLK + BLK)
            forward[rows, :] = forward[rows, :] * (1.0 / columns[b])
            backward[rows, :] = jnp.transpose(turned[b] * inverse[b : b + 1])

    @pl.when(jnp.logical_not(good))
    def _():
        down_rows(g, blocks, g_wide)
        pass_sums(pairs_ref, kept, x_ref, y_ref, scale, *scratch[:6])
        row_log = settle(row_high, row_sum, blocks)
        col_log = settle(col_high, col_sum, blocks)
        logs[0] = row_log
        logs[1] = col_log
        down_rows(row_log, blocks, f_wide)
        images(pairs_ref, kept, x_ref, y_ref, scale, lanes, f_wide, forward, False)
        spread_lanes(f, blocks, lanes)
        down_rows(col_log, blocks, g_wide)
        images(pairs_ref, kept, y_ref, x_ref, scale, lanes, g_wide, backward, True)

    n = lines_ref.shape[0]
    rows = blocks * BLK // n
    for b, line in enumerate(receivers_lines(logs[0], n, blocks)):
        lines_ref[b] = line
    me = place_ref[1]

    def put(out, r, high):
        to = ((me + r) % RING) + RING * high
        out[:rows, :] = forward[pl.ds(pl.multiple_of(to * rows, 16), rows), :]
        out[rows : rows + 1, :] = lines_ref[to]

    put(up_first, 2, 0)
    put(down_first, 2, 1)
    put(own.at[0], 0, 0)
    put(own.at[1], 0, 1)
    put(up_own.at[0], 1, 0)
    put(up_own.at[1], 1, 1)
    put(down_own.at[0], 3, 1)
    put(down_own.at[1], 3, 0)

    half = keep_out.shape[0]
    small = blocks * BLK // (2 * half)
    lines = receivers_lines(logs[1], 2 * half, blocks)
    core = place_ref[0]
    for q in range(half):
        for ref, side in ((keep_out, core), (send_out, 1 - core)):
            first = pl.multiple_of((2 * q + side) * small, 16)
            ref[q, :small, :] = backward[pl.ds(first, small), :]
            ref[q, small : small + 1, :] = jnp.where(side == 0, lines[2 * q], lines[2 * q + 1])


def pair_kernel(rows, a_ref, b_ref, out_ref):
    n = a_ref.shape[0]
    a = jnp.concatenate([a_ref[q, rows : rows + 1, :] for q in range(n)], axis=0)
    b = jnp.concatenate([b_ref[q, rows : rows + 1, :] for q in range(n)], axis=0)
    high = jnp.maximum(a, b)
    both = jnp.exp2(a - high) + jnp.exp2(b - high)
    merged = high + jnp.log2(both)
    a_part = jnp.transpose(jnp.exp2(a - high) / both)
    b_part = jnp.transpose(jnp.exp2(b - high) / both)
    for q in range(n):
        out_ref[q, :rows, :] = (
            a_part[:rows, q : q + 1] * a_ref[q, :rows, :]
            + b_part[:rows, q : q + 1] * b_ref[q, :rows, :]
        )
        out_ref[q, rows : rows + 1, :] = merged[q : q + 1]


def blend(parts, rows):
    logs = jnp.concatenate([part[rows : rows + 1, :] for part in parts], axis=0)
    high = jnp.max(logs, axis=0, keepdims=True)
    lifted = jnp.exp2(logs - high)
    whole = jnp.sum(lifted, axis=0, keepdims=True)
    upright = jnp.transpose(lifted / whole)
    total = jnp.zeros((rows, BLK), jnp.float32)
    for d, part in enumerate(parts):
        total += upright[:rows, d : d + 1] * part[:rows, :]
    return total, high + jnp.log2(whole)


def put_blend(out, blended, rows):
    out[:rows, :] = blended[0]
    if out.shape[0] > rows:
        out[rows : rows + 1, :] = blended[1]


def z_kernel(rows, place_ref, paired, up_came, down_came, keep_ref, send_ref):
    here = 2 * place_ref[0]
    for out, low in ((keep_ref, place_ref[1]), (send_ref, 1 - place_ref[1])):
        parts = [paired.at[here + low], up_came.at[low], down_came.at[low]]
        put_blend(out, blend(parts, rows), rows)


def relay_kernel(rows, up_own, up_came, down_own, down_came, up_out, down_out):
    for own, relayed, out in ((up_own, up_came, up_out), (down_own, down_came, down_out)):
        put_blend(out.at[0], blend([own.at[0], relayed], rows), rows)
        out[1] = own[1]


def core_kernel(rows, place_ref, keep, came, paired, up_out, down_out):
    pair_kernel(rows, keep, came, paired)
    n = paired.shape[0] // 2
    far = 2 * ((place_ref[0] + n // 2) % n)
    up_out[...] = paired[far]
    down_out[...] = paired[far + 1]


def ring_kernel(rows, away, place_ref, paired, up_came, down_came, up_out, down_out):
    n = paired.shape[0] // 2
    up_at = 2 * ((place_ref[0] + away) % n)
    down_at = 2 * ((place_ref[0] + n - away) % n)
    for low in range(2):
        for at, came, out, whole in ((up_at, up_came, up_out, 0), (down_at, down_came, down_out, 1)):
            own = paired.at[at + low]
            if len(came.shape) == 3:
                put_blend(out.at[low], blend([own, came.at[low]], rows), rows)
            elif low == whole:
                put_blend(out.at[low], blend([own, came], rows), rows)
            else:
                out[low] = own[...]


def x_kernel(rows, place_ref, own, up_came, down_came, keep_ref, send_ref):
    low = blend([own.at[0], up_came.at[0], down_came.at[1]], rows)
    high = blend([own.at[1], down_came.at[0], up_came.at[1]], rows)

    @pl.when(place_ref[0] == 0)
    def _():
        put_blend(keep_ref, low, rows)
        put_blend(send_ref, high, rows)

    @pl.when(place_ref[0] == 1)
    def _():
        put_blend(keep_ref, high, rows)
        put_blend(send_ref, low, rows)


def last_kernel(rows, a_ref, b_ref, out_ref):
    put_blend(out_ref, blend([a_ref, b_ref], rows), rows)


def in_vmem(n):
    return [pl.BlockSpec(memory_space=pltpu.VMEM)] * n


def shape(*dims):
    return jax.ShapeDtypeStruct(dims, jnp.float32)


def sums_scratch(blocks):
    wide = pltpu.VMEM((blocks, BLK, 128), jnp.float32)
    deep = pltpu.VMEM((blocks, 8, BLK), jnp.float32)
    return [wide] * 2 + [deep] * 5 + [wide, deep, pltpu.VMEM((blocks, blocks, BLK, BLK), jnp.float32)]


def per_device(n_src, n_tgt, sources, targets, pairs, counts):
    width = sources.shape[1]
    scale = math.log2(math.e) / (math.sqrt(width) / 4.0)
    blocks = sources.shape[0] // BLK
    x = sources.reshape(blocks, BLK, width)
    y = targets.reshape(blocks, BLK, width)
    pair_list = jnp.transpose(pairs[0, 0])
    kept = counts.reshape(-1)
    smem = pl.BlockSpec(memory_space=pltpu.SMEM)
    large = pltpu.CompilerParams(vmem_limit_bytes=36 * 1024 * 1024)
    little = pltpu.CompilerParams(vmem_limit_bytes=8 * 1024 * 1024)

    def swap(value, axis, size, bit):
        return lax.ppermute(value, axis, [(k, k ^ bit) for k in range(size)])

    n_z = n_src // 4
    along_z = [list(range(k, n_src, 4)) for k in range(4)]

    def exchange(row, col):
        row = log_sum([row, swap(row, "tgt", n_tgt, RING)])
        col = log_sum([col] + [swap(col, "src", n_src, bits) for bits in (1, 2, 3)])
        row = log_sum([row, swap(row, "tgt", n_tgt, 2)])
        copies = jnp.broadcast_to(col[None], (n_z, *col.shape))
        cols = lax.all_to_all(copies, "src", 0, 0, axis_index_groups=along_z, tiled=True)
        return [row, swap(row, "tgt", n_tgt, 1), cols]

    f, g, row, col = pl.pallas_call(
        functools.partial(first_kernel, scale, blocks),
        out_shape=[shape(8, BLK)] * 4,
        in_specs=[smem] * 2 + in_vmem(2),
        out_specs=in_vmem(4),
        scratch_shapes=sums_scratch(blocks),
        compiler_params=large,
    )(pair_list, kept, x, y)
    parts = exchange(row, col)
    f, g, row, col = pl.pallas_call(
        functools.partial(second_kernel, 2, scale, blocks),
        out_shape=[shape(8, BLK)] * 4,
        in_specs=[smem] * 2 + in_vmem(7),
        out_specs=in_vmem(4),
        scratch_shapes=sums_scratch(blocks),
        compiler_params=large,
    )(pair_list, kept, x, y, f, g, *parts)
    parts = exchange(row, col)

    f_rows, b_rows = blocks * BLK // n_tgt, blocks * BLK // n_src
    half = n_src // 2
    s_at = lax.axis_index("src").astype(jnp.int32)
    t_at = lax.axis_index("tgt").astype(jnp.int32)

    def call(kernel, operands, outs, places=()):
        return pl.pallas_call(
            kernel,
            out_shape=outs,
            in_specs=[smem] * len(places) + in_vmem(len(operands)),
            out_specs=in_vmem(len(outs)),
            compiler_params=little,
        )(*places, *operands)

    block = shape(f_rows + 8, width)
    two = shape(2, f_rows + 8, width)
    keep, send, own, up_first, down_first, up_own, down_own = pl.pallas_call(
        functools.partial(maps_kernel, 2, scale, blocks),
        out_shape=[shape(half, b_rows + 8, width)] * 2 + [two, block, block, two, two],
        in_specs=[smem] * 3 + in_vmem(7),
        out_specs=in_vmem(7),
        scratch_shapes=sums_scratch(blocks)
        + [
            pltpu.VMEM((blocks, width, BLK), jnp.bfloat16),
            pltpu.VMEM((blocks * BLK, width), jnp.float32),
            pltpu.VMEM((blocks * BLK, width), jnp.float32),
            pltpu.VMEM((blocks, width, BLK), jnp.float32),
            pltpu.VMEM((2, 8, BLK), jnp.float32),
            pltpu.VMEM((n_tgt, 1, BLK), jnp.float32),
            pltpu.VMEM((2, BLK, BLK), jnp.bfloat16),
            pltpu.VMEM((2, BLK, BLK), jnp.bfloat16),
        ],
        compiler_params=large,
    )(jnp.stack([s_at % 2, t_at % RING]), pair_list, kept, x, y, f, g, *parts)
    came = swap(send, "src", n_src, 1)

    ups = [(k, k // RING * RING + (k + 1) % RING) for k in range(n_tgt)]
    downs = [(b, a) for a, b in ups]
    up_came = lax.ppermute(up_first, "tgt", ups)
    down_came = lax.ppermute(down_first, "tgt", downs)
    small = shape(b_rows + 8, width)
    small_two = shape(2, b_rows + 8, width)
    z_at = (s_at // 4).reshape(1)
    paired, z_up, z_down = call(
        functools.partial(core_kernel, b_rows),
        [keep, came],
        [shape(half, b_rows + 8, width), small, small],
        [z_at],
    )
    z_ups = [(k, (k + 4) % n_src) for k in range(n_src)]
    z_downs = [(b, a) for a, b in z_ups]
    for away in range(n_z // 2 - 1, -1, -1):
        z_up = lax.ppermute(z_up, "src", z_ups)
        z_down = lax.ppermute(z_down, "src", z_downs)
        if away == n_z // 2 - 1:
            up_came, down_came, _, _ = lax.optimization_barrier((up_came, down_came, z_up, z_down))
        if away:
            z_up, z_down = call(
                functools.partial(ring_kernel, b_rows, away),
                [paired, z_up, z_down],
                [small_two, small_two],
                [z_at],
            )
    keep, send = call(
        functools.partial(z_kernel, b_rows),
        [paired, z_up, z_down],
        [small, small],
        [jnp.stack([s_at // 4, s_at // 2 % 2])],
    )
    came = swap(send, "src", n_src, 2)
    (backward,) = call(functools.partial(last_kernel, b_rows), [keep, came], [shape(b_rows, width)])

    up, down = call(
        functools.partial(relay_kernel, f_rows),
        [up_own, up_came, down_own, down_came],
        [two, two],
    )
    up_came = lax.ppermute(up, "tgt", ups)
    down_came = lax.ppermute(down, "tgt", downs)
    keep, send = call(
        functools.partial(x_kernel, f_rows),
        [own, up_came, down_came],
        [block, block],
        [(t_at // RING).reshape(1)],
    )
    came = swap(send, "tgt", n_tgt, RING)
    (forward,) = call(functools.partial(last_kernel, f_rows), [keep, came], [shape(f_rows, width)])
    return (forward, backward)


def solution(mesh):
    return jax.shard_map(
        functools.partial(per_device, mesh.shape["src"], mesh.shape["tgt"]),
        mesh=mesh,
        in_specs=(P("src", None), P("tgt", None), P("src", "tgt", None, None), P("src", "tgt")),
        out_specs=(P(("src", "tgt"), None), P(("tgt", "src"), None)),
        check_vma=False,
    )
```
